32 devices in a mesh: dp: 2 (over core), fsdp: 16 (over z, y, x).
Axes of the slice: x: 2, y: 2, z: 4, core: 2. Of those that a mesh axis runs over, the one named last changes fastest.
Arguments:
- latents: float32 [32, 576, 1536], P(('dp', 'fsdp')), may hold values from -6 to 6
- text_embed: bfloat16 [32, 4, 77, 1280], P(('dp', 'fsdp')), may hold values from -6 to 6
- time_embed: float32 [32, 4, 64], P(('dp', 'fsdp')), may hold values from -6 to 6
- heights: int32 [32, 4], P(('dp', 'fsdp')), may hold values from 0 to 24, as said below
- widths: int32 [32, 4], P(('dp', 'fsdp')), may hold values from 0 to 24, as said below
- text_counts: int32 [32, 4], P(('dp', 'fsdp')), may hold values from 1 to 77
- res_vecs: float32 [11, 1536], P(None, ('dp', 'fsdp')), may hold values from -4 to 4
- fc1_w: float32 [1536, 6144], P(None, ('dp', 'fsdp')), may hold values from -0.15625 to 0.15625
- ff_vecs: float32 [3, 6144], P(None, ('dp', 'fsdp')), may hold values from -4 to 4
- fc2_w: float32 [6144, 1536], P(('dp', 'fsdp')), may hold values from -0.078125 to 0.078125
- time_w: float32 [64, 3072], P(None, ('dp', 'fsdp')), may hold values from -0.375 to 0.375
- time_b: float32 [3072], P(('dp', 'fsdp')), may hold values from -4 to 4
- kv_w: float32 [1280, 1536], P(('dp', 'fsdp')), may hold values from -0.15625 to 0.15625
- attn_w: float32 [1536, 6144], P(None, ('dp', 'fsdp'))
- attn_vecs: float32 [4, 1536], P(None, ('dp', 'fsdp')), may hold values from -4 to 4
- cotangent: float32 [32, 576, 1536], P(('dp', 'fsdp')), may hold values from -6 to 6
Outputs:
- output: float32 [32, 576, 1536], P(('dp', 'fsdp'))
- latents_grad: float32 [32, 576, 1536], P(('dp', 'fsdp'))
- text_grad: float32 [32, 4, 77, 1280], P(('dp', 'fsdp'))
- res_vecs_grad: float32 [11, 1536], P(None, ('dp', 'fsdp'))
- fc1_w_grad: float32 [1536, 6144], P(None, ('dp', 'fsdp'))
- ff_vecs_grad: float32 [3, 6144], P(None, ('dp', 'fsdp'))
- fc2_w_grad: float32 [6144, 1536], P(('dp', 'fsdp'))
- time_w_grad: float32 [64, 3072], P(None, ('dp', 'fsdp'))
- time_b_grad: float32 [3072], P(('dp', 'fsdp'))
- kv_w_grad: float32 [1280, 1536], P(('dp', 'fsdp'))
- attn_w_grad: float32 [1536, 6144], P(None, ('dp', 'fsdp'))
- attn_vecs_grad: float32 [4, 1536], P(None, ('dp', 'fsdp'))
The draws below stay inside these ranges and needn't reach their ends.
Inputs may be any that keep to these rules, and one draw needn't show every extreme that they name: `heights`: each packed row holds its latents end to end from slot 0 in the order of the latent places; a present latent has height and width each one of 12, 16, 24; an absent one has height and width 0 and may stand before present ones; the pixels of a row never exceed 576. `widths`: A width is 0 exactly where the height is 0.
All inputs are finite; a program needn't handle non-finite values.
Results may differ from the reference program's by a relative error of at most 0.012.
The reference program's roundings to bfloat16 on the way count: a program that leaves them out, or rounds other values in their place, can miss the bound.
Values may be sent and summed in bfloat16 or wider, within the bound.
No kernel may reach another device: no remote copies, remote signals or barrier semaphores. Data moves between devices by JAX's collectives and lax.ppermute only.
A program may use at most 448 MiB of HBM per device.

```python
import math
import jax
import jax.numpy as jnp
from jax import lax

C = 1536
HEADS = 24
FF = 6144
CC = 1280
TDIM = 64
TEXT = 77
SIDE_UNIT = 4
SLOTS = 576
LAT_ROW = 4
HEAD_DIM = 64
ROWS = 32


def packing(key):
    side_values = jnp.array([3, 4, 6], jnp.int32) * SIDE_UNIT
    picks = jax.random.randint(key, (ROWS, LAT_ROW, 2), 0, 3)
    chosen = jnp.sum(jnp.where(picks[..., None] == jnp.arange(3, dtype=jnp.int32), side_values, 0), axis=-1).astype(jnp.int32)
    leading = (jnp.arange(ROWS)[:, None] == 0) & (jnp.arange(LAT_ROW)[None, :] == 0)
    chosen = jnp.where(leading[..., None], 6 * SIDE_UNIT, chosen).astype(jnp.int32)
    filled = jnp.zeros((ROWS,), jnp.int32)
    keeping = []
    for index in range(LAT_ROW):
        size_now = chosen[:, index, 0] * chosen[:, index, 1]
        fits = filled + size_now <= SLOTS
        filled = (filled + jnp.where(fits, size_now, 0)).astype(jnp.int32)
        keeping.append(fits)
    kept_mask = jnp.stack(keeping, axis=1)
    return (jnp.where(kept_mask, chosen[..., 0], 0).astype(jnp.int32), jnp.where(kept_mask, chosen[..., 1], 0).astype(jnp.int32))


def draw_heights(key, part):
    shapes = packing(key)
    return shapes[0]


def draw_widths(key, part):
    shapes = packing(key)
    return shapes[1]


def draw_attn_w(key, part):
    key = jax.random.fold_in(key, 7)
    base = jax.random.normal(key, (C, 4 * C), jnp.float32)
    column = jnp.arange(4 * C)
    scale = jnp.where(column < 3 * C, 1.0, 4.0) * C ** (-0.5)
    return base * scale[None, :]


def place_ends(drawn, own_key, least, largest):
    extent = drawn.shape
    spot = [jax.random.randint(jax.random.fold_in(own_key, axis), (), 0, extent[axis]) for axis in range(len(extent))]
    drawn = drawn.at[tuple(spot)].set(least)
    longest = extent.index(max(extent))
    spot[longest] = (spot[longest] + 1) % extent[longest]
    return drawn.at[tuple(spot)].set(largest)


def level_of(key, extent, pieces, least, largest):
    def one(dim, parts):
        steps = jax.random.uniform(jax.random.fold_in(jax.random.fold_in(key, 6), dim), (parts,), jnp.float32, least / len(pieces), largest / len(pieces))
        return jnp.repeat(jnp.exp(steps), extent[dim] // parts).reshape((-1,) + (1,) * (len(extent) - dim - 1))

    factor_of = one(*pieces[0])
    for cut in pieces[1:]:
        factor_of = factor_of * one(*cut)
    return factor_of


def bell_draw(rng, extent, width, limit, split=(), kind=jnp.bfloat16):
    loudness = level_of(rng, extent, split, -0.22, 0.18) if split else 1.0
    values = jax.random.normal(rng, extent, jnp.float32) * width * loudness
    return jnp.minimum(jnp.maximum(values, -limit), limit).astype(kind)


def setup_inputs(seed: int = 0) -> dict:
    streams_of = jax.random.split(jax.random.key(seed), 17)
    latents = bell_draw(streams_of[0], (ROWS, SLOTS, C), 1.0, 6.0, ((0, 32),), jnp.float32)
    text_embed = bell_draw(streams_of[1], (ROWS, LAT_ROW, TEXT, CC), 1.0, 6.0, ((0, 32),))
    time_embed = bell_draw(streams_of[2], (ROWS, LAT_ROW, TDIM), 1.0, 6.0, ((0, 32),), jnp.float32)
    heights = draw_heights(jax.random.fold_in(streams_of[16], 71), 0)
    widths = draw_widths(jax.random.fold_in(streams_of[16], 71), 0)
    text_counts = place_ends(jax.random.randint(streams_of[5], (ROWS, LAT_ROW), 1, TEXT + 1), jax.random.fold_in(streams_of[5], 1), 1, TEXT).astype(jnp.int32)
    res_vecs = bell_draw(streams_of[6], (11, C), 0.4, 4.0, ((1, 32),), jnp.float32)
    fc1_w = bell_draw(streams_of[7], (C, FF), C ** -0.5, 0.15625, ((1, 32),), jnp.float32)
    ff_vecs = bell_draw(streams_of[8], (3, FF), 0.5, 4.0, ((1, 32),), jnp.float32)
    fc2_w = bell_draw(streams_of[9], (FF, C), FF ** -0.5, 0.078125, ((0, 32),), jnp.float32)
    time_w = bell_draw(streams_of[10], (TDIM, 2 * C), (4 * TDIM) ** -0.5, 0.375, ((1, 32),), jnp.float32)
    time_b = bell_draw(streams_of[11], (2 * C,), 0.3, 4.0, ((0, 32),), jnp.float32)
    kv_w = bell_draw(streams_of[12], (CC, C), CC ** -0.5, 0.15625, ((0, 32),), jnp.float32)
    attn_w = draw_attn_w(jax.random.fold_in(streams_of[16], 71), 0)
    attn_vecs = bell_draw(streams_of[14], (4, C), 0.3, 4.0, ((1, 32),), jnp.float32)
    cotangent = bell_draw(streams_of[15], (ROWS, SLOTS, C), 1.0, 6.0, ((0, 32),), jnp.float32)
    return dict(latents=latents, text_embed=text_embed, time_embed=time_embed, heights=heights, widths=widths, text_counts=text_counts, res_vecs=res_vecs, fc1_w=fc1_w, ff_vecs=ff_vecs, fc2_w=fc2_w, time_w=time_w, time_b=time_b, kv_w=kv_w, attn_w=attn_w, attn_vecs=attn_vecs, cotangent=cotangent)


@jax.custom_vjp
def low(v):
    return lax.optimization_barrier(v.astype(jnp.bfloat16)).astype(jnp.float32)

@jax.custom_vjp
def low_back(v):
    return v

def low_keep(v):
    return (low(v), None)

def low_pass(kept, grad):
    return (grad,)

def back_keep(v):
    return (v, None)

def back_low(kept, grad):
    return (low(grad),)
low.defvjp(low_keep, low_pass)
low_back.defvjp(back_keep, back_low)
HIGHEST = lax.Precision.HIGHEST
NORM_EPS = 1e-06
MASKED = -1000000000.0

def layout(heights_row, widths_row):
    pixels = (heights_row * widths_row).astype(jnp.int32)
    ends_at = jnp.cumsum(pixels).astype(jnp.int32)
    starts_at = (ends_at - pixels).astype(jnp.int32)
    slot_ids = jnp.arange(SLOTS, dtype=jnp.int32)
    segment = lax.optimization_barrier(jnp.sum((ends_at[None, :] <= slot_ids[:, None]).astype(jnp.int32), axis=1)).astype(jnp.int32)
    member = segment[:, None] == jnp.arange(LAT_ROW, dtype=jnp.int32)[None, :]
    start_at = lax.optimization_barrier(jnp.sum(jnp.where(member, starts_at[None, :], 0), axis=1)).astype(jnp.int32)
    height_at = lax.optimization_barrier(jnp.sum(jnp.where(member, heights_row[None, :], 0), axis=1)).astype(jnp.int32)
    width_at = lax.optimization_barrier(jnp.sum(jnp.where(member, widths_row[None, :], 0), axis=1)).astype(jnp.int32)
    place_in = (slot_ids - start_at).astype(jnp.int32)
    safe_width = jnp.maximum(width_at, 1).astype(jnp.int32)
    column = (place_in % safe_width).astype(jnp.int32)
    row_index = (place_in // safe_width).astype(jnp.int32)
    return (segment, member, height_at, width_at, row_index, column)

def layer_norm(values):
    center = values - lax.optimization_barrier(jnp.mean(values, axis=-1, keepdims=True))
    return center * lax.rsqrt(lax.optimization_barrier(jnp.mean(center * center, axis=-1, keepdims=True)) + NORM_EPS)

def depthwise(values, conv_taps, conv_bias, geometry):
    segment, member, height_at, width_at, row_index, column = geometry
    live_query = segment < LAT_ROW
    slot_ids = jnp.arange(SLOTS, dtype=jnp.int32)
    result = jnp.zeros_like(values) + conv_bias
    for step_y in (-1, 0, 1):
        for step_x in (-1, 0, 1):
            inside = live_query & (row_index + step_y >= 0) & (row_index + step_y < height_at)
            inside = inside & (column + step_x >= 0) & (column + step_x < width_at)
            source_ids = jnp.clip(slot_ids[None, :] + step_y * width_at + step_x, 0, SLOTS - 1).astype(jnp.int32)
            neighbour = jax.vmap(lambda values_row, ids_row: values_row[ids_row])(values, source_ids)
            result = result + jnp.where(inside[..., None], neighbour, 0.0) * conv_taps[(step_y + 1) * 3 + step_x + 1]
    return result

def response_norm(hidden, grn_gain, grn_shift, onehot):
    active = jax.nn.gelu(hidden, approximate=False)
    power = jnp.einsum('rsl,rsf->rlf', onehot, active * active, precision=HIGHEST)
    global_norm = jnp.sqrt(power + NORM_EPS)
    scaled = global_norm / (lax.optimization_barrier(jnp.mean(global_norm, axis=2, keepdims=True)) + NORM_EPS)
    spread = jnp.einsum('rsl,rlf->rsf', onehot, scaled, precision=HIGHEST)
    return grn_gain * (active * spread) + grn_shift + active

def timestep(after_res, time_pair, onehot):
    per_slot = jnp.einsum('rsl,rlc->rsc', onehot, time_pair, precision=HIGHEST)
    half_width = time_pair.shape[-1] // 2
    return after_res + after_res * per_slot[..., :half_width] + per_slot[..., half_width:]

def attention_mask(segment, counts_row):
    live_query = segment < LAT_ROW
    image_ok = (segment[:, None] == segment[None, :]) & live_query[:, None]
    text_index = jnp.arange(LAT_ROW * TEXT, dtype=jnp.int32)
    text_latent = (text_index // TEXT).astype(jnp.int32)
    text_limit = lax.optimization_barrier(jnp.sum(jnp.where(text_latent[:, None] == jnp.arange(LAT_ROW, dtype=jnp.int32)[None, :], counts_row[None, :], 0), axis=1)).astype(jnp.int32)
    text_ok = (text_latent[None, :] == segment[:, None]) & (text_index % TEXT < text_limit)[None, :]
    return jnp.concatenate([image_ok, text_ok], axis=1)

def layer_block(values, text_rows, time_rows, heights_rows, widths_rows, counts_rows, params):
    conv_taps, conv_bias, fc2_bias, fc1_weight, fc1_bias, grn_gain, grn_shift, fc2_weight, time_weight, time_bias, text_weight, w_query, w_key, w_value, w_output, bias_query, bias_value, bias_output, bias_text = params
    row_count = values.shape[0]
    geometry = jax.vmap(layout)(heights_rows, widths_rows)
    segment = geometry[0]
    onehot = geometry[1].astype(jnp.float32)
    live_mask = (segment < LAT_ROW).astype(jnp.float32)[..., None]
    normed = layer_norm(depthwise(values, conv_taps, conv_bias, geometry))
    hidden = low_back(jnp.einsum('rsc,cf->rsf', low(normed), fc1_weight, precision=HIGHEST) + fc1_bias)
    response = response_norm(hidden, grn_gain, grn_shift, onehot)
    branch = low_back(jnp.einsum('rsf,fc->rsc', low(response), fc2_weight, precision=HIGHEST) + fc2_bias)
    after_res = values + live_mask * branch
    time_pair = jnp.einsum('rlt,tc->rlc', low(time_rows), time_weight, precision=HIGHEST) + time_bias
    after_time = timestep(after_res, time_pair, onehot)
    normed_two = low(layer_norm(after_time))
    flat_text = text_rows.reshape(row_count, LAT_ROW * TEXT, CC)
    mapped = low(low_back(jnp.einsum('rtk,kc->rtc', low(jax.nn.silu(flat_text)), text_weight, precision=HIGHEST) + bias_text))
    source = jnp.concatenate([normed_two, mapped], axis=1)
    query = low(low_back(jnp.einsum('rsc,cd->rsd', normed_two, w_query, precision=HIGHEST) + bias_query))
    key_rows = low(low_back(jnp.einsum('rkc,cd->rkd', source, w_key, precision=HIGHEST)))
    value_rows = low(low_back(jnp.einsum('rkc,cd->rkd', source, w_value, precision=HIGHEST) + bias_value))
    key_count = SLOTS + LAT_ROW * TEXT
    masks = jax.vmap(attention_mask)(segment, counts_rows)
    query_heads = query.reshape(row_count, SLOTS, HEADS, HEAD_DIM)
    key_heads = key_rows.reshape(row_count, key_count, HEADS, HEAD_DIM)
    value_heads = value_rows.reshape(row_count, key_count, HEADS, HEAD_DIM)
    scores = low_back(jnp.einsum('rqhd,rkhd->rhqk', query_heads, key_heads, precision=HIGHEST) * HEAD_DIM ** (-0.5))
    weights = jax.nn.softmax(jnp.where(masks[:, None], scores, MASKED), axis=-1)
    attended = jnp.einsum('rhqk,rkhd->rqhd', low(weights), value_heads, precision=HIGHEST).reshape(row_count, SLOTS, C)
    attended = low(low_back(attended))
    attn_out = low_back(jnp.einsum('rsc,cd->rsd', attended, w_output, precision=HIGHEST) + bias_output)
    return after_time + live_mask * attn_out

def reference(latents, text_embed, time_embed, heights, widths, text_counts, res_vecs, fc1_w, ff_vecs, fc2_w, time_w, time_b, kv_w, attn_w, attn_vecs, cotangent):
    text_float = text_embed.astype(jnp.float32)
    group_rows = math.gcd(ROWS, 4)
    groups = ROWS // group_rows

    def forward(latents, text_float, res_vecs, fc1_w, ff_vecs, fc2_w, time_w, time_b, kv_w, attn_w, attn_vecs):
        res_low = low(res_vecs)
        ff_low = low(ff_vecs)
        attn_low = low(attn_w)
        vecs_low = low(attn_vecs)
        params = (res_low[:9], res_low[9], res_low[10], low(fc1_w), ff_low[0], ff_low[1], ff_low[2], low(fc2_w), low(time_w), low(time_b), low(kv_w), attn_low[:, :C], attn_low[:, C:2 * C], attn_low[:, 2 * C:3 * C], attn_low[:, 3 * C:], vecs_low[0], vecs_low[1], vecs_low[2], vecs_low[3])

        def run_block(block):
            return layer_block(block[0], block[1], block[2], block[3], block[4], block[5], params)
        blocks = (latents.reshape(groups, group_rows, SLOTS, C), text_float.reshape(groups, group_rows, LAT_ROW, TEXT, CC), time_embed.reshape(groups, group_rows, LAT_ROW, TDIM), heights.reshape(groups, group_rows, LAT_ROW), widths.reshape(groups, group_rows, LAT_ROW), text_counts.reshape(groups, group_rows, LAT_ROW))
        return lax.map(jax.checkpoint(run_block), blocks).reshape(ROWS, SLOTS, C)
    output, pullback = jax.vjp(forward, latents, text_float, res_vecs, fc1_w, ff_vecs, fc2_w, time_w, time_b, kv_w, attn_w, attn_vecs)
    grads = pullback(cotangent)
    return (output, grads[0], grads[1], grads[2], grads[3], grads[4], grads[5], grads[6], grads[7], grads[8], grads[9], grads[10])
```

```python
import functools

import jax
import jax.numpy as jnp
from jax import lax
from jax.experimental import pallas as pl
from jax.experimental.pallas import tpu as pltpu
from jax.sharding import PartitionSpec as P

HEADS = 24
TEXT = 77
SIDE_UNIT = 4
SLOTS = 576
LAT_ROW = 4


HIGHEST = lax.Precision.HIGHEST
NORM_EPS = 1e-06
MASKED = -1000000000.0


def bit_count(size):
    return size.bit_length() - 1


def swap(values, axis_name, size, bit):
    return lax.ppermute(values, axis_name, [(i, i ^ (1 << bit)) for i in range(size)])


def scatter_orders(size):
    bits = list(range(bit_count(size)))
    orders = []
    for first in ([0, 1], [1, 0], [2, 0, 1]):
        first = [b for b in first if b in bits]
        orders.append(first + [b for b in bits if b not in first])
    return orders


def keep_kernel(*refs):
    pass


def tie(values, *others):
    some = pl.BlockSpec(memory_space=pl.ANY)
    return pl.pallas_call(
        keep_kernel,
        out_shape=jax.ShapeDtypeStruct(values.shape, values.dtype),
        in_specs=[some] * (1 + len(others)),
        out_specs=some,
        input_output_aliases={0: 0},
    )(values, *others)


class Gather:
    def __init__(self, shard, orders, inner, outer):
        self.rows, width = shard.shape
        self.piece = width // len(orders)
        self.inner, self.outer = inner, outer
        self.orders = [order[::-1] for order in orders]
        self.held = [
            shard[None, :, number * self.piece : (number + 1) * self.piece]
            for number in range(len(orders))
        ]
        self.offsets = [[0] for _ in orders]

    def step(self, number, after=()):
        came = []
        for index, order in enumerate(self.orders):
            bit = order[number]
            held = tie(self.held[index], *after) if after else self.held[index]
            came.append(swap(held, "fsdp", self.outer, bit))
            if number < len(order) - 1:
                self.held[index] = jnp.concatenate([held, came[-1]], axis=0)
                self.offsets[index] = self.offsets[index] + [o ^ (1 << bit) for o in self.offsets[index]]
        self.came = came
        return came

    def parts(self):
        last = [1 << order[-1] for order in self.orders]
        parts = [self.held, self.came]
        places = [self.offsets, [[o ^ b for o in offs] for offs, b in zip(self.offsets, last)]]
        for bit in range(bit_count(self.inner)):
            parts = parts + [[swap(p, "dp", self.inner, bit) for p in part] for part in parts]
            places = places + [
                [[o ^ (self.outer << bit) for o in offs] for offs in place] for place in places
            ]
        return parts, places

    def whole(self):
        parts, places = self.parts()
        return place_blocks(parts, places, self.rows, self.piece, self.inner * self.outer)


def place_blocks(parts, places, rows, piece, blocks):
    count, pieces = len(parts), len(parts[0])
    where = {}
    for number, place in enumerate(places):
        for index, offs in enumerate(place):
            for k, o in enumerate(offs):
                where[(index, o)] = (number, k)
    me = lax.axis_index("dp") * (blocks // lax.axis_size("dp")) + lax.axis_index("fsdp")
    offsets = [o for place in places for o in place[0]]
    part_of = [[where[(i, o)][0] for o in offsets] for i in range(pieces)]
    slot_of = [[where[(i, o)][1] for o in offsets] for i in range(pieces)]
    goal = jnp.asarray(offsets, jnp.int32) ^ me.astype(jnp.int32)

    shown = []
    for i in range(pieces):
        for p in range(count):
            now, row = 0, []
            for step in range(blocks):
                if part_of[i][step] == p:
                    now = slot_of[i][step]
                row.append(now)
            shown.append(row)
    shown = jnp.asarray(shown, jnp.int32)
    part_table = jnp.asarray(part_of, jnp.int32)
    return pl.pallas_call(
        functools.partial(place_kernel, count, pieces, piece),
        out_shape=jax.ShapeDtypeStruct((blocks, rows, piece * pieces), parts[0][0].dtype),
        grid_spec=pltpu.PrefetchScalarGridSpec(
            num_scalar_prefetch=3,
            grid=(blocks,),
            in_specs=[
                pl.BlockSpec(
                    (1, rows, piece),
                    lambda b, goal, shown, part, n=i * count + p: (shown[n, b], 0, 0),
                )
                for i in range(pieces)
                for p in range(count)
            ],
            out_specs=pl.BlockSpec((1, rows, piece * pieces), lambda b, goal, shown, part: (goal[b], 0, 0)),
        ),
        compiler_params=pltpu.CompilerParams(vmem_limit_bytes=40 << 20),
        cost_estimate=pl.CostEstimate(
            flops=0,
            transcendentals=0,
            bytes_accessed=2 * blocks * rows * piece * pieces * parts[0][0].dtype.itemsize,
        ),
    )(goal, shown, part_table, *[parts[p][i] for i in range(pieces) for p in range(count)])


def place_kernel(count, pieces, piece, goal_ref, shown_ref, part_ref, *refs):
    target = refs[-1]
    step = pl.program_id(0)
    for i in range(pieces):
        for p in range(count):

            @pl.when(part_ref[i, step] == p)
            def _(i=i, source=refs[i * count + p]):
                target[:, :, i * piece : (i + 1) * piece] = source[...]


def halve(values, axis, axis_name, size, bit):
    mine = (lax.axis_index(axis_name) >> bit) & 1
    away = lax.dynamic_index_in_dim(values, 1 - mine, axis, keepdims=False)
    kept = lax.dynamic_index_in_dim(values, mine, axis, keepdims=False)
    come = swap(away, axis_name, size, bit)
    return (kept.astype(jnp.float32) + come.astype(jnp.float32)).astype(values.dtype)


def scatter_sum(values, inner_left, orders, inner, outer):
    blocks, rows, width = values.shape
    outer_bits = bit_count(outer)
    values = values.reshape((2,) * (inner_left + outer_bits) + (rows, width))
    for bit in reversed(range(inner_left)):
        values = halve(values, 0, "dp", inner, bit)
    piece = width // len(orders)
    done = []
    for number, order in enumerate(orders):
        part = values[..., number * piece : (number + 1) * piece]
        left = list(reversed(range(outer_bits)))
        for bit in order:
            part = halve(part, left.index(bit), "fsdp", outer, bit)
            left.remove(bit)
        done.append(part)
    return jnp.concatenate(done, axis=1) if len(done) > 1 else done[0]


def scatter_made(make, orders, inner, outer):
    top = bit_count(inner) - 1
    mine = (lax.axis_index("dp") >> top) & 1
    away = make(1 - mine)
    come = swap(away, "dp", inner, top)
    kept = make(mine)
    both = (kept.astype(jnp.float32) + come.astype(jnp.float32)).astype(kept.dtype)
    blocks = both.reshape(inner * outer // 2, -1, both.shape[1])
    return scatter_sum(blocks, top, orders, inner, outer).astype(jnp.float32)


def attention_kernel(q_ref, k_ref, v_ref, g_ref, bias_ref, att_ref, dq_ref, dk_ref, dv_ref):
    width = q_ref.shape[1]
    half = width // 2
    low, full = jnp.bfloat16, jnp.float32
    lanes = lax.broadcasted_iota(jnp.int32, (1, width), 1)
    sublanes = lax.broadcasted_iota(jnp.int32, (width, 1), 0)
    keys, values = k_ref[...], v_ref[...]
    att_t = dq_t = d_key = d_value = None

    def product(a, b, da, db):
        return lax.dot_general(a, b, (((da,), (db,)), ((), ())), preferred_element_type=full)

    for head in range(2):
        own = (lanes >= head * half) & (lanes < (head + 1) * half)
        query = jnp.where(own, q_ref[...], jnp.zeros((), low))
        grad = jnp.where(own, g_ref[...], jnp.zeros((), low))
        scores = product(keys, query, 1, 1) + bias_ref[...]
        exponent = jnp.exp(scores - jnp.max(scores, axis=0, keepdims=True))
        probs = exponent * (1.0 / jnp.sum(exponent, axis=0, keepdims=True))
        probs_low = probs.astype(low)
        att_head = product(values, probs_low, 0, 0)
        grad_probs = product(values, grad, 1, 1)
        inner_sum = jnp.sum(probs * grad_probs, axis=0, keepdims=True)
        grad_scores = (probs * (grad_probs - inner_sum)).astype(low)
        value_part = product(probs_low, grad, 1, 0)
        key_part = product(grad_scores, query, 1, 0)
        dq_head = product(keys, grad_scores, 0, 0)
        if head == 0:
            att_t, dq_t, d_key, d_value = att_head, dq_head, key_part, value_part
        else:
            upper = sublanes < half
            att_t = jnp.where(upper, att_t, att_head)
            dq_t = jnp.where(upper, dq_t, dq_head)
            d_key, d_value = d_key + key_part, d_value + value_part
    att_ref[...] = att_t.T.astype(low)
    dq_ref[...] = (dq_t.T * ((width // 2) ** -0.5)).astype(low)
    dk_ref[...] = d_key.astype(low)
    dv_ref[...] = d_value.astype(low)


def attention(query, keys, values, grad, bias):
    slots, width = query.shape
    count = keys.shape[0]
    pair = 2 * (width // HEADS)

    def columns(rows):
        return pl.BlockSpec((rows, pair), lambda h: (0, h))

    low = jnp.bfloat16
    return pl.pallas_call(
        attention_kernel,
        grid=(width // pair,),
        in_specs=[columns(slots), columns(count), columns(count), columns(slots)]
        + [pl.BlockSpec((count, slots), lambda h: (0, 0))],
        out_specs=[columns(slots), columns(slots), columns(count), columns(count)],
        out_shape=[
            jax.ShapeDtypeStruct((slots, width), low),
            jax.ShapeDtypeStruct((slots, width), low),
            jax.ShapeDtypeStruct((count, width), low),
            jax.ShapeDtypeStruct((count, width), low),
        ],
        compiler_params=pltpu.CompilerParams(vmem_limit_bytes=56 << 20),
        cost_estimate=pl.CostEstimate(
            flops=6 * 2 * 2 * slots * count * width,
            transcendentals=slots * count * HEADS,
            bytes_accessed=2 * width * (4 * slots + 4 * count) + 4 * slots * count,
        ),
    )(query, keys, values, grad, bias)


def layout(heights_row, widths_row):
    pixels = heights_row * widths_row
    ends_at = jnp.cumsum(pixels)
    starts_at = ends_at - pixels
    slot_ids = jnp.arange(SLOTS, dtype=jnp.int32)
    segment = jnp.sum((ends_at[None, :] <= slot_ids[:, None]).astype(jnp.int32), axis=1)
    member = segment[:, None] == jnp.arange(LAT_ROW, dtype=jnp.int32)[None, :]
    start_at = jnp.sum(jnp.where(member, starts_at[None, :], 0), axis=1)
    height_at = jnp.sum(jnp.where(member, heights_row[None, :], 0), axis=1)
    width_at = jnp.sum(jnp.where(member, widths_row[None, :], 0), axis=1)
    place_in = slot_ids - start_at
    safe_width = jnp.maximum(width_at, 1)
    column = place_in % safe_width
    row_index = place_in // safe_width
    return (segment, member, height_at, width_at, row_index, column)


def layer_norm(values):
    center = values - jnp.mean(values, axis=-1, keepdims=True)
    return center * lax.rsqrt(jnp.mean(center * center, axis=-1, keepdims=True) + NORM_EPS)


def depthwise(values, conv_taps, conv_bias, geometry):
    segment, member, height_at, width_at, row_index, column = geometry
    live_query = segment < LAT_ROW
    margin = 6 * SIDE_UNIT + 1
    padded = jnp.pad(values, ((0, 0), (margin, margin), (0, 0)))
    result = jnp.zeros_like(values) + conv_bias
    for step_y in (-1, 0, 1):
        for step_x in (-1, 0, 1):
            inside = live_query & (row_index + step_y >= 0) & (row_index + step_y < height_at)
            inside = inside & (column + step_x >= 0) & (column + step_x < width_at)
            weight_row = conv_taps[(step_y + 1) * 3 + step_x + 1]
            side_list = (1,) if step_y == 0 else (3 * SIDE_UNIT, 4 * SIDE_UNIT, 6 * SIDE_UNIT)
            for side_len in side_list:
                offset = step_y * side_len + step_x
                chosen = inside if step_y == 0 else inside & (width_at == side_len)
                shifted = lax.slice_in_dim(padded, margin + offset, margin + offset + SLOTS, axis=1)
                result = result + jnp.where(chosen[..., None], shifted, 0.0) * weight_row
    return result


def response_norm(hidden, grn_gain, grn_shift, onehot):
    active = jax.nn.gelu(hidden, approximate=False)
    power = jnp.einsum("rsl,rsf->rlf", onehot, active * active, precision=HIGHEST)
    global_norm = jnp.sqrt(power + NORM_EPS)
    scaled = global_norm / (jnp.mean(global_norm, axis=2, keepdims=True) + NORM_EPS)
    spread = jnp.einsum("rsl,rlf->rsf", onehot, scaled, precision=HIGHEST)
    return grn_gain * (active * spread) + grn_shift + active


def timestep(after_res, time_pair, onehot):
    per_slot = jnp.einsum("rsl,rlc->rsc", onehot, time_pair, precision=HIGHEST)
    half_width = time_pair.shape[-1] // 2
    return after_res + after_res * per_slot[..., :half_width] + per_slot[..., half_width:]


def score_bias(segment, counts_row, key_pad):
    live_query = segment < LAT_ROW
    image_ok = (segment[:, None] == segment[None, :]) & live_query[None, :]
    text_index = jnp.arange(LAT_ROW * TEXT, dtype=jnp.int32)
    text_latent = text_index // TEXT
    text_limit = jnp.sum(
        jnp.where(
            text_latent[:, None] == jnp.arange(LAT_ROW, dtype=jnp.int32)[None, :],
            counts_row[None, :],
            0,
        ),
        axis=1,
    )
    text_ok = (text_latent[:, None] == segment[None, :]) & (text_index % TEXT < text_limit)[:, None]
    no_pad = jnp.zeros((key_pad, segment.shape[0]), bool)
    return jnp.where(jnp.concatenate([image_ok, text_ok, no_pad], axis=0), 0.0, MASKED)


def local(
    inner,
    outer,
    latents,
    text_embed,
    time_embed,
    heights,
    widths,
    text_counts,
    res_vecs,
    fc1_w,
    ff_vecs,
    fc2_w,
    time_w,
    time_b,
    kv_w,
    attn_w,
    attn_vecs,
    cotangent,
):
    half_type = jnp.bfloat16
    orders = scatter_orders(outer)
    small_owned = (res_vecs, ff_vecs, time_w, time_b[None], attn_vecs)
    small_sizes = [v.size for v in small_owned]
    small_pad = -sum(small_sizes) % 1024
    small_shard = jnp.concatenate(
        [v.astype(half_type).reshape(-1) for v in small_owned] + [jnp.zeros((small_pad,), half_type)]
    )
    low_fc1, low_fc2, low_attn, low_kv = (
        v.astype(half_type) for v in (fc1_w.T, fc2_w, attn_w.T, kv_w)
    )
    steps = bit_count(outer)
    small_gather = Gather(small_shard.reshape(-1, 128), orders[:1], inner, outer)
    fc1_gather = Gather(low_fc1, orders, inner, outer)
    fc2_gather = Gather(low_fc2, orders, inner, outer)
    attn_gather = Gather(low_attn, orders, inner, outer)
    kv_gather = Gather(low_kv, orders[1:2], inner, outer)
    for number in range(steps):
        small_gather.step(number)
    ahead = ()
    for number in range(steps):
        came = fc1_gather.step(number)
        ahead = came if number == 1 else ahead
    for number in range(steps):
        came = fc2_gather.step(number, ahead if number == 0 else ())
        ahead = came if number == 1 else ahead
    for number in range(steps):
        attn_gather.step(number, ahead if number == 0 else ())
        kv_gather.step(number, ahead if number == 0 else ())
    small_all = small_gather.whole().reshape(inner * outer, -1)
    small_full = []
    taken = 0
    for owned, size in zip(small_owned, small_sizes):
        some = small_all[:, taken : taken + size].reshape(inner * outer, owned.shape[0], owned.shape[1])
        small_full.append(some.transpose(1, 0, 2).reshape(owned.shape[0], -1))
        taken += size
    res_all, ff_all, time_w_all, time_b_all, vecs_all = small_full

    def rows_of(gathered):
        whole = gathered.whole()
        return whole.reshape(-1, whole.shape[2])

    fc1_t = rows_of(fc1_gather)
    fc2_full = rows_of(fc2_gather)
    attn_t = rows_of(attn_gather)
    kv_full = rows_of(kv_gather)
    row_count, slot_count, model_width = latents.shape
    cond_width = text_embed.shape[3]
    head_dim = model_width // HEADS
    score_scale = head_dim ** (-0.5)
    geometry = jax.vmap(layout)(heights, widths)
    segment = geometry[0]
    onehot = geometry[1].astype(jnp.float32)
    live_mask = (segment < LAT_ROW).astype(jnp.float32)[..., None]
    text_count = LAT_ROW * TEXT
    key_pad = -(slot_count + text_count) % 128
    bias = score_bias(segment[0], text_counts[0], key_pad)
    res_vals = res_all.astype(jnp.float32)
    ff_vals = ff_all.astype(jnp.float32)

    def res_entry(values, conv_taps, conv_bias):
        return layer_norm(depthwise(values, conv_taps, conv_bias, geometry))

    normed, res_entry_back = jax.vjp(res_entry, latents, res_vals[:9], res_vals[9])
    normed_low = normed.astype(half_type)
    hidden = (
        jnp.einsum("rsc,fc->rsf", normed_low, fc1_t, preferred_element_type=jnp.float32)
        + ff_vals[0]
    )

    def grn_piece(hidden_in, grn_gain, grn_shift):
        return response_norm(hidden_in, grn_gain, grn_shift, onehot)

    response, grn_back = jax.vjp(grn_piece, hidden, ff_vals[1], ff_vals[2])
    response_low = response.astype(half_type)
    branch = (
        jnp.einsum("rsf,fc->rsc", response_low, fc2_full, preferred_element_type=jnp.float32)
        + res_vals[10]
    )
    after_res = latents + live_mask * branch
    mid_vals = vecs_all.astype(jnp.float32)
    time_low = time_embed.astype(half_type)
    time_pair = jnp.einsum(
        "rlt,tc->rlc", time_low, time_w_all, preferred_element_type=jnp.float32
    ) + time_b_all[0].astype(jnp.float32)

    def time_piece(after_in, pair_in):
        return timestep(after_in, pair_in, onehot)

    after_time, time_back = jax.vjp(time_piece, after_res, time_pair)
    normed_two, norm_two_back = jax.vjp(layer_norm, after_time)
    normed_two_low = normed_two.astype(half_type)
    text_flat = text_embed.astype(jnp.float32).reshape(row_count, LAT_ROW * TEXT, cond_width)
    silu_text, silu_back = jax.vjp(jax.nn.silu, text_flat)
    silu_low = silu_text.astype(half_type)
    mapped_low = (
        jnp.einsum("rtk,kc->rtc", silu_low, kv_full, preferred_element_type=jnp.float32)
        + mid_vals[3]
    ).astype(half_type)
    normed_row = normed_two_low[0]
    source_low = jnp.concatenate(
        [normed_row, mapped_low[0], jnp.zeros((key_pad, model_width), half_type)], axis=0
    )

    def along(spec, a, b):
        return jnp.einsum(spec, a, b, preferred_element_type=jnp.float32)

    w_query, w_key, w_value, w_out = (
        attn_t[i * model_width : (i + 1) * model_width] for i in range(4)
    )
    query_low = (along("sc,dc->sd", normed_row, w_query) + mid_vals[0]).astype(half_type)
    query_low = query_low * jnp.asarray(score_scale, half_type)
    key_low = along("kc,dc->kd", source_low, w_key).astype(half_type)
    value_low = (along("kc,dc->kd", source_low, w_value) + mid_vals[1]).astype(half_type)
    grad_proj = (live_mask * cotangent)[0].astype(half_type)
    grad_attended = along("sd,dc->sc", grad_proj, w_out).astype(half_type)
    attended_low, grad_query, grad_key, grad_value = attention(
        query_low, key_low, value_low, grad_attended, bias
    )
    output = after_time + live_mask * (along("sc,dc->sd", attended_low, w_out) + mid_vals[2])

    def long(values):
        return jnp.pad(values, ((0, source_low.shape[0] - slot_count), (0, 0)))

    query_long, proj_long, attended_long = long(grad_query), long(grad_proj), long(attended_low)

    def attn_half(half):
        first = half == 0
        one = along("kd,kc->dc", jnp.where(first, query_long, grad_value), source_low)
        two = along(
            "kd,kc->dc",
            jnp.where(first, grad_key, proj_long),
            jnp.where(first, source_low, attended_long),
        )
        return jnp.concatenate([one, two], axis=0).astype(half_type)

    attn_grad = scatter_made(attn_half, orders, inner, outer).T
    grad_bias_out = jnp.sum(grad_proj.astype(jnp.float32), axis=0)
    grad_bias_query = jnp.sum(grad_query.astype(jnp.float32), axis=0)
    grad_bias_value = jnp.sum(grad_value.astype(jnp.float32), axis=0)
    grad_source = along("kd,dc->kc", grad_key, w_key) + along("kd,dc->kc", grad_value, w_value)
    grad_normed_two = (along("sd,dc->sc", grad_query, w_query) + grad_source[:slot_count])[None]
    grad_mapped = grad_source[None, slot_count : slot_count + text_count].astype(half_type)
    grad_kv_w = jnp.einsum("rtk,rtc->kc", silu_low, grad_mapped, preferred_element_type=jnp.float32)
    grad_bias_kv = jnp.sum(grad_mapped.astype(jnp.float32), axis=(0, 1))
    grad_silu = jnp.einsum(
        "rtc,kc->rtk", grad_mapped, kv_full, preferred_element_type=jnp.float32
    )
    text_grad = silu_back(grad_silu)[0].reshape(row_count, LAT_ROW, TEXT, cond_width)
    grad_time = cotangent + norm_two_back(grad_normed_two)[0]
    grad_after_res, grad_pair = time_back(grad_time)
    grad_time_w = jnp.einsum(
        "rlt,rlc->tc", time_low.astype(jnp.float32), grad_pair, precision=HIGHEST
    )
    grad_time_b = jnp.sum(grad_pair, axis=(0, 1))
    grad_attn_vecs = jnp.stack([grad_bias_query, grad_bias_value, grad_bias_out, grad_bias_kv])

    kv_grad = scatter_sum(
        grad_kv_w.astype(half_type).reshape(inner * outer, -1, model_width),
        bit_count(inner),
        orders[1:2],
        inner,
        outer,
    ).astype(jnp.float32)
    grad_branch = (live_mask * grad_after_res).astype(half_type)
    hidden_half = response_low.shape[2] // 2

    def rows_half(left, right):
        def make(half):
            some = lax.dynamic_slice_in_dim(left, half * hidden_half, hidden_half, axis=1)
            return along("sf,sc->fc", some, right).astype(half_type)

        return make

    fc2_grad = scatter_made(rows_half(response_low[0], grad_branch[0]), orders, inner, outer)
    grad_fc2_bias = jnp.sum(grad_branch.astype(jnp.float32), axis=(0, 1))
    grad_response = jnp.einsum(
        "rsc,fc->rsf", grad_branch, fc2_full, preferred_element_type=jnp.float32
    )
    grad_hidden, grad_gain, grad_shift = grn_back(grad_response)
    grad_hidden_low = grad_hidden.astype(half_type)
    fc1_grad = scatter_made(rows_half(grad_hidden_low[0], normed_low[0]), orders, inner, outer).T
    grad_fc1_bias = jnp.sum(grad_hidden_low.astype(jnp.float32), axis=(0, 1))
    grad_normed = jnp.einsum(
        "rsf,fc->rsc", grad_hidden_low, fc1_t, preferred_element_type=jnp.float32
    )
    grad_entry, grad_taps, grad_conv_bias = res_entry_back(grad_normed)
    latents_grad = grad_after_res + grad_entry
    grad_res_vecs = jnp.concatenate([grad_taps, grad_conv_bias[None], grad_fc2_bias[None]], axis=0)
    grad_ff_vecs = jnp.stack([grad_fc1_bias, grad_gain, grad_shift])
    small_terms = (grad_res_vecs, grad_ff_vecs, grad_time_w, grad_time_b[None], grad_attn_vecs)
    small_blocks = jnp.concatenate(
        [
            g.reshape(g.shape[0], inner * outer, -1).transpose(1, 0, 2).reshape(inner * outer, -1)
            for g in small_terms
        ]
        + [jnp.zeros((inner * outer, small_pad), jnp.float32)],
        axis=1,
    ).reshape(inner * outer, -1, 128)
    small_sum = scatter_sum(small_blocks, bit_count(inner), orders[1:2], inner, outer).reshape(-1)
    small_grads = []
    taken = 0
    for owned, size in zip(small_owned, small_sizes):
        small_grads.append(small_sum[taken : taken + size].reshape(owned.shape))
        taken += size
    return (
        output,
        latents_grad,
        text_grad,
        small_grads[0],
        fc1_grad,
        small_grads[1],
        fc2_grad,
        small_grads[2],
        small_grads[3][0],
        kv_grad,
        attn_grad,
        small_grads[4],
    )


def solution(mesh):
    return jax.shard_map(
        functools.partial(local, mesh.shape["dp"], mesh.shape["fsdp"]),
        mesh=mesh,
        in_specs=(
            P(("dp", "fsdp"), None, None),
            P(("dp", "fsdp"), None, None, None),
            P(("dp", "fsdp"), None, None),
            P(("dp", "fsdp"), None),
            P(("dp", "fsdp"), None),
            P(("dp", "fsdp"), None),
            P(None, ("dp", "fsdp")),
            P(None, ("dp", "fsdp")),
            P(None, ("dp", "fsdp")),
            P(("dp", "fsdp"), None),
            P(None, ("dp", "fsdp")),
            P(("dp", "fsdp")),
            P(("dp", "fsdp"), None),
            P(None, ("dp", "fsdp")),
            P(None, ("dp", "fsdp")),
            P(("dp", "fsdp"), None, None),
        ),
        out_specs=(
            P(("dp", "fsdp"), None, None),
            P(("dp", "fsdp"), None, None),
            P(("dp", "fsdp"), None, None, None),
            P(None, ("dp", "fsdp")),
            P(None, ("dp", "fsdp")),
            P(None, ("dp", "fsdp")),
            P(("dp", "fsdp"), None),
            P(None, ("dp", "fsdp")),
            P(("dp", "fsdp")),
            P(("dp", "fsdp"), None),
            P(None, ("dp", "fsdp")),
            P(None, ("dp", "fsdp")),
        ),
        check_vma=False,
    )
```

```python
import functools

import jax
import jax.numpy as jnp
from jax import lax
from jax.experimental import pallas as pl
from jax.experimental.pallas import tpu as pltpu
from jax.sharding import PartitionSpec as P

HEADS = 24
TEXT = 77
SIDE_UNIT = 4
SLOTS = 576
LAT_ROW = 4
GROUP = 16
SEATS = 8

HEAD_SCALE = 64**-0.5
LANES = 128
UNITS = 768
HIGHEST = lax.Precision.HIGHEST
NORM_EPS = 1e-06
MASKED = -1000000000.0


def bit_count(size):
    return size.bit_length() - 1


def swap(values, axis_name, size, bit):
    return lax.ppermute(values, axis_name, [(i, i ^ (1 << bit)) for i in range(size)])


def scatter_orders(size):
    bits = list(range(bit_count(size) - 1))
    return [bits[turn:] + bits[:turn] + [len(bits)] for turn in range(3)]


def column_pieces(width, count):
    if count == 1:
        return [(0, width)]
    unit = width // 12
    return [(0, 5 * unit), (5 * unit, 5 * unit), (10 * unit, 2 * unit)]


class Chain:
    def __init__(self):
        self.token = None

    def call(self, kernel, grid, ins, outs, scratch, *operands, scalars=()):
        earlier = () if self.token is None else (self.token,)
        held, count = len(scalars), len(operands)

        def body(*refs):
            before, rest = refs[: held + count], refs[held + count + len(earlier) :]
            rest[len(outs)][...] = jnp.zeros_like(rest[len(outs)])
            kernel(*before, *rest[: len(outs)], *rest[len(outs) + 1 :])

        token_spec = pl.BlockSpec((8, 128), lambda *_: (0, 0))
        done = pl.pallas_call(
            body,
            grid_spec=pltpu.PrefetchScalarGridSpec(
                num_scalar_prefetch=held,
                grid=grid,
                in_specs=list(ins) + [pl.BlockSpec(memory_space=pl.ANY)] * len(earlier),
                out_specs=[spec for _, _, spec in outs] + [token_spec],
                scratch_shapes=list(scratch),
            ),
            out_shape=[jax.ShapeDtypeStruct(shape, dtype) for shape, dtype, _ in outs]
            + [jax.ShapeDtypeStruct((8, 128), jnp.float32)],
            compiler_params=pltpu.CompilerParams(vmem_limit_bytes=56 << 20),
        )(*scalars, *operands, *earlier)
        self.token = done[-1]
        return done[:-1]


def whole_array(shape):
    return pl.BlockSpec(shape, lambda *_: (0,) * len(shape))


class Weight:
    def __init__(self, gathered, place, rows, block=lambda step: step):
        if rows % GROUP:
            some = gathered[:, place * rows : (place + 1) * rows]
            gathered, place, rows = some.reshape(-1, UNITS, some.shape[2]), 0, UNITS
        self.gathered, self.place, self.rows, self.block = gathered, place, rows, block
        self.total = gathered.shape[0] * rows
        self.width = gathered.shape[2]

    def by(self, block):
        return Weight(self.gathered, self.place, self.rows, block)

    def spec(self):
        return pl.BlockSpec(
            (UNITS // self.rows, self.rows, self.width), lambda i, *_: (self.block(i), self.place, 0)
        )


def rows_of(ref):
    return ref[...].reshape(UNITS, ref.shape[2])


class Piece:
    def __init__(self, base, order, bits, cut=0, width=None):
        self.base, self.order, self.bits, self.cut = base, list(order), list(bits), cut
        self.free, self.fixed, self.come = list(bits), [], None
        self.width = base.shape[-1] if width is None else width


def fold(chain, pieces, inner, outer):
    if len(pieces[0].free) == 1:
        return fold_last(chain, pieces, inner, outer)
    low_bits = bit_count(outer)
    me = lax.axis_index("dp") * outer + lax.axis_index("fsdp")
    left = len(pieces[0].free) - 1
    inside = min(max(left - 1, 0), 2)
    ins, outs, operands, plans, bits = [], [], [], [], []
    for piece in pieces:
        lazy = piece.come is None
        bit = piece.order.pop(0)
        bits.append(bit)
        rest = [b for b in piece.free if b != bit]
        near = rest[len(rest) - inside :]
        far = rest[: len(rest) - inside]

        def spec(axes, cut, width, rows, bit=bit, near=near, far=far, fixed=tuple(piece.fixed), lazy=lazy):
            def where(k, me_ref):
                place = []
                for b in axes:
                    if b in fixed:
                        place.append((me_ref[0] >> b) & 1)
                    elif b == bit:
                        place.append(1 - ((me_ref[0] >> b) & 1) if lazy else 0)
                    elif b in near:
                        place.append(0)
                    else:
                        place.append((k >> (len(far) - 1 - far.index(b))) & 1)
                return tuple(place) + (0, cut)

            shape = tuple(
                2 if (b in near and b not in fixed) or (b == bit and not lazy) else None for b in axes
            )
            return pl.BlockSpec(shape + (rows, width), where)

        rows = piece.base.shape[-2]
        ins.append(spec(piece.bits, piece.cut, piece.width, rows))
        operands.append(piece.base)
        if not lazy:
            ins.append(spec(piece.free, 0, piece.width, rows))
            operands.append(piece.come)
        shape = (2,) * len(rest) + (rows, piece.width)
        outs += [(shape, piece.base.dtype, spec(rest, 0, piece.width, rows))] * (1 if lazy else 2)
        plans.append((lazy, bit, sum(1 for b in near if b > bit)))
        piece.free = rest
    done = list(
        chain.call(
            functools.partial(fold_kernel, plans),
            (1 << (left - inside),),
            ins,
            outs,
            [],
            *operands,
            scalars=(me.astype(jnp.int32)[None],),
        )
    )
    for piece, (lazy, bit, _) in zip(pieces, plans):
        away = done.pop(0)
        if lazy:
            piece.fixed.append(bit)
        else:
            piece.base, piece.cut, piece.fixed, piece.bits = done.pop(0), 0, [], list(piece.free)
        if bit < low_bits:
            piece.come = swap(away, "fsdp", outer, bit)
        else:
            piece.come = swap(away, "dp", inner, bit - low_bits)


def fold_kernel(plans, me_ref, *refs):
    count = sum(1 if lazy else 2 for lazy, _, _ in plans)
    ins, outs = list(refs[:count]), list(refs[count:])
    for lazy, bit, before in plans:
        if lazy:
            outs.pop(0)[...] = ins.pop(0)[...]
            continue
        base, come = ins.pop(0), ins.pop(0)
        own = (me_ref[0] >> bit) & 1
        for out, side in ((outs.pop(0), 1 - own), (outs.pop(0), own)):
            at = (slice(None),) * before + (side,)
            out[...] = (base[at].astype(jnp.float32) + come[at].astype(jnp.float32)).astype(out.dtype)


def turn_kernel(values_ref, late_ref, out_ref):
    out_ref[...] = values_ref[...].T.astype(jnp.bfloat16)


def turn_late(chain, values, late):
    shape = values.shape[::-1]
    return chain.call(
        turn_kernel,
        (1,),
        [whole_array(values.shape), pl.BlockSpec(memory_space=pl.ANY)],
        [(shape, jnp.bfloat16, whole_array(shape))],
        [],
        values,
        late,
    )[0]


def last_kernel(cuts, bit, me_ref, *refs):
    own = (me_ref[0] >> bit) & 1
    ins, outs = refs[: 2 * len(cuts)], refs[2 * len(cuts) :]
    for n, (group, cut) in enumerate(cuts):
        both = ins[2 * n][...].astype(jnp.float32) + ins[2 * n + 1][...].astype(jnp.float32)
        both = both.astype(outs[2 * group].dtype)
        outs[2 * group][:, :, cut] = jnp.where(own == 0, both[1:2], both[0:1])
        outs[2 * group + 1][:, :, cut] = jnp.where(own == 0, both[0:1], both[1:2])


def fold_last(chain, pieces, inner, outer):
    bit = pieces[0].order.pop(0)
    me = lax.axis_index("dp") * outer + lax.axis_index("fsdp")
    operands, cuts, shapes = [], [], []
    for piece in pieces:
        operands += [piece.base, piece.come]
        rows = piece.base.shape[1]
        if not shapes or shapes[-1][1] != rows:
            shapes.append([1, rows, 0])
        start = shapes[-1][2]
        cuts.append((len(shapes) - 1, slice(start, start + piece.width)))
        shapes[-1][2] = start + piece.width
    dtypes = {piece.base.shape[1]: piece.base.dtype for piece in pieces}
    done = chain.call(
        functools.partial(last_kernel, cuts, bit),
        (1,),
        [whole_array(v.shape) for v in operands],
        [(tuple(shape), dtypes[shape[1]], whole_array(tuple(shape))) for shape in shapes for _ in range(2)],
        [],
        *operands,
        scalars=(me.astype(jnp.int32)[None],),
    )
    pieces[:] = [Piece(kept, [], []) for kept in done[1::2]]
    for piece, away in zip(pieces, done[::2]):
        piece.come = swap(away, "fsdp", outer, bit)


def total_kernel(turned, *refs):
    for n, turn in enumerate(turned):
        total = (refs[2 * n][...].astype(jnp.float32) + refs[2 * n + 1][...].astype(jnp.float32))[0]
        refs[2 * len(turned) + n][...] = total.T if turn else total


def totals_of(chain, pieces, turned):
    shapes = [
        piece.base.shape[:0:-1] if turn else piece.base.shape[1:] for piece, turn in zip(pieces, turned)
    ]
    operands = [v for piece in pieces for v in (piece.base, piece.come)]
    return chain.call(
        functools.partial(total_kernel, turned),
        (1,),
        [whole_array(v.shape) for v in operands],
        [(shape, jnp.float32, whole_array(shape)) for shape in shapes],
        [],
        *operands,
    )


def product(a, b, da, db):
    return lax.dot_general(a, b, (((da,), (db,)), ((), ())), preferred_element_type=jnp.float32)


def by_group(values):
    return values.reshape(values.shape[0] // GROUP, GROUP, values.shape[1])


def spread(seats, member):
    total = member[:, 0:1] * seats[0:1, :]
    for place in range(1, LAT_ROW):
        total = total + member[:, place : place + 1] * seats[place : place + 1, :]
    return total[:, None, :]


def gathered(values, member):
    by = jnp.sum(by_group(values), axis=1)
    rows = [jnp.sum(by * member[:, place : place + 1], axis=0, keepdims=True) for place in range(LAT_ROW)]
    return jnp.concatenate(rows + [jnp.zeros((SEATS - LAT_ROW, values.shape[1]), jnp.float32)], axis=0)


def neighbours(x, geometry):
    slots = x.shape[0]
    above = below = None
    for index, side in enumerate((3 * SIDE_UNIT, 4 * SIDE_UNIT, 6 * SIDE_UNIT)):
        up = geometry[3 + index] * pltpu.roll(x, side, 0)
        down = geometry[6 + index] * pltpu.roll(x, slots - side, 0)
        above = up if above is None else above + up
        below = down if below is None else below + down
    return above, geometry[0] * x, below


def geometry_columns(geometry_ref):
    return [geometry_ref[:, k : k + 1] for k in range(9)]


def entry_kernel(x_ref, taps_ref, geometry_ref, low_ref, normed_ref, scale_ref, conv_ref):
    slots, width = x_ref.shape
    geometry = geometry_columns(geometry_ref)
    total = jnp.zeros((slots, LANES), jnp.float32)
    for start in range(0, width, LANES):
        cut = slice(start, start + LANES)
        rows = neighbours(x_ref[:, cut], geometry)
        left, mid, right = (
            sum(taps_ref[3 * a + b : 3 * a + b + 1, cut] * rows[a] for a in range(3)) for b in range(3)
        )
        conv = (
            taps_ref[9:10, cut]
            + mid
            + geometry[1] * pltpu.roll(left, 1, 0)
            + geometry[2] * pltpu.roll(right, slots - 1, 0)
        )
        conv_ref[:, cut] = conv
        total = total + conv
    mean = jnp.sum(total, axis=1, keepdims=True) * (1.0 / width)
    square = jnp.zeros((slots, LANES), jnp.float32)
    for start in range(0, width, LANES):
        center = conv_ref[:, start : start + LANES] - mean
        square = square + center * center
    scale = lax.rsqrt(jnp.sum(square, axis=1, keepdims=True) * (1.0 / width) + NORM_EPS)
    scale_ref[...] = jnp.broadcast_to(scale, scale_ref.shape)
    for start in range(0, width, LANES):
        cut = slice(start, start + LANES)
        normed = (conv_ref[:, cut] - mean) * scale
        normed_ref[:, cut] = normed
        low_ref[:, cut] = normed.astype(jnp.bfloat16)


def entry(chain, x, taps, geometry):
    slots, width = x.shape
    return chain.call(
        entry_kernel,
        (1,),
        [whole_array(v.shape) for v in (x, taps, geometry)],
        [
            ((slots, width), jnp.bfloat16, whole_array((slots, width))),
            ((slots, width), jnp.float32, whole_array((slots, width))),
            ((slots, LANES), jnp.float32, whole_array((slots, LANES))),
        ],
        [pltpu.VMEM((slots, width), jnp.float32)],
        x,
        taps,
        geometry,
    )


def entry_back_kernel(q_ref, normed_ref, scale_ref, x_ref, res_ref, taps_ref, geometry_ref, bias_grad_ref, grad_ref, taps_grad_ref):
    slots, width = x_ref.shape
    geometry = geometry_columns(geometry_ref)
    scale = scale_ref[:, 0:1]
    plain = jnp.zeros((slots, LANES), jnp.float32)
    along = jnp.zeros((slots, LANES), jnp.float32)
    for start in range(0, width, LANES):
        cut = slice(start, start + LANES)
        q = q_ref[:, cut]
        plain = plain + q
        along = along + q * normed_ref[:, cut]
    plain = jnp.sum(plain, axis=1, keepdims=True) * (1.0 / width)
    along = jnp.sum(along, axis=1, keepdims=True) * (1.0 / width)
    for start in range(0, width, LANES):
        cut = slice(start, start + LANES)
        grad = (q_ref[:, cut] - plain - normed_ref[:, cut] * along) * scale
        sides = (
            pltpu.roll(grad * geometry[1], slots - 1, 0),
            grad,
            pltpu.roll(grad * geometry[2], 1, 0),
        )
        rows = neighbours(x_ref[:, cut], geometry)
        sums = [
            jnp.sum(rows[a] * sides[b], axis=0, keepdims=True) for a in range(3) for b in range(3)
        ]
        sums.append(jnp.sum(grad, axis=0, keepdims=True))
        sums.append(bias_grad_ref[0:1, cut])
        sums.append(jnp.zeros((5, LANES), jnp.float32))
        taps_grad_ref[:, cut] = jnp.concatenate(sums, axis=0)
        above, mid, below = (
            sum(taps_ref[3 * a + b : 3 * a + b + 1, cut] * sides[b] for b in range(3)) for a in range(3)
        )
        back = res_ref[:, cut] + geometry[0] * mid
        for index, side in enumerate((3 * SIDE_UNIT, 4 * SIDE_UNIT, 6 * SIDE_UNIT)):
            back = back + pltpu.roll(geometry[3 + index] * above, slots - side, 0)
            back = back + pltpu.roll(geometry[6 + index] * below, side, 0)
        grad_ref[:, cut] = back


def entry_back(chain, q, normed, scale, x, res, taps, geometry, bias_grad):
    slots, width = x.shape
    operands = (q, normed, scale, x, res, taps, geometry, bias_grad)
    return chain.call(
        entry_back_kernel,
        (1,),
        [whole_array(v.shape) for v in operands],
        [
            ((slots, width), jnp.float32, whole_array((slots, width))),
            ((16, width), jnp.float32, whole_array((16, width))),
        ],
        [],
        *operands,
    )


def hidden_kernel(normed_ref, vecs_ref, member_ref, *refs):
    weight_ref, act_ref, slope_ref, power_ref = refs
    hidden = product(normed_ref[...], rows_of(weight_ref), 1, 1) + vecs_ref[0:1, :]
    below = 0.5 + 0.5 * lax.erf(hidden * (0.5**0.5))
    act = hidden * below
    act_ref[...] = act
    slope_ref[...] = below + hidden * (jnp.exp(-0.5 * hidden * hidden) * (0.5 / jnp.pi) ** 0.5)
    power_ref[...] = gathered(act * act, member_ref[...])


def unit_columns(rows):
    return pl.BlockSpec((rows, UNITS), lambda i, *_: (0, i))


def hidden_step(chain, normed, weight, vecs, member):
    slots, width = normed.shape
    units = weight.total
    return chain.call(
        hidden_kernel,
        (units // UNITS,),
        [whole_array((slots, width)), unit_columns(vecs.shape[0]), whole_array(member.shape)] + [weight.spec()],
        [
            ((slots, units), jnp.float32, unit_columns(slots)),
            ((slots, units), jnp.float32, unit_columns(slots)),
            ((SEATS, units), jnp.float32, unit_columns(SEATS)),
        ],
        [],
        normed,
        vecs,
        member,
        weight.gathered,
    )


def norm_rows(values):
    center = values - jnp.mean(values, axis=-1, keepdims=True)
    scale = lax.rsqrt(jnp.mean(center * center, axis=-1, keepdims=True) + NORM_EPS)
    return center * scale, scale


def branch_kernel(act_ref, norms_ref, vecs_ref, member_ref, live_ref, x_ref, bias_ref, pair_ref, *refs):
    weight_ref, response_ref, res_ref, time_ref, low_ref, total_ref = refs
    step = pl.program_id(0)
    member = member_ref[...]
    act = by_group(act_ref[...])
    response = act * (1.0 + vecs_ref[1:2, :][None] * spread(norms_ref[...], member)) + vecs_ref[2:3, :][None]
    response = response.reshape(act_ref.shape).astype(jnp.bfloat16)
    response_ref[...] = response
    part = product(response, rows_of(weight_ref), 1, 0)

    @pl.when(step == 0)
    def _():
        total_ref[...] = part

    @pl.when(step > 0)
    def _():
        total_ref[...] += part

    @pl.when(step == pl.num_programs(0) - 1)
    def _():
        width = x_ref.shape[1]
        after_res = x_ref[...] + live_ref[:, 0:1] * (total_ref[...] + bias_ref[...])
        res_ref[...] = after_res
        per = spread(pair_ref[...], member)
        after_time = by_group(after_res) * (1.0 + per[:, :, :width]) + per[:, :, width:]
        after_time = after_time.reshape(after_res.shape)
        time_ref[...] = after_time
        low_ref[...] = norm_rows(after_time)[0].astype(jnp.bfloat16)


def branch_step(chain, act, norms, vecs, weight, member, live, x, bias, pair):
    slots, units = act.shape
    width = x.shape[1]
    return chain.call(
        branch_kernel,
        (units // UNITS,),
        [
            unit_columns(slots),
            unit_columns(SEATS),
            unit_columns(vecs.shape[0]),
            whole_array(member.shape),
            whole_array(live.shape),
            whole_array(x.shape),
            whole_array(bias.shape),
            whole_array(pair.shape),
        ]
        + [weight.spec()],
        [
            ((slots, units), jnp.bfloat16, unit_columns(slots)),
            ((slots, width), jnp.float32, whole_array((slots, width))),
            ((slots, width), jnp.float32, whole_array((slots, width))),
            ((slots, width), jnp.bfloat16, whole_array((slots, width))),
        ],
        [pltpu.VMEM((slots, width), jnp.float32)],
        act,
        norms,
        vecs,
        member,
        live,
        x,
        bias,
        pair,
        weight.gathered,
    )


def time_back_kernel(q_ref, time_ref, res_ref, cot_ref, pair_ref, member_ref, live_ref, grad_ref, low_ref, pair_grad_ref, bias_grad_ref):
    width = q_ref.shape[1]
    member = member_ref[...]
    normed, scale = norm_rows(time_ref[...])
    q = q_ref[...]
    plain = jnp.mean(q, axis=-1, keepdims=True)
    along = jnp.mean(q * normed, axis=-1, keepdims=True)
    grad_time = cot_ref[...] + (q - plain - normed * along) * scale
    pair_grad_ref[:, :width] = gathered(grad_time * res_ref[...], member)
    pair_grad_ref[:, width:] = gathered(grad_time, member)
    per = spread(pair_ref[:, :width], member)
    grad_res = (by_group(grad_time) * (1.0 + per)).reshape(q.shape)
    grad_ref[...] = grad_res
    low = (live_ref[:, 0:1] * grad_res).astype(jnp.bfloat16)
    low_ref[...] = low
    bias_grad_ref[...] = jnp.broadcast_to(jnp.sum(low.astype(jnp.float32), axis=0, keepdims=True), bias_grad_ref.shape)


def time_back(chain, q, after_time, after_res, cot, pair, member, live):
    slots, width = q.shape
    operands = (q, after_time, after_res, cot, pair, member, live)
    return chain.call(
        time_back_kernel,
        (1,),
        [whole_array(v.shape) for v in operands],
        [
            ((slots, width), jnp.float32, whole_array((slots, width))),
            ((slots, width), jnp.bfloat16, whole_array((slots, width))),
            ((SEATS, 2 * width), jnp.float32, whole_array((SEATS, 2 * width))),
            ((SEATS, width), jnp.float32, whole_array((SEATS, width))),
        ],
        [],
        *operands,
    )


def response_back_kernel(branch_ref, act_ref, member_ref, *refs):
    weight_ref, grad_ref, sums_ref, shift_ref = refs
    grad = product(branch_ref[...], rows_of(weight_ref), 1, 1)
    grad_ref[...] = grad
    sums_ref[...] = gathered(grad * act_ref[...], member_ref[...])
    shift_ref[...] = jnp.broadcast_to(jnp.sum(grad, axis=0, keepdims=True), shift_ref.shape)


def response_back(chain, branch, weight, act, member):
    slots, width = branch.shape
    units = weight.total
    return chain.call(
        response_back_kernel,
        (units // UNITS,),
        [whole_array(branch.shape), unit_columns(slots), whole_array(member.shape)] + [weight.spec()],
        [
            ((slots, units), jnp.float32, unit_columns(slots)),
            ((SEATS, units), jnp.float32, unit_columns(SEATS)),
            ((SEATS, units), jnp.float32, unit_columns(SEATS)),
        ],
        [],
        branch,
        act,
        member,
        weight.gathered,
    )


def hidden_back_kernel(grad_ref, act_ref, slope_ref, vecs_ref, norms_ref, ratio_ref, member_ref, *refs):
    weight_ref, low_ref, bias_ref, normed_grad_ref, total_ref = refs
    step = pl.program_id(0)
    member = member_ref[...]
    grad = by_group(grad_ref[...]) * (1.0 + vecs_ref[1:2, :][None] * spread(norms_ref[...], member))
    grad = grad + by_group(act_ref[...]) * spread(ratio_ref[...], member)
    low = (grad.reshape(act_ref.shape) * slope_ref[...]).astype(jnp.bfloat16)
    low_ref[...] = low
    bias_ref[...] = jnp.broadcast_to(jnp.sum(low.astype(jnp.float32), axis=0, keepdims=True), bias_ref.shape)
    part = product(low, rows_of(weight_ref), 1, 0)

    @pl.when(step == 0)
    def _():
        total_ref[...] = part

    @pl.when(step > 0)
    def _():
        total_ref[...] += part

    @pl.when(step == pl.num_programs(0) - 1)
    def _():
        normed_grad_ref[...] = total_ref[...]


def hidden_back(chain, grad, act, slope, vecs, norms, ratio, member, weight):
    slots, units = act.shape
    width = weight.width
    return chain.call(
        hidden_back_kernel,
        (units // UNITS,),
        [unit_columns(slots)] * 3
        + [unit_columns(vecs.shape[0]), unit_columns(SEATS), unit_columns(SEATS)]
        + [whole_array(member.shape)]
        + [weight.spec()],
        [
            ((slots, units), jnp.bfloat16, unit_columns(slots)),
            ((SEATS, units), jnp.float32, unit_columns(SEATS)),
            ((slots, width), jnp.float32, whole_array((slots, width))),
        ],
        [pltpu.VMEM((slots, width), jnp.float32)],
        grad,
        act,
        slope,
        vecs,
        norms,
        ratio,
        member,
        weight.gathered,
    )


def project_kernel(source_ref, grad_ref, bias_ref, *refs):
    weight_ref, out_ref, att_grad_ref, total_ref = refs
    step = pl.program_id(0)
    each = pl.num_programs(0) // 4
    weight = rows_of(weight_ref)

    @pl.when(step < 3 * each)
    def _():
        out = (product(source_ref[...], weight, 1, 1) + bias_ref[0:1, :]).astype(jnp.bfloat16)
        scale = jnp.where(step < each, HEAD_SCALE, 1.0).astype(jnp.bfloat16)
        out_ref[...] = out * scale

    @pl.when(step >= 3 * each)
    def _():
        part = product(grad_ref[...], weight, 1, 0)

        @pl.when(step == 3 * each)
        def _():
            total_ref[...] = part

        @pl.when(step > 3 * each)
        def _():
            total_ref[...] += part

        @pl.when(step == 4 * each - 1)
        def _():
            att_grad_ref[...] = total_ref[...].astype(jnp.bfloat16)


def project(chain, source, grad, bias, weight):
    count, width = source.shape
    slots = grad.shape[0]
    each = width // UNITS
    return chain.call(
        project_kernel,
        (4 * each,),
        [
            whole_array(source.shape),
            pl.BlockSpec((slots, UNITS), lambda i, *_: (0, jnp.maximum(i - 3 * each, 0))),
            pl.BlockSpec((SEATS, UNITS), lambda i, *_: (0, jnp.minimum(i, 3 * each - 1))),
        ]
        + [weight.spec()],
        [
            (
                (count, 3 * width),
                jnp.bfloat16,
                pl.BlockSpec((count, UNITS), lambda i, *_: (0, jnp.minimum(i, 3 * each - 1))),
            ),
            ((slots, width), jnp.bfloat16, whole_array((slots, width))),
        ],
        [pltpu.VMEM((slots, width), jnp.float32)],
        source,
        grad,
        bias,
        weight.gathered,
    )


def source_back_kernel(query_ref, key_ref, value_ref, *refs):
    weight_ref, slot_ref, text_ref, total_ref = refs
    step = pl.program_id(0)
    each = pl.num_programs(0) // 3
    slots = slot_ref.shape[0]
    weight = rows_of(weight_ref)

    @pl.when(step == 0)
    def _():
        total_ref[...] = product(key_ref[...], weight, 1, 0)

    @pl.when((step > 0) & (step < each))
    def _():
        total_ref[...] += product(key_ref[...], weight, 1, 0)

    @pl.when((step >= each) & (step < 2 * each))
    def _():
        total_ref[...] += product(value_ref[...], weight, 1, 0)

    @pl.when(step >= 2 * each)
    def _():
        total_ref[:slots, :] += product(query_ref[...], weight, 1, 0)

    @pl.when(step == 3 * each - 1)
    def _():
        slot_ref[...] = total_ref[:slots, :]
        text_ref[...] = total_ref[slots:, :].astype(jnp.bfloat16)


def source_back(chain, query, keys, values, weight):
    slots, width = query.shape
    count = keys.shape[0]
    each = width // UNITS

    def columns(rows, turn):
        return pl.BlockSpec((rows, UNITS), lambda i, *_: (0, jnp.clip(i - turn * each, 0, each - 1)))

    return chain.call(
        source_back_kernel,
        (3 * each,),
        [columns(slots, 2), columns(count, 0), columns(count, 1)]
        + [weight.spec()],
        [
            ((slots, width), jnp.float32, whole_array((slots, width))),
            ((count - slots, width), jnp.bfloat16, whole_array((count - slots, width))),
        ],
        [pltpu.VMEM((count, width), jnp.float32)],
        query,
        keys,
        values,
        weight.gathered,
    )


def output_kernel(attended_ref, time_ref, live_ref, bias_ref, weight_ref, out_ref):
    out = product(attended_ref[...], rows_of(weight_ref), 1, 1) + bias_ref[0:1, :]
    out_ref[...] = time_ref[...] + live_ref[:, 0:1] * out


def output_step(chain, attended, after_time, live, bias, weight):
    slots, width = attended.shape
    each = width // UNITS
    columns = pl.BlockSpec((slots, UNITS), lambda i, *_: (0, i))
    return chain.call(
        output_kernel,
        (each,),
        [
            whole_array(attended.shape),
            columns,
            whole_array(live.shape),
            pl.BlockSpec((SEATS, UNITS), lambda i, *_: (0, i)),
        ]
        + [weight.spec()],
        [((slots, width), jnp.float32, columns)],
        [],
        attended,
        after_time,
        live,
        bias,
        weight.gathered,
    )[0]


def half_kernel(added, half_ref, left_ref, right_ref, *refs):
    total = product(left_ref[...], right_ref[...], 0, 0)
    if added:
        total = total + refs[0][...].astype(jnp.float32)
    refs[-1][...] = total.astype(jnp.bfloat16)


def half_rows(chain, left, right, half, come=None):
    slots, units = left.shape
    width = right.shape[1]
    steps = units // 2 // UNITS
    rows = pl.BlockSpec((UNITS, width), lambda i, *_: (i, 0))
    return chain.call(
        functools.partial(half_kernel, come is not None),
        (steps,),
        [
            pl.BlockSpec((slots, UNITS), lambda i, half_ref: (0, half_ref[0] * steps + i)),
            whole_array(right.shape),
        ]
        + ([] if come is None else [rows]),
        [((units // 2, width), jnp.bfloat16, rows)],
        [],
        left,
        right,
        *(() if come is None else (come,)),
        scalars=(half.astype(jnp.int32)[None],),
    )[0]


def attn_half_kernel(added, half_ref, query_ref, key_ref, value_ref, proj_ref, source_ref, attended_ref, *refs):
    out_ref = refs[-1]
    role = 2 * half_ref[0] + pl.program_id(0) // (pl.num_programs(0) // 2)
    slots = query_ref.shape[0]

    def store(total):
        if added:
            total = total + refs[0][...].astype(jnp.float32)
        out_ref[...] = total.astype(jnp.bfloat16)

    @pl.when(role == 0)
    def _():
        store(product(query_ref[...], source_ref[:slots, :], 0, 0))

    @pl.when(role == 1)
    def _():
        store(product(key_ref[...], source_ref[...], 0, 0))

    @pl.when(role == 2)
    def _():
        store(product(value_ref[...], source_ref[...], 0, 0))

    @pl.when(role == 3)
    def _():
        store(product(proj_ref[...], attended_ref[...], 0, 0))


def attn_half(chain, query, keys, values, proj, source, attended, half, come=None):
    width = source.shape[1]
    each = width // UNITS
    rows = pl.BlockSpec((UNITS, width), lambda i, *_: (i, 0))

    def columns(values, role):
        def where(i, half_ref):
            return (0, jnp.where(2 * half_ref[0] + i // each == role, i % each, 0))

        return pl.BlockSpec((values.shape[0], UNITS), where)

    return chain.call(
        functools.partial(attn_half_kernel, come is not None),
        (2 * each,),
        [columns(v, n) for n, v in enumerate((query, keys, values, proj))]
        + [whole_array(source.shape), whole_array(attended.shape)]
        + ([] if come is None else [rows]),
        [((2 * width, width), jnp.bfloat16, rows)],
        [],
        query,
        keys,
        values,
        proj,
        source,
        attended,
        *(() if come is None else (come,)),
        scalars=(half.astype(jnp.int32)[None],),
    )[0]


def attention_kernel(q_ref, k_ref, v_ref, g_ref, bias_ref, att_ref, dq_ref, dk_ref, dv_ref):
    width = q_ref.shape[1]
    half = width // 2
    low = jnp.bfloat16
    lanes = lax.broadcasted_iota(jnp.int32, (1, width), 1)
    sublanes = lax.broadcasted_iota(jnp.int32, (width, 1), 0)
    keys, values = k_ref[...], v_ref[...]
    att_t = dq_t = d_key = d_value = None

    for head in range(2):
        own = (lanes >= head * half) & (lanes < (head + 1) * half)
        query = jnp.where(own, q_ref[...], jnp.zeros((), low))
        grad = jnp.where(own, g_ref[...], jnp.zeros((), low))
        scores = product(keys, query, 1, 1) + bias_ref[...]
        exponent = jnp.exp(scores - jnp.max(scores, axis=0, keepdims=True))
        probs = exponent * (1.0 / jnp.sum(exponent, axis=0, keepdims=True))
        probs_low = probs.astype(low)
        att_head = product(values, probs_low, 0, 0)
        grad_probs = product(values, grad, 1, 1)
        inner_sum = jnp.sum(probs * grad_probs, axis=0, keepdims=True)
        grad_scores = (probs * (grad_probs - inner_sum)).astype(low)
        value_part = product(probs_low, grad, 1, 0)
        key_part = product(grad_scores, query, 1, 0)
        dq_head = product(keys, grad_scores, 0, 0)
        if head == 0:
            att_t, dq_t, d_key, d_value = att_head, dq_head, key_part, value_part
        else:
            upper = sublanes < half
            att_t = jnp.where(upper, att_t, att_head)
            dq_t = jnp.where(upper, dq_t, dq_head)
            d_key, d_value = d_key + key_part, d_value + value_part
    att_ref[...] = att_t.T.astype(low)
    dq_ref[...] = (dq_t.T * ((width // 2) ** -0.5)).astype(low)
    dk_ref[...] = d_key.astype(low)
    dv_ref[...] = d_value.astype(low)


def attention(chain, mixed, grad, bias):
    slots, width = grad.shape
    count = mixed.shape[0]
    pair = 2 * (width // HEADS)
    each = width // pair

    def columns(rows, turn=0):
        return pl.BlockSpec((rows, pair), lambda h, *_: (0, turn * each + h))

    low = jnp.bfloat16
    return chain.call(
        attention_kernel,
        (each,),
        [columns(slots), columns(count, 1), columns(count, 2), columns(slots), whole_array(bias.shape)],
        [
            ((slots, width), low, columns(slots)),
            ((slots, width), low, columns(slots)),
            ((count, width), low, columns(count)),
            ((count, width), low, columns(count)),
        ],
        [],
        mixed,
        mixed,
        mixed,
        grad,
        bias,
    )


def layout(heights_row, widths_row):
    pixels = heights_row * widths_row
    ends_at = jnp.cumsum(pixels)
    starts_at = ends_at - pixels
    slot_ids = jnp.arange(SLOTS, dtype=jnp.int32)
    segment = jnp.sum((ends_at[None, :] <= slot_ids[:, None]).astype(jnp.int32), axis=1)
    member = segment[:, None] == jnp.arange(LAT_ROW, dtype=jnp.int32)[None, :]
    start_at = jnp.sum(jnp.where(member, starts_at[None, :], 0), axis=1)
    height_at = jnp.sum(jnp.where(member, heights_row[None, :], 0), axis=1)
    width_at = jnp.sum(jnp.where(member, widths_row[None, :], 0), axis=1)
    place_in = slot_ids - start_at
    safe_width = jnp.maximum(width_at, 1)
    column = place_in % safe_width
    row_index = place_in // safe_width
    return (segment, member, height_at, width_at, row_index, column)


def score_bias(segment, counts_row, key_pad):
    live_query = segment < LAT_ROW
    image_ok = (segment[:, None] == segment[None, :]) & live_query[None, :]
    text_index = jnp.arange(LAT_ROW * TEXT, dtype=jnp.int32)
    text_latent = text_index // TEXT
    text_limit = jnp.sum(
        jnp.where(
            text_latent[:, None] == jnp.arange(LAT_ROW, dtype=jnp.int32)[None, :],
            counts_row[None, :],
            0,
        ),
        axis=1,
    )
    text_ok = (text_latent[:, None] == segment[None, :]) & (text_index % TEXT < text_limit)[:, None]
    no_pad = jnp.zeros((key_pad, segment.shape[0]), bool)
    return jnp.where(jnp.concatenate([image_ok, text_ok, no_pad], axis=0), 0.0, MASKED)


def geometry_table(heights_row, widths_row):
    segment, member, height_at, width_at, row_index, column = layout(heights_row, widths_row)
    live = segment < LAT_ROW
    left = live & (column >= 1)
    right = live & (column + 1 < width_at)
    up = live & (row_index >= 1)
    down = live & (row_index + 1 < height_at)
    sides = [width_at == k * SIDE_UNIT for k in (3, 4, 6)]
    columns = [live, left, right] + [up & s for s in sides] + [down & s for s in sides]
    columns = columns + [jnp.zeros_like(live)] * 7
    return segment, member, jnp.stack(columns, axis=1).astype(jnp.float32)


def local(
    inner,
    outer,
    latents,
    text_embed,
    time_embed,
    heights,
    widths,
    text_counts,
    res_vecs,
    fc1_w,
    ff_vecs,
    fc2_w,
    time_w,
    time_b,
    kv_w,
    attn_w,
    attn_vecs,
    cotangent,
):
    low, full = jnp.bfloat16, jnp.float32
    orders = scatter_orders(outer)
    outer_bits, inner_bits = bit_count(outer), bit_count(inner)
    blocks = inner * outer
    x, cot = latents[0], cotangent[0]
    slots, width = x.shape
    text_width = text_embed.shape[3]
    text_total = LAT_ROW * TEXT
    key_pad = -(slots + text_total) % 128
    mine = lax.axis_index("dp") >> (inner_bits - 1)
    chain = Chain()

    def along(spec, a, b):
        return jnp.einsum(spec, a, b, preferred_element_type=full)

    small_owned = (res_vecs, ff_vecs, time_w, time_b[None], attn_vecs)
    small_sizes = [v.size for v in small_owned]
    small_pad = -sum(small_sizes) % (8 * width)
    small_shard = jnp.concatenate(
        [v.astype(low).reshape(-1) for v in small_owned] + [jnp.zeros((small_pad,), low)]
    )

    def to_all(*shards):
        shard = jnp.concatenate([v.astype(low) for v in shards], axis=0)
        shard = jnp.pad(shard, ((0, -shard.shape[0] % 8), (0, 0)))
        full_rows = lax.all_gather(shard, ("dp", "fsdp"), axis=0, tiled=True)
        return full_rows.reshape(blocks, -1, width)

    rows, kv_rows = fc2_w.shape[0], kv_w.shape[0]
    small_rows = small_shard.size // width
    res_weights = to_all(fc1_w.T, fc2_w, kv_w, small_shard.reshape(-1, width))
    attn_weights = to_all(turn_late(chain, attn_w, res_weights))
    fc1_t, fc2_full = Weight(res_weights, 0, rows), Weight(res_weights, 1, rows)
    attn_t = Weight(attn_weights, 0, rows)
    kv_full = res_weights[:, 2 * rows : 2 * rows + kv_rows].reshape(-1, width)
    small_all = res_weights[:, 2 * rows + kv_rows : 2 * rows + kv_rows + small_rows].reshape(blocks, -1)
    small_full = []
    taken = 0
    for owned, size in zip(small_owned, small_sizes):
        some = small_all[:, taken : taken + size].reshape(blocks, owned.shape[0], owned.shape[1])
        small_full.append(some.transpose(1, 0, 2).reshape(owned.shape[0], -1).astype(full))
        taken += size
    res_all, ff_all, time_w_all, time_b_all, vecs_all = small_full
    taps = jnp.pad(res_all[:10], ((0, 6), (0, 0)))
    vecs = jnp.pad(ff_all, ((0, 5), (0, 0)))

    segment, member_slots, geometry = geometry_table(heights[0], widths[0])
    member = jnp.pad(member_slots[::GROUP].astype(full), ((0, 0), (0, SEATS - LAT_ROW)))
    bias = score_bias(segment, text_counts[0], key_pad)
    live = geometry

    normed_low, normed, entry_scale = entry(chain, x, taps, geometry)
    act, slope, power = hidden_step(chain, normed_low, fc1_t, vecs, member)
    units = act.shape[1]
    norm = jnp.sqrt(power + NORM_EPS)
    norm_mean = jnp.mean(norm, axis=1, keepdims=True) + NORM_EPS
    norms = norm / norm_mean
    time_low = jnp.pad(time_embed[0].astype(low), ((0, SEATS - LAT_ROW), (0, 0)))
    pair = along("lt,tc->lc", time_low, time_w_all.astype(low)) + time_b_all
    response, after_res, after_time, normed_two = branch_step(
        chain, act, norms, vecs, fc2_full, member, live, x, res_all[10:11], pair
    )

    each = width // UNITS
    text = text_embed[0].astype(full).reshape(text_total, text_width)
    silu_text, silu_back = jax.vjp(jax.nn.silu, text)
    silu_low = silu_text.astype(low)
    mapped = (along("tk,kc->tc", silu_low, kv_full) + vecs_all[3]).astype(low)
    source = jnp.concatenate([normed_two, mapped, jnp.zeros((key_pad, width), low)], axis=0)
    grad_proj = (live[:, 0:1] * cot).astype(low)
    mixed_bias = jnp.concatenate([vecs_all[0], jnp.zeros((width,), full), vecs_all[1]])
    mixed, grad_attended = project(
        chain, source, grad_proj, jnp.broadcast_to(mixed_bias, (SEATS, 3 * width)), attn_t
    )
    attended, grad_query, grad_key, grad_value = attention(chain, mixed, grad_attended, bias)

    free = list(reversed(range(outer_bits + inner_bits - 1)))
    early = [b for b in free if b >= outer_bits]

    def pieces_of(both):
        both = both.reshape((2,) * len(free) + (-1, width))
        return [
            Piece(both, early + order, free, start // size, size)
            for order, (start, size) in zip(orders, column_pieces(width, len(orders)))
        ]

    def to_partner(away):
        return swap(away, "dp", inner, inner_bits - 1)

    def halved(terms):
        half = blocks // 2
        come = to_partner(lax.dynamic_slice_in_dim(terms, (1 - mine) * half, half, axis=0))
        kept = lax.dynamic_slice_in_dim(terms, mine * half, half, axis=0)
        some = Piece(kept.reshape((2,) * len(free) + terms.shape[1:]), early + orders[1], free)
        some.come = come.reshape(some.base.shape)
        return some

    def step(*groups):
        for group in groups:
            fold(chain, group, inner, outer)

    def finished(group, *turned):
        while group[0].order:
            step(group)
        return totals_of(chain, group, turned)

    parts = (grad_query, grad_key, grad_value, grad_proj, source, attended)
    come = to_partner(attn_half(chain, *parts, 1 - mine))
    grad_normed_two, grad_text = source_back(
        chain,
        grad_query,
        grad_key,
        grad_value,
        attn_t.by(lambda i: jnp.where(i < 2 * each, i + each, i - 2 * each)),
    )
    grad_mapped = grad_text[:text_total]
    kv_terms = along("tk,tc->kc", silu_low, grad_mapped).astype(low)
    kv_piece = halved(kv_terms.reshape(blocks, -1, width))
    attn_sum = pieces_of(attn_half(chain, *parts, mine, come)) + [kv_piece]
    for _ in early:
        step(attn_sum)
    step(attn_sum)
    grad_res, grad_branch, pair_grad, res_bias_grad = time_back(
        chain, grad_normed_two, after_time, after_res, cot, pair, member, live
    )
    come = to_partner(half_rows(chain, response, grad_branch, 1 - mine))
    grad_response, act_sums, shift_grad = response_back(chain, grad_branch, fc2_full, act, member)
    step(attn_sum)
    fc2_sum = pieces_of(half_rows(chain, response, grad_branch, mine, come))
    step(attn_sum)
    for _ in early:
        step(fc2_sum)
    for _ in range(outer_bits - 3):
        step(attn_sum)
    step(fc2_sum)
    gain_grad = jnp.sum(act_sums * norms, axis=0, keepdims=True)
    norms_grad = vecs[1:2] * act_sums
    norm_grad = norms_grad / norm_mean - jnp.sum(norms_grad * norm, axis=1, keepdims=True) / (
        units * norm_mean * norm_mean
    )
    hidden_low, hidden_bias_grad, grad_normed = hidden_back(
        chain, grad_response, act, slope, vecs, norms, norm_grad / norm, member, fc1_t
    )
    attn_grad, kv_grad = finished(attn_sum, True, False)
    step(fc2_sum)
    come = to_partner(half_rows(chain, hidden_low, normed_low, 1 - mine))
    latents_grad, taps_grad = entry_back(
        chain, grad_normed, normed, entry_scale, x, grad_res, taps, geometry, res_bias_grad
    )
    step(fc2_sum)
    time_grad = jnp.einsum("lt,lc->tc", time_low.astype(full), pair_grad, precision=HIGHEST)
    small_terms = (
        taps_grad[: res_vecs.shape[0]],
        jnp.concatenate([hidden_bias_grad[:1], gain_grad, shift_grad[:1]], axis=0),
        time_grad,
        jnp.sum(pair_grad, axis=0, keepdims=True),
        jnp.stack(
            [
                jnp.sum(grad_query.astype(full), axis=0),
                jnp.sum(grad_value.astype(full), axis=0),
                jnp.sum(grad_proj.astype(full), axis=0),
                jnp.sum(grad_mapped.astype(full), axis=0),
            ]
        ),
    )
    small_blocks = jnp.concatenate(
        [g.reshape(g.shape[0], blocks, -1).transpose(1, 0, 2).reshape(blocks, -1) for g in small_terms]
        + [jnp.zeros((blocks, -sum(small_sizes) % 1024), full)],
        axis=1,
    ).reshape(blocks, -1, 128)
    small_piece = halved(small_blocks)
    fc1_sum = pieces_of(half_rows(chain, hidden_low, normed_low, mine, come)) + [small_piece]
    for _ in early:
        step(fc1_sum)
    for _ in range(outer_bits - 3):
        step(fc2_sum)
    step(fc1_sum)
    output = output_step(
        chain,
        attended,
        after_time,
        live,
        jnp.broadcast_to(vecs_all[2], (SEATS, width)),
        attn_t.by(lambda i: 3 * each + i),
    )
    (fc2_grad,) = finished(fc2_sum, False)
    step(fc1_sum)
    step(fc1_sum)
    fc1_grad, small_total = finished(fc1_sum, True, False)
    small_total = small_total.reshape(-1)
    text_grad = silu_back(along("tc,kc->tk", grad_mapped, kv_full))[0]

    small_grads = []
    taken = 0
    for owned, size in zip(small_owned, small_sizes):
        small_grads.append(small_total[taken : taken + size].reshape(owned.shape))
        taken += size
    return (
        output[None],
        latents_grad[None],
        text_grad.reshape(text_embed.shape),
        small_grads[0],
        fc1_grad,
        small_grads[1],
        fc2_grad,
        small_grads[2],
        small_grads[3][0],
        kv_grad,
        attn_grad,
        small_grads[4],
    )


def solution(mesh):
    return jax.shard_map(
        functools.partial(local, mesh.shape["dp"], mesh.shape["fsdp"]),
        mesh=mesh,
        in_specs=(
            P(("dp", "fsdp"), None, None),
            P(("dp", "fsdp"), None, None, None),
            P(("dp", "fsdp"), None, None),
            P(("dp", "fsdp"), None),
            P(("dp", "fsdp"), None),
            P(("dp", "fsdp"), None),
            P(None, ("dp", "fsdp")),
            P(None, ("dp", "fsdp")),
            P(None, ("dp", "fsdp")),
            P(("dp", "fsdp"), None),
            P(None, ("dp", "fsdp")),
            P(("dp", "fsdp")),
            P(("dp", "fsdp"), None),
            P(None, ("dp", "fsdp")),
            P(None, ("dp", "fsdp")),
            P(("dp", "fsdp"), None, None),
        ),
        out_specs=(
            P(("dp", "fsdp"), None, None),
            P(("dp", "fsdp"), None, None),
            P(("dp", "fsdp"), None, None, None),
            P(None, ("dp", "fsdp")),
            P(None, ("dp", "fsdp")),
            P(None, ("dp", "fsdp")),
            P(("dp", "fsdp"), None),
            P(None, ("dp", "fsdp")),
            P(("dp", "fsdp")),
            P(("dp", "fsdp"), None),
            P(None, ("dp", "fsdp")),
            P(None, ("dp", "fsdp")),
        ),
        check_vma=False,
    )
```

```python
import functools

import jax
import jax.numpy as jnp
from jax import lax
from jax.experimental import pallas as pl
from jax.experimental.pallas import tpu as pltpu
from jax.sharding import PartitionSpec as P

HEADS = 24
TEXT = 77
SIDE_UNIT = 4
SLOTS = 576
LAT_ROW = 4
GROUP = 16
SEATS = 8

HEAD_SCALE = 64**-0.5
LANES = 128
UNITS = 768
HIGHEST = lax.Precision.HIGHEST
NORM_EPS = 1e-06
MASKED = -1000000000.0


def bit_count(size):
    return size.bit_length() - 1


def swap(values, axis_name, size, bit):
    return lax.ppermute(values, axis_name, [(i, i ^ (1 << bit)) for i in range(size)])


def scatter_orders(size):
    bits = list(range(bit_count(size) - 1))
    return [bits[turn:] + bits[:turn] + [len(bits)] for turn in range(3)]


def column_pieces(width, count):
    if count == 1:
        return [(0, width)]
    unit = width // 12
    return [(0, 5 * unit), (5 * unit, 5 * unit), (10 * unit, 2 * unit)]


class Chain:
    def __init__(self):
        self.token = None

    def call(self, kernel, grid, ins, outs, scratch, *operands, scalars=(), after=()):
        earlier = (() if self.token is None else (self.token,)) + tuple(after)
        held, count = len(scalars), len(operands)

        def body(*refs):
            before, rest = refs[: held + count], refs[held + count + len(earlier) :]
            rest[len(outs)][...] = jnp.zeros_like(rest[len(outs)])
            kernel(*before, *rest[: len(outs)], *rest[len(outs) + 1 :])

        token_spec = pl.BlockSpec((8, 128), lambda *_: (0, 0))
        done = pl.pallas_call(
            body,
            grid_spec=pltpu.PrefetchScalarGridSpec(
                num_scalar_prefetch=held,
                grid=grid,
                in_specs=list(ins) + [pl.BlockSpec(memory_space=pl.ANY)] * len(earlier),
                out_specs=[spec for _, _, spec in outs] + [token_spec],
                scratch_shapes=list(scratch),
            ),
            out_shape=[jax.ShapeDtypeStruct(shape, dtype) for shape, dtype, _ in outs]
            + [jax.ShapeDtypeStruct((8, 128), jnp.float32)],
            compiler_params=pltpu.CompilerParams(vmem_limit_bytes=56 << 20),
        )(*scalars, *operands, *earlier)
        self.token = done[-1]
        return done[:-1]


def whole_array(shape):
    return pl.BlockSpec(shape, lambda *_: (0,) * len(shape))


class Weight:
    def __init__(self, gathered, place, rows, block=lambda step, *_: step):
        if rows % GROUP:
            some = gathered[:, place * rows : (place + 1) * rows]
            gathered, place, rows = some.reshape(-1, UNITS, some.shape[2]), 0, UNITS
        self.gathered, self.place, self.rows, self.block = gathered, place, rows, block
        self.total = gathered.shape[0] * rows
        self.width = gathered.shape[2]

    def by(self, block):
        return Weight(self.gathered, self.place, self.rows, block)

    def spec(self):
        return pl.BlockSpec(
            (UNITS // self.rows, self.rows, self.width), lambda *at: (self.block(*at), self.place, 0)
        )


def rows_of(ref):
    return ref[...].reshape(UNITS, ref.shape[2])


class Piece:
    def __init__(self, base, order, bits, cut=0, width=None):
        self.base, self.order, self.bits, self.cut = base, list(order), list(bits), cut
        self.free, self.fixed, self.come, self.come_cut = list(bits), [], None, 0
        self.width = base.shape[-1] if width is None else width


def fold(chain, pieces, inner, outer, after=(), hold=False):
    if len(pieces[0].free) == 1:
        return fold_last(chain, pieces, inner, outer, after)
    me = lax.axis_index("dp") * outer + lax.axis_index("fsdp")
    left = len(pieces[0].free) - 1
    inside = min(max(left - 1, 0), 2)
    ins, outs, operands, plans, bits = [], [], [], [], []
    for piece in pieces:
        lazy = piece.come is None
        bit = piece.order.pop(0)
        bits.append(bit)
        rest = [b for b in piece.free if b != bit]
        near = rest[len(rest) - inside :]
        far = rest[: len(rest) - inside]

        def spec(axes, cut, width, rows, bit=bit, near=near, far=far, fixed=tuple(piece.fixed), lazy=lazy):
            def where(k, me_ref):
                place = []
                for b in axes:
                    if b in fixed:
                        place.append((me_ref[0] >> b) & 1)
                    elif b == bit:
                        place.append(1 - ((me_ref[0] >> b) & 1) if lazy else 0)
                    elif b in near:
                        place.append(0)
                    else:
                        place.append((k >> (len(far) - 1 - far.index(b))) & 1)
                return tuple(place) + (0, cut)

            shape = tuple(
                2 if (b in near and b not in fixed) or (b == bit and not lazy) else None for b in axes
            )
            return pl.BlockSpec(shape + (rows, width), where)

        rows = piece.base.shape[-2]
        ins.append(spec(piece.bits, piece.cut, piece.width, rows))
        operands.append(piece.base)
        if not lazy:
            ins.append(spec(piece.free, piece.come_cut, piece.width, rows))
            operands.append(piece.come)
        shape = (2,) * len(rest) + (rows, piece.width)
        outs += [(shape, piece.base.dtype, spec(rest, 0, piece.width, rows))] * (1 if lazy else 2)
        plans.append((lazy, bit, sum(1 for b in near if b > bit)))
        piece.free, piece.come_cut = rest, 0
    done = list(
        chain.call(
            functools.partial(fold_kernel, plans),
            (1 << (left - inside),),
            ins,
            outs,
            [],
            *operands,
            scalars=(me.astype(jnp.int32)[None],),
            after=after,
        )
    )
    for piece, (lazy, bit, _) in zip(pieces, plans):
        away = done.pop(0)
        if lazy:
            piece.fixed.append(bit)
        else:
            piece.base, piece.cut, piece.fixed, piece.bits = done.pop(0), 0, [], list(piece.free)
        piece.away = (away, bit)
    if not hold:
        send(chain, pieces, inner, outer, False)


def send(chain, pieces, inner, outer, wait=True):
    low_bits = bit_count(outer)
    for piece in pieces:
        away, bit = piece.away
        away = late(chain, away) if wait else away
        if bit < low_bits:
            piece.come = swap(away, "fsdp", outer, bit)
        else:
            piece.come = swap(away, "dp", inner, bit - low_bits)


def fold_kernel(plans, me_ref, *refs):
    count = sum(1 if lazy else 2 for lazy, _, _ in plans)
    ins, outs = list(refs[:count]), list(refs[count:])
    for lazy, bit, before in plans:
        if lazy:
            outs.pop(0)[...] = ins.pop(0)[...]
            continue
        base, come = ins.pop(0), ins.pop(0)
        own = (me_ref[0] >> bit) & 1
        for out, side in ((outs.pop(0), 1 - own), (outs.pop(0), own)):
            at = (slice(None),) * before + (side,)
            out[...] = (base[at].astype(jnp.float32) + come[at].astype(jnp.float32)).astype(out.dtype)


def round_kernel(values_ref, late_ref, out_ref):
    out_ref[...] = values_ref[...].astype(jnp.bfloat16)


def round_late(chain, values, late):
    shape = values.shape
    return chain.call(
        round_kernel,
        (1,),
        [whole_array(values.shape), pl.BlockSpec(memory_space=pl.ANY)],
        [(shape, jnp.bfloat16, whole_array(shape))],
        [],
        values,
        late,
    )[0]


def copy_kernel(values_ref, out_ref):
    out_ref[...] = values_ref[...]


def copy_late(chain, values):
    spec = whole_array(values.shape)
    return chain.call(copy_kernel, (1,), [spec], [(values.shape, values.dtype, spec)], [], values)[0]


def keep_kernel(values_ref, token_ref, out_ref):
    pass


def late(chain, values):
    some = pl.BlockSpec(memory_space=pl.ANY)
    return pl.pallas_call(
        keep_kernel,
        out_shape=jax.ShapeDtypeStruct(values.shape, values.dtype),
        in_specs=[some, some],
        out_specs=some,
        input_output_aliases={0: 0},
    )(values, chain.token)


def last_kernel(cuts, bit, me_ref, *refs):
    own = (me_ref[0] >> bit) & 1
    ins, outs = refs[: 2 * len(cuts)], refs[2 * len(cuts) :]
    for n, (group, cut) in enumerate(cuts):
        both = ins[2 * n][...].astype(jnp.float32) + ins[2 * n + 1][...].astype(jnp.float32)
        both = both.astype(outs[2 * group].dtype)
        outs[2 * group][:, :, cut] = jnp.where(own == 0, both[1:2], both[0:1])
        outs[2 * group + 1][:, :, cut] = jnp.where(own == 0, both[0:1], both[1:2])


def fold_last(chain, pieces, inner, outer, after):
    bit = pieces[0].order.pop(0)
    me = lax.axis_index("dp") * outer + lax.axis_index("fsdp")
    operands, cuts, shapes = [], [], []
    for piece in pieces:
        operands += [piece.base, piece.come]
        rows = piece.base.shape[1]
        if not shapes or shapes[-1][1] != rows:
            shapes.append([1, rows, 0])
        start = shapes[-1][2]
        cuts.append((len(shapes) - 1, slice(start, start + piece.width)))
        shapes[-1][2] = start + piece.width
    dtypes = {piece.base.shape[1]: piece.base.dtype for piece in pieces}
    done = chain.call(
        functools.partial(last_kernel, cuts, bit),
        (1,),
        [whole_array(v.shape) for v in operands],
        [(tuple(shape), dtypes[shape[1]], whole_array(tuple(shape))) for shape in shapes for _ in range(2)],
        [],
        *operands,
        scalars=(me.astype(jnp.int32)[None],),
        after=after,
    )
    pieces[:] = [Piece(kept, [], []) for kept in done[1::2]]
    for piece, away in zip(pieces, done[::2]):
        piece.come = swap(away, "fsdp", outer, bit)


def total_kernel(count, *refs):
    for n in range(count):
        refs[2 * count + n][...] = (refs[2 * n][...].astype(jnp.float32) + refs[2 * n + 1][...].astype(jnp.float32))[0]


def totals_of(chain, pieces):
    operands = [v for piece in pieces for v in (piece.base, piece.come)]
    shapes = [piece.base.shape[1:] for piece in pieces]
    return chain.call(
        functools.partial(total_kernel, len(pieces)),
        (1,),
        [whole_array(v.shape) for v in operands],
        [(shape, jnp.float32, whole_array(shape)) for shape in shapes],
        [],
        *operands,
    )


def product(a, b, da, db):
    return lax.dot_general(a, b, (((da,), (db,)), ((), ())), preferred_element_type=jnp.float32)


def by_group(values):
    return values.reshape(values.shape[0] // GROUP, GROUP, values.shape[1])


def spread(seats, member):
    total = member[:, 0:1] * seats[0:1, :]
    for place in range(1, LAT_ROW):
        total = total + member[:, place : place + 1] * seats[place : place + 1, :]
    return total[:, None, :]


def gathered(values, member):
    by = jnp.sum(by_group(values), axis=1)
    rows = [jnp.sum(by * member[:, place : place + 1], axis=0, keepdims=True) for place in range(LAT_ROW)]
    return jnp.concatenate(rows + [jnp.zeros((SEATS - LAT_ROW, values.shape[1]), jnp.float32)], axis=0)


def neighbours(x, geometry):
    slots = x.shape[0]
    above = below = None
    for index, side in enumerate((3 * SIDE_UNIT, 4 * SIDE_UNIT, 6 * SIDE_UNIT)):
        up = geometry[3 + index] * pltpu.roll(x, side, 0)
        down = geometry[6 + index] * pltpu.roll(x, slots - side, 0)
        above = up if above is None else above + up
        below = down if below is None else below + down
    return above, geometry[0] * x, below


def geometry_columns(geometry_ref):
    return [geometry_ref[:, k : k + 1] for k in range(9)]


def entry_kernel(x_ref, taps_ref, geometry_ref, low_ref, normed_ref, scale_ref, conv_ref):
    slots, width = x_ref.shape
    geometry = geometry_columns(geometry_ref)
    total = jnp.zeros((slots, LANES), jnp.float32)
    for start in range(0, width, LANES):
        cut = slice(start, start + LANES)
        rows = neighbours(x_ref[:, cut], geometry)
        left, mid, right = (
            sum(taps_ref[3 * a + b : 3 * a + b + 1, cut] * rows[a] for a in range(3)) for b in range(3)
        )
        conv = (
            taps_ref[9:10, cut]
            + mid
            + geometry[1] * pltpu.roll(left, 1, 0)
            + geometry[2] * pltpu.roll(right, slots - 1, 0)
        )
        conv_ref[:, cut] = conv
        total = total + conv
    mean = jnp.sum(total, axis=1, keepdims=True) * (1.0 / width)
    square = jnp.zeros((slots, LANES), jnp.float32)
    for start in range(0, width, LANES):
        center = conv_ref[:, start : start + LANES] - mean
        square = square + center * center
    scale = lax.rsqrt(jnp.sum(square, axis=1, keepdims=True) * (1.0 / width) + NORM_EPS)
    scale_ref[...] = jnp.broadcast_to(scale, scale_ref.shape)
    for start in range(0, width, LANES):
        cut = slice(start, start + LANES)
        normed = (conv_ref[:, cut] - mean) * scale
        normed_ref[:, cut] = normed
        low_ref[:, cut] = normed.astype(jnp.bfloat16)


def entry(chain, x, taps, geometry):
    slots, width = x.shape
    return chain.call(
        entry_kernel,
        (1,),
        [whole_array(v.shape) for v in (x, taps, geometry)],
        [
            ((slots, width), jnp.bfloat16, whole_array((slots, width))),
            ((slots, width), jnp.float32, whole_array((slots, width))),
            ((slots, LANES), jnp.float32, whole_array((slots, LANES))),
        ],
        [pltpu.VMEM((slots, width), jnp.float32)],
        x,
        taps,
        geometry,
    )


def entry_back_kernel(q_ref, normed_ref, scale_ref, x_ref, res_ref, taps_ref, geometry_ref, bias_grad_ref, grad_ref, taps_grad_ref):
    slots, width = x_ref.shape
    geometry = geometry_columns(geometry_ref)
    scale = scale_ref[:, 0:1]
    plain = jnp.zeros((slots, LANES), jnp.float32)
    along = jnp.zeros((slots, LANES), jnp.float32)
    for start in range(0, width, LANES):
        cut = slice(start, start + LANES)
        q = q_ref[:, cut]
        plain = plain + q
        along = along + q * normed_ref[:, cut]
    plain = jnp.sum(plain, axis=1, keepdims=True) * (1.0 / width)
    along = jnp.sum(along, axis=1, keepdims=True) * (1.0 / width)
    for start in range(0, width, LANES):
        cut = slice(start, start + LANES)
        grad = (q_ref[:, cut] - plain - normed_ref[:, cut] * along) * scale
        sides = (
            pltpu.roll(grad * geometry[1], slots - 1, 0),
            grad,
            pltpu.roll(grad * geometry[2], 1, 0),
        )
        rows = neighbours(x_ref[:, cut], geometry)
        sums = [
            jnp.sum(rows[a] * sides[b], axis=0, keepdims=True) for a in range(3) for b in range(3)
        ]
        sums.append(jnp.sum(grad, axis=0, keepdims=True))
        sums.append(bias_grad_ref[0:1, cut])
        sums.append(jnp.zeros((5, LANES), jnp.float32))
        taps_grad_ref[:, cut] = jnp.concatenate(sums, axis=0)
        above, mid, below = (
            sum(taps_ref[3 * a + b : 3 * a + b + 1, cut] * sides[b] for b in range(3)) for a in range(3)
        )
        back = res_ref[:, cut] + geometry[0] * mid
        for index, side in enumerate((3 * SIDE_UNIT, 4 * SIDE_UNIT, 6 * SIDE_UNIT)):
            back = back + pltpu.roll(geometry[3 + index] * above, slots - side, 0)
            back = back + pltpu.roll(geometry[6 + index] * below, side, 0)
        grad_ref[:, cut] = back


def entry_back(chain, q, normed, scale, x, res, taps, geometry, bias_grad):
    slots, width = x.shape
    operands = (q, normed, scale, x, res, taps, geometry, bias_grad)
    return chain.call(
        entry_back_kernel,
        (1,),
        [whole_array(v.shape) for v in operands],
        [
            ((slots, width), jnp.float32, whole_array((slots, width))),
            ((16, width), jnp.float32, whole_array((16, width))),
        ],
        [],
        *operands,
    )


def hidden_kernel(normed_ref, vecs_ref, member_ref, *refs):
    weight_ref, act_ref, slope_ref, power_ref = refs
    hidden = product(normed_ref[...], rows_of(weight_ref), 1, 1) + vecs_ref[0:1, :]
    below = 0.5 + 0.5 * lax.erf(hidden * (0.5**0.5))
    act = hidden * below
    act_ref[...] = act
    slope_ref[...] = below + hidden * (jnp.exp(-0.5 * hidden * hidden) * (0.5 / jnp.pi) ** 0.5)
    power_ref[...] = gathered(act * act, member_ref[...])


def unit_columns(rows):
    return pl.BlockSpec((rows, UNITS), lambda i, *_: (0, i))


def hidden_step(chain, normed, weight, vecs, member):
    slots, width = normed.shape
    units = weight.total
    return chain.call(
        hidden_kernel,
        (units // UNITS,),
        [whole_array((slots, width)), unit_columns(vecs.shape[0]), whole_array(member.shape)] + [weight.spec()],
        [
            ((slots, units), jnp.float32, unit_columns(slots)),
            ((slots, units), jnp.float32, unit_columns(slots)),
            ((SEATS, units), jnp.float32, unit_columns(SEATS)),
        ],
        [],
        normed,
        vecs,
        member,
        weight.gathered,
    )


def norm_rows(values):
    center = values - jnp.mean(values, axis=-1, keepdims=True)
    scale = lax.rsqrt(jnp.mean(center * center, axis=-1, keepdims=True) + NORM_EPS)
    return center * scale, scale


def branch_kernel(act_ref, norms_ref, vecs_ref, member_ref, live_ref, x_ref, bias_ref, pair_ref, *refs):
    weight_ref, response_ref, res_ref, time_ref, low_ref, total_ref = refs
    step = pl.program_id(0)
    member = member_ref[...]
    act = by_group(act_ref[...])
    response = act * (1.0 + vecs_ref[1:2, :][None] * spread(norms_ref[...], member)) + vecs_ref[2:3, :][None]
    response = response.reshape(act_ref.shape).astype(jnp.bfloat16)
    response_ref[...] = response
    part = product(response, rows_of(weight_ref), 1, 0)

    @pl.when(step == 0)
    def _():
        total_ref[...] = part

    @pl.when(step > 0)
    def _():
        total_ref[...] += part

    @pl.when(step == pl.num_programs(0) - 1)
    def _():
        width = x_ref.shape[1]
        after_res = x_ref[...] + live_ref[:, 0:1] * (total_ref[...] + bias_ref[...])
        res_ref[...] = after_res
        per = spread(pair_ref[...], member)
        after_time = by_group(after_res) * (1.0 + per[:, :, :width]) + per[:, :, width:]
        after_time = after_time.reshape(after_res.shape)
        time_ref[...] = after_time
        low_ref[...] = norm_rows(after_time)[0].astype(jnp.bfloat16)


def branch_step(chain, act, norms, vecs, weight, member, live, x, bias, pair):
    slots, units = act.shape
    width = x.shape[1]
    return chain.call(
        branch_kernel,
        (units // UNITS,),
        [
            unit_columns(slots),
            unit_columns(SEATS),
            unit_columns(vecs.shape[0]),
            whole_array(member.shape),
            whole_array(live.shape),
            whole_array(x.shape),
            whole_array(bias.shape),
            whole_array(pair.shape),
        ]
        + [weight.spec()],
        [
            ((slots, units), jnp.bfloat16, unit_columns(slots)),
            ((slots, width), jnp.float32, whole_array((slots, width))),
            ((slots, width), jnp.float32, whole_array((slots, width))),
            ((slots, width), jnp.bfloat16, whole_array((slots, width))),
        ],
        [pltpu.VMEM((slots, width), jnp.float32)],
        act,
        norms,
        vecs,
        member,
        live,
        x,
        bias,
        pair,
        weight.gathered,
    )


def time_back_kernel(q_ref, time_ref, res_ref, cot_ref, pair_ref, member_ref, live_ref, grad_ref, low_ref, pair_grad_ref, bias_grad_ref):
    width = q_ref.shape[1]
    member = member_ref[...]
    normed, scale = norm_rows(time_ref[...])
    q = q_ref[...]
    plain = jnp.mean(q, axis=-1, keepdims=True)
    along = jnp.mean(q * normed, axis=-1, keepdims=True)
    grad_time = cot_ref[...] + (q - plain - normed * along) * scale
    pair_grad_ref[:, :width] = gathered(grad_time * res_ref[...], member)
    pair_grad_ref[:, width:] = gathered(grad_time, member)
    per = spread(pair_ref[:, :width], member)
    grad_res = (by_group(grad_time) * (1.0 + per)).reshape(q.shape)
    grad_ref[...] = grad_res
    low = (live_ref[:, 0:1] * grad_res).astype(jnp.bfloat16)
    low_ref[...] = low
    bias_grad_ref[...] = jnp.broadcast_to(jnp.sum(low.astype(jnp.float32), axis=0, keepdims=True), bias_grad_ref.shape)


def time_back(chain, q, after_time, after_res, cot, pair, member, live):
    slots, width = q.shape
    operands = (q, after_time, after_res, cot, pair, member, live)
    return chain.call(
        time_back_kernel,
        (1,),
        [whole_array(v.shape) for v in operands],
        [
            ((slots, width), jnp.float32, whole_array((slots, width))),
            ((slots, width), jnp.bfloat16, whole_array((slots, width))),
            ((SEATS, 2 * width), jnp.float32, whole_array((SEATS, 2 * width))),
            ((SEATS, width), jnp.float32, whole_array((SEATS, width))),
        ],
        [],
        *operands,
    )


def partner_first(half):
    def block(step, mine_ref):
        return jnp.where(step < half, 1 - mine_ref[0], mine_ref[0]) * half + step % half

    return block


def half_specs(units, width):
    half = units // UNITS // 2
    shape = (units // 2, width)
    return [
        (shape, jnp.bfloat16, pl.BlockSpec((UNITS, width), lambda i, _: (jnp.minimum(i, half - 1), 0))),
        (shape, jnp.bfloat16, pl.BlockSpec((UNITS, width), lambda i, _: (jnp.maximum(i - half, 0), 0))),
    ]


def store_half(away_ref, kept_ref, left, right):
    rows = product(left, right, 0, 0).astype(jnp.bfloat16)
    half = pl.num_programs(0) // 2

    @pl.when(pl.program_id(0) < half)
    def _():
        away_ref[...] = rows

    @pl.when(pl.program_id(0) >= half)
    def _():
        kept_ref[...] = rows


def response_back_kernel(mine_ref, branch_ref, act_ref, response_ref, member_ref, weight_ref, grad_ref, sums_ref, shift_ref, away_ref, kept_ref):
    grad = product(branch_ref[...], rows_of(weight_ref), 1, 1)
    grad_ref[...] = grad
    sums_ref[...] = gathered(grad * act_ref[...], member_ref[...])
    shift_ref[...] = jnp.broadcast_to(jnp.sum(grad, axis=0, keepdims=True), shift_ref.shape)
    store_half(away_ref, kept_ref, response_ref[...], branch_ref[...])


def response_back(chain, branch, weight, act, response, member, mine):
    slots, width = branch.shape
    units = weight.total
    block = partner_first(units // UNITS // 2)

    def columns(rows):
        return pl.BlockSpec((rows, UNITS), lambda *at: (0, block(*at)))

    return chain.call(
        response_back_kernel,
        (units // UNITS,),
        [whole_array(branch.shape), columns(slots), columns(slots), whole_array(member.shape)]
        + [weight.by(block).spec()],
        [
            ((slots, units), jnp.float32, columns(slots)),
            ((SEATS, units), jnp.float32, columns(SEATS)),
            ((SEATS, units), jnp.float32, columns(SEATS)),
        ]
        + half_specs(units, width),
        [],
        branch,
        act,
        response,
        member,
        weight.gathered,
        scalars=(mine,),
    )


def hidden_back_kernel(added, side_ref, grad_ref, act_ref, slope_ref, vecs_ref, norms_ref, ratio_ref, member_ref, normed_ref, weight_ref, *refs):
    bias_ref, normed_grad_ref, rows_ref, total_ref = refs[-4:]
    step = pl.program_id(0)
    member = member_ref[...]
    grad = by_group(grad_ref[...]) * (1.0 + vecs_ref[1:2, :][None] * spread(norms_ref[...], member))
    grad = grad + by_group(act_ref[...]) * spread(ratio_ref[...], member)
    low = (grad.reshape(act_ref.shape) * slope_ref[...]).astype(jnp.bfloat16)
    bias_ref[...] = jnp.broadcast_to(jnp.sum(low.astype(jnp.float32), axis=0, keepdims=True), bias_ref.shape)
    rows_ref[...] = product(low, normed_ref[...], 0, 0).astype(jnp.bfloat16)
    part = product(low, rows_of(weight_ref), 1, 0)

    @pl.when(step == 0)
    def _():
        total_ref[...] = part + refs[0][...] if added else part

    @pl.when(step > 0)
    def _():
        total_ref[...] += part

    @pl.when(step == pl.num_programs(0) - 1)
    def _():
        normed_grad_ref[...] = total_ref[...]


def hidden_back(chain, grad, act, slope, vecs, norms, ratio, member, normed, weight, side, before=None):
    slots, units = act.shape
    width = weight.width
    half = units // UNITS // 2

    def block(step, side_ref):
        return side_ref[0] * half + step

    def columns(rows):
        return pl.BlockSpec((rows, UNITS), lambda *at: (0, block(*at)))

    before = () if before is None else (before,)
    return chain.call(
        functools.partial(hidden_back_kernel, len(before) > 0),
        (half,),
        [columns(slots)] * 3
        + [columns(vecs.shape[0]), columns(SEATS), columns(SEATS)]
        + [whole_array(member.shape), whole_array(normed.shape), weight.by(block).spec()]
        + [whole_array(v.shape) for v in before],
        [
            ((SEATS, units // 2), jnp.float32, unit_columns(SEATS)),
            ((slots, width), jnp.float32, whole_array((slots, width))),
            ((units // 2, width), jnp.bfloat16, pl.BlockSpec((UNITS, width), lambda i, *_: (i, 0))),
        ],
        [pltpu.VMEM((slots, width), jnp.float32)],
        grad,
        act,
        slope,
        vecs,
        norms,
        ratio,
        member,
        normed,
        weight.gathered,
        *before,
        scalars=(side,),
    )


def project_kernel(source_ref, grad_ref, bias_ref, *refs):
    weight_ref, out_ref, att_grad_ref, total_ref = refs
    step = pl.program_id(0)
    each = pl.num_programs(0) // 4
    weight = rows_of(weight_ref)

    @pl.when(step < 3 * each)
    def _():
        out = (product(source_ref[...], weight, 1, 1) + bias_ref[0:1, :]).astype(jnp.bfloat16)
        scale = jnp.where(step < each, HEAD_SCALE, 1.0).astype(jnp.bfloat16)
        out_ref[...] = out * scale

    @pl.when(step >= 3 * each)
    def _():
        part = product(grad_ref[...], weight, 1, 0)

        @pl.when(step == 3 * each)
        def _():
            total_ref[...] = part

        @pl.when(step > 3 * each)
        def _():
            total_ref[...] += part

        @pl.when(step == 4 * each - 1)
        def _():
            att_grad_ref[...] = total_ref[...].astype(jnp.bfloat16)


def project(chain, source, grad, bias, weight):
    count, width = source.shape
    slots = grad.shape[0]
    each = width // UNITS
    return chain.call(
        project_kernel,
        (4 * each,),
        [
            whole_array(source.shape),
            pl.BlockSpec((slots, UNITS), lambda i, *_: (0, jnp.maximum(i - 3 * each, 0))),
            pl.BlockSpec((SEATS, UNITS), lambda i, *_: (0, jnp.minimum(i, 3 * each - 1))),
        ]
        + [weight.spec()],
        [
            (
                (count, 3 * width),
                jnp.bfloat16,
                pl.BlockSpec((count, UNITS), lambda i, *_: (0, jnp.minimum(i, 3 * each - 1))),
            ),
            ((slots, width), jnp.bfloat16, whole_array((slots, width))),
        ],
        [pltpu.VMEM((slots, width), jnp.float32)],
        source,
        grad,
        bias,
        weight.gathered,
    )


def source_back_kernel(query_ref, key_ref, value_ref, *refs):
    weight_ref, slot_ref, text_ref, total_ref = refs
    step = pl.program_id(0)
    each = pl.num_programs(0) // 3
    slots = slot_ref.shape[0]
    weight = rows_of(weight_ref)

    @pl.when(step == 0)
    def _():
        total_ref[...] = product(key_ref[...], weight, 1, 0)

    @pl.when((step > 0) & (step < each))
    def _():
        total_ref[...] += product(key_ref[...], weight, 1, 0)

    @pl.when((step >= each) & (step < 2 * each))
    def _():
        total_ref[...] += product(value_ref[...], weight, 1, 0)

    @pl.when(step >= 2 * each)
    def _():
        total_ref[:slots, :] += product(query_ref[...], weight, 1, 0)

    @pl.when(step == 3 * each - 1)
    def _():
        slot_ref[...] = total_ref[:slots, :]
        text_ref[...] = total_ref[slots:, :].astype(jnp.bfloat16)


def source_back(chain, query, keys, values, weight):
    slots, width = query.shape
    count = keys.shape[0]
    each = width // UNITS

    def columns(rows, turn):
        return pl.BlockSpec((rows, UNITS), lambda i, *_: (0, jnp.clip(i - turn * each, 0, each - 1)))

    return chain.call(
        source_back_kernel,
        (3 * each,),
        [columns(slots, 2), columns(count, 0), columns(count, 1)]
        + [weight.spec()],
        [
            ((slots, width), jnp.float32, whole_array((slots, width))),
            ((count - slots, width), jnp.bfloat16, whole_array((count - slots, width))),
        ],
        [pltpu.VMEM((count, width), jnp.float32)],
        query,
        keys,
        values,
        weight.gathered,
    )


def output_kernel(attended_ref, time_ref, live_ref, bias_ref, weight_ref, out_ref):
    out = product(attended_ref[...], rows_of(weight_ref), 1, 1) + bias_ref[0:1, :]
    out_ref[...] = time_ref[...] + live_ref[:, 0:1] * out


def output_step(chain, attended, after_time, live, bias, weight):
    slots, width = attended.shape
    each = width // UNITS
    columns = pl.BlockSpec((slots, UNITS), lambda i, *_: (0, i))
    return chain.call(
        output_kernel,
        (each,),
        [
            whole_array(attended.shape),
            columns,
            whole_array(live.shape),
            pl.BlockSpec((SEATS, UNITS), lambda i, *_: (0, i)),
        ]
        + [weight.spec()],
        [((slots, width), jnp.float32, columns)],
        [],
        attended,
        after_time,
        live,
        bias,
        weight.gathered,
    )[0]


def attn_half_kernel(added, half_ref, query_ref, key_ref, value_ref, proj_ref, source_ref, attended_ref, *refs):
    out_ref = refs[-1]
    role = 2 * half_ref[0] + pl.program_id(0) // (pl.num_programs(0) // 2)
    slots = query_ref.shape[0]

    def store(total):
        if added:
            total = total + refs[0][...].astype(jnp.float32)
        out_ref[...] = total.astype(jnp.bfloat16)

    @pl.when(role == 0)
    def _():
        store(product(query_ref[...], source_ref[:slots, :], 0, 0))

    @pl.when(role == 1)
    def _():
        store(product(key_ref[...], source_ref[...], 0, 0))

    @pl.when(role == 2)
    def _():
        store(product(value_ref[...], source_ref[...], 0, 0))

    @pl.when(role == 3)
    def _():
        store(product(proj_ref[...], attended_ref[...], 0, 0))


def attn_half(chain, query, keys, values, proj, source, attended, half, come=None):
    width = source.shape[1]
    each = width // UNITS
    rows = pl.BlockSpec((UNITS, width), lambda i, *_: (i, 0))

    def columns(values, role):
        def where(i, half_ref):
            return (0, jnp.where(2 * half_ref[0] + i // each == role, i % each, 0))

        return pl.BlockSpec((values.shape[0], UNITS), where)

    return chain.call(
        functools.partial(attn_half_kernel, come is not None),
        (2 * each,),
        [columns(v, n) for n, v in enumerate((query, keys, values, proj))]
        + [whole_array(source.shape), whole_array(attended.shape)]
        + ([] if come is None else [rows]),
        [((2 * width, width), jnp.bfloat16, rows)],
        [],
        query,
        keys,
        values,
        proj,
        source,
        attended,
        *(() if come is None else (come,)),
        scalars=(half.astype(jnp.int32)[None],),
    )[0]


def attention_kernel(q_ref, k_ref, v_ref, g_ref, bias_ref, att_ref, dq_ref, dk_ref, dv_ref):
    width = q_ref.shape[1]
    half = width // 2
    low = jnp.bfloat16
    lanes = lax.broadcasted_iota(jnp.int32, (1, width), 1)
    sublanes = lax.broadcasted_iota(jnp.int32, (width, 1), 0)
    keys, values = k_ref[...], v_ref[...]
    att_t = dq_t = d_key = d_value = None

    for head in range(2):
        own = (lanes >= head * half) & (lanes < (head + 1) * half)
        query = jnp.where(own, q_ref[...], jnp.zeros((), low))
        grad = jnp.where(own, g_ref[...], jnp.zeros((), low))
        scores = product(keys, query, 1, 1) + bias_ref[...]
        exponent = jnp.exp(scores - jnp.max(scores, axis=0, keepdims=True))
        probs = exponent * (1.0 / jnp.sum(exponent, axis=0, keepdims=True))
        probs_low = probs.astype(low)
        att_head = product(values, probs_low, 0, 0)
        grad_probs = product(values, grad, 1, 1)
        inner_sum = jnp.sum(probs * grad_probs, axis=0, keepdims=True)
        grad_scores = (probs * (grad_probs - inner_sum)).astype(low)
        value_part = product(probs_low, grad, 1, 0)
        key_part = product(grad_scores, query, 1, 0)
        dq_head = product(keys, grad_scores, 0, 0)
        if head == 0:
            att_t, dq_t, d_key, d_value = att_head, dq_head, key_part, value_part
        else:
            upper = sublanes < half
            att_t = jnp.where(upper, att_t, att_head)
            dq_t = jnp.where(upper, dq_t, dq_head)
            d_key, d_value = d_key + key_part, d_value + value_part
    att_ref[...] = att_t.T.astype(low)
    dq_ref[...] = (dq_t.T * ((width // 2) ** -0.5)).astype(low)
    dk_ref[...] = d_key.astype(low)
    dv_ref[...] = d_value.astype(low)


def attention(chain, mixed, grad, bias):
    slots, width = grad.shape
    count = mixed.shape[0]
    pair = 2 * (width // HEADS)
    each = width // pair

    def columns(rows, turn=0):
        return pl.BlockSpec((rows, pair), lambda h, *_: (0, turn * each + h))

    low = jnp.bfloat16
    return chain.call(
        attention_kernel,
        (each,),
        [columns(slots), columns(count, 1), columns(count, 2), columns(slots), whole_array(bias.shape)],
        [
            ((slots, width), low, columns(slots)),
            ((slots, width), low, columns(slots)),
            ((count, width), low, columns(count)),
            ((count, width), low, columns(count)),
        ],
        [],
        mixed,
        mixed,
        mixed,
        grad,
        bias,
    )


def layout(heights_row, widths_row):
    pixels = heights_row * widths_row
    ends_at = jnp.cumsum(pixels)
    starts_at = ends_at - pixels
    slot_ids = jnp.arange(SLOTS, dtype=jnp.int32)
    segment = jnp.sum((ends_at[None, :] <= slot_ids[:, None]).astype(jnp.int32), axis=1)
    member = segment[:, None] == jnp.arange(LAT_ROW, dtype=jnp.int32)[None, :]
    start_at = jnp.sum(jnp.where(member, starts_at[None, :], 0), axis=1)
    height_at = jnp.sum(jnp.where(member, heights_row[None, :], 0), axis=1)
    width_at = jnp.sum(jnp.where(member, widths_row[None, :], 0), axis=1)
    place_in = slot_ids - start_at
    safe_width = jnp.maximum(width_at, 1)
    column = place_in % safe_width
    row_index = place_in // safe_width
    return (segment, member, height_at, width_at, row_index, column)


def score_bias(segment, counts_row, key_pad):
    live_query = segment < LAT_ROW
    image_ok = (segment[:, None] == segment[None, :]) & live_query[None, :]
    text_index = jnp.arange(LAT_ROW * TEXT, dtype=jnp.int32)
    text_latent = text_index // TEXT
    text_limit = jnp.sum(
        jnp.where(
            text_latent[:, None] == jnp.arange(LAT_ROW, dtype=jnp.int32)[None, :],
            counts_row[None, :],
            0,
        ),
        axis=1,
    )
    text_ok = (text_latent[:, None] == segment[None, :]) & (text_index % TEXT < text_limit)[:, None]
    no_pad = jnp.zeros((key_pad, segment.shape[0]), bool)
    return jnp.where(jnp.concatenate([image_ok, text_ok, no_pad], axis=0), 0.0, MASKED)


def geometry_table(heights_row, widths_row):
    segment, member, height_at, width_at, row_index, column = layout(heights_row, widths_row)
    live = segment < LAT_ROW
    left = live & (column >= 1)
    right = live & (column + 1 < width_at)
    up = live & (row_index >= 1)
    down = live & (row_index + 1 < height_at)
    sides = [width_at == k * SIDE_UNIT for k in (3, 4, 6)]
    columns = [live, left, right] + [up & s for s in sides] + [down & s for s in sides]
    columns = columns + [jnp.zeros_like(live)] * 7
    return segment, member, jnp.stack(columns, axis=1).astype(jnp.float32)


def local(
    inner,
    outer,
    latents,
    text_embed,
    time_embed,
    heights,
    widths,
    text_counts,
    res_vecs,
    fc1_w,
    ff_vecs,
    fc2_w,
    time_w,
    time_b,
    kv_w,
    attn_w,
    attn_vecs,
    cotangent,
):
    low, full = jnp.bfloat16, jnp.float32
    orders = scatter_orders(outer)
    outer_bits, inner_bits = bit_count(outer), bit_count(inner)
    blocks = inner * outer
    x, cot = latents[0], cotangent[0]
    slots, width = x.shape
    text_width = text_embed.shape[3]
    text_total = LAT_ROW * TEXT
    key_pad = -(slots + text_total) % 128
    mine = lax.axis_index("dp") >> (inner_bits - 1)
    chain = Chain()

    def along(spec, a, b):
        return jnp.einsum(spec, a, b, preferred_element_type=full)

    small_owned = (res_vecs, ff_vecs, time_w, time_b[None], attn_vecs)
    small_sizes = [v.size for v in small_owned]
    small_pad = -sum(small_sizes) % (8 * width)
    small_shard = jnp.concatenate(
        [v.astype(low).reshape(-1) for v in small_owned] + [jnp.zeros((small_pad,), low)]
    )

    def to_all(*shards):
        shard = jnp.concatenate([v.astype(low) for v in shards], axis=0)
        shard = jnp.pad(shard, ((0, -shard.shape[0] % 8), (0, 0)))
        full_rows = lax.all_gather(shard, ("dp", "fsdp"), axis=0, tiled=True)
        return full_rows.reshape(blocks, -1, width)

    rows, kv_rows = fc2_w.shape[0], kv_w.shape[0]
    small_rows = small_shard.size // width
    res_weights = to_all(fc1_w.T, fc2_w, kv_w, small_shard.reshape(-1, width))
    attn_weights = to_all(round_late(chain, attn_w.T, res_weights))
    fc1_t, fc2_full = Weight(res_weights, 0, rows), Weight(res_weights, 1, rows)
    attn_t = Weight(attn_weights, 0, rows)
    kv_full = res_weights[:, 2 * rows : 2 * rows + kv_rows].reshape(-1, width)
    small_all = res_weights[:, 2 * rows + kv_rows : 2 * rows + kv_rows + small_rows].reshape(blocks, -1)
    small_full = []
    taken = 0
    for owned, size in zip(small_owned, small_sizes):
        some = small_all[:, taken : taken + size].reshape(blocks, owned.shape[0], owned.shape[1])
        small_full.append(some.transpose(1, 0, 2).reshape(owned.shape[0], -1).astype(full))
        taken += size
    res_all, ff_all, time_w_all, time_b_all, vecs_all = small_full
    taps = jnp.pad(res_all[:10], ((0, 6), (0, 0)))
    vecs = jnp.pad(ff_all, ((0, 5), (0, 0)))

    segment, member_slots, geometry = geometry_table(heights[0], widths[0])
    member = jnp.pad(member_slots[::GROUP].astype(full), ((0, 0), (0, SEATS - LAT_ROW)))
    bias = score_bias(segment, text_counts[0], key_pad)
    live = geometry

    normed_low, normed, entry_scale = entry(chain, x, taps, geometry)
    act, slope, power = hidden_step(chain, normed_low, fc1_t, vecs, member)
    units = act.shape[1]
    norm = jnp.sqrt(power + NORM_EPS)
    norm_mean = jnp.mean(norm, axis=1, keepdims=True) + NORM_EPS
    norms = norm / norm_mean
    time_low = jnp.pad(time_embed[0].astype(low), ((0, SEATS - LAT_ROW), (0, 0)))
    pair = along("lt,tc->lc", time_low, time_w_all.astype(low)) + time_b_all
    response, after_res, after_time, normed_two = branch_step(
        chain, act, norms, vecs, fc2_full, member, live, x, res_all[10:11], pair
    )

    each = width // UNITS
    text = text_embed[0].astype(full).reshape(text_total, text_width)
    silu_text, silu_back = jax.vjp(jax.nn.silu, text)
    silu_low = silu_text.astype(low)
    mapped = (along("tk,kc->tc", silu_low, kv_full) + vecs_all[3]).astype(low)
    source = jnp.concatenate([normed_two, mapped, jnp.zeros((key_pad, width), low)], axis=0)
    grad_proj = (live[:, 0:1] * cot).astype(low)
    mixed_bias = jnp.concatenate([vecs_all[0], jnp.zeros((width,), full), vecs_all[1]])
    mixed, grad_attended = project(
        chain, source, grad_proj, jnp.broadcast_to(mixed_bias, (SEATS, 3 * width)), attn_t
    )
    attended, grad_query, grad_key, grad_value = attention(chain, mixed, grad_attended, bias)

    free = list(reversed(range(outer_bits + inner_bits - 1)))
    early = [b for b in free if b >= outer_bits]

    def pieces_of(kept, come=None):
        kept = kept.reshape((2,) * len(free) + (-1, width))
        pieces = []
        for order, (start, size) in zip(orders, column_pieces(width, len(orders))):
            pieces.append(Piece(kept, early + order, free, start // size, size))
            if come is not None:
                pieces[-1].come, pieces[-1].come_cut = come.reshape(kept.shape), start // size
        return pieces

    def to_partner(away):
        return swap(away, "dp", inner, inner_bits - 1)

    def halved(terms):
        half = blocks // 2
        come = to_partner(lax.dynamic_slice_in_dim(terms, (1 - mine) * half, half, axis=0))
        kept = lax.dynamic_slice_in_dim(terms, mine * half, half, axis=0)
        some = Piece(kept.reshape((2,) * len(free) + terms.shape[1:]), early + orders[2], free)
        some.come = come.reshape(some.base.shape)
        return some

    def step(group, hold=False):
        fold(chain, group, inner, outer, (), hold)

    def finished(group):
        while group[0].order:
            step(group)
        return totals_of(chain, group)

    parts = (grad_query, grad_key, grad_value, grad_proj, source, attended)
    come = to_partner(attn_half(chain, *parts, 1 - mine))
    grad_normed_two, grad_text = source_back(
        chain,
        grad_query,
        grad_key,
        grad_value,
        attn_t.by(lambda i, *_: jnp.where(i < 2 * each, i + each, i - 2 * each)),
    )
    grad_mapped = grad_text[:text_total]
    kv_terms = along("tk,tc->kc", silu_low, grad_mapped).astype(low)
    kv_piece = halved(kv_terms.reshape(blocks, -1, width))
    attn_sum = pieces_of(attn_half(chain, *parts, mine, come)) + [kv_piece]
    for _ in early:
        step(attn_sum)
    step(attn_sum)
    grad_res, grad_branch, pair_grad, res_bias_grad = time_back(
        chain, grad_normed_two, after_time, after_res, cot, pair, member, live
    )
    mine_index = mine.astype(jnp.int32)[None]
    grad_response, act_sums, shift_grad, fc2_away, fc2_kept = response_back(
        chain, grad_branch, fc2_full, act, response, member, mine_index
    )
    step(attn_sum)
    fc2_come = to_partner(late(chain, fc2_away))
    gain_grad = jnp.sum(act_sums * norms, axis=0, keepdims=True)
    norms_grad = vecs[1:2] * act_sums
    norm_grad = norms_grad / norm_mean - jnp.sum(norms_grad * norm, axis=1, keepdims=True) / (
        units * norm_mean * norm_mean
    )
    hidden_parts = (grad_response, act, slope, vecs, norms, norm_grad / norm, member, normed_low, fc1_t)
    bias_away, grad_normed, fc1_away = hidden_back(chain, *hidden_parts, 1 - mine_index)
    step(attn_sum)
    fc2_sum = pieces_of(fc2_kept, fc2_come)
    for _ in early:
        step(fc2_sum)
    step(fc2_sum, True)
    for _ in range(outer_bits - 3):
        step(attn_sum)
    send(chain, fc2_sum, inner, outer)
    bias_kept, grad_normed, fc1_kept = hidden_back(chain, *hidden_parts, mine_index, grad_normed)
    hidden_bias_grad = jnp.where(
        mine == 0,
        jnp.concatenate([bias_kept[:1], bias_away[:1]], axis=1),
        jnp.concatenate([bias_away[:1], bias_kept[:1]], axis=1),
    )
    latents_grad, taps_grad = entry_back(
        chain, grad_normed, normed, entry_scale, x, grad_res, taps, geometry, res_bias_grad
    )
    output = output_step(
        chain,
        attended,
        after_time,
        live,
        jnp.broadcast_to(vecs_all[2], (SEATS, width)),
        attn_t.by(lambda i, *_: 3 * each + i),
    )
    attn_grad, kv_grad = finished(attn_sum)
    step(fc2_sum)
    taps_grad = copy_late(chain, taps_grad)
    fc1_come = to_partner(late(chain, fc1_away))
    time_grad = jnp.einsum("lt,lc->tc", time_low.astype(full), pair_grad, precision=HIGHEST)
    small_terms = (
        taps_grad[: res_vecs.shape[0]],
        jnp.concatenate([hidden_bias_grad[:1], gain_grad, shift_grad[:1]], axis=0),
        time_grad,
        jnp.sum(pair_grad, axis=0, keepdims=True),
        jnp.stack(
            [
                jnp.sum(grad_query.astype(full), axis=0),
                jnp.sum(grad_value.astype(full), axis=0),
                jnp.sum(grad_proj.astype(full), axis=0),
                jnp.sum(grad_mapped.astype(full), axis=0),
            ]
        ),
    )
    small_blocks = jnp.concatenate(
        [g.reshape(g.shape[0], blocks, -1).transpose(1, 0, 2).reshape(blocks, -1) for g in small_terms]
        + [jnp.zeros((blocks, -sum(small_sizes) % 1024), full)],
        axis=1,
    ).reshape(blocks, -1, 128)
    small_piece = halved(small_blocks)
    step(fc2_sum)
    fc1_sum = pieces_of(fc1_kept, fc1_come) + [small_piece]
    for _ in early:
        step(fc1_sum)
    step(fc1_sum, True)
    for _ in range(outer_bits - 3):
        step(fc2_sum)
    send(chain, fc1_sum, inner, outer)
    (fc2_grad,) = finished(fc2_sum)
    step(fc1_sum)
    step(fc1_sum)
    fc1_grad, small_total = finished(fc1_sum)
    small_total = small_total.reshape(-1)
    text_grad = silu_back(along("tc,kc->tk", grad_mapped, kv_full))[0]

    small_grads = []
    taken = 0
    for owned, size in zip(small_owned, small_sizes):
        small_grads.append(small_total[taken : taken + size].reshape(owned.shape))
        taken += size
    return (
        output[None],
        latents_grad[None],
        text_grad.reshape(text_embed.shape),
        small_grads[0],
        fc1_grad.T,
        small_grads[1],
        fc2_grad,
        small_grads[2],
        small_grads[3][0],
        kv_grad,
        attn_grad.T,
        small_grads[4],
    )


def solution(mesh):
    return jax.shard_map(
        functools.partial(local, mesh.shape["dp"], mesh.shape["fsdp"]),
        mesh=mesh,
        in_specs=(
            P(("dp", "fsdp"), None, None),
            P(("dp", "fsdp"), None, None, None),
            P(("dp", "fsdp"), None, None),
            P(("dp", "fsdp"), None),
            P(("dp", "fsdp"), None),
            P(("dp", "fsdp"), None),
            P(None, ("dp", "fsdp")),
            P(None, ("dp", "fsdp")),
            P(None, ("dp", "fsdp")),
            P(("dp", "fsdp"), None),
            P(None, ("dp", "fsdp")),
            P(("dp", "fsdp")),
            P(("dp", "fsdp"), None),
            P(None, ("dp", "fsdp")),
            P(None, ("dp", "fsdp")),
            P(("dp", "fsdp"), None, None),
        ),
        out_specs=(
            P(("dp", "fsdp"), None, None),
            P(("dp", "fsdp"), None, None),
            P(("dp", "fsdp"), None, None, None),
            P(None, ("dp", "fsdp")),
            P(None, ("dp", "fsdp")),
            P(None, ("dp", "fsdp")),
            P(("dp", "fsdp"), None),
            P(None, ("dp", "fsdp")),
            P(("dp", "fsdp")),
            P(("dp", "fsdp"), None),
            P(None, ("dp", "fsdp")),
            P(None, ("dp", "fsdp")),
        ),
        check_vma=False,
    )
```

```python
import functools

import jax
import jax.numpy as jnp
from jax import lax
from jax.experimental import pallas as pl
from jax.experimental.pallas import tpu as pltpu
from jax.sharding import PartitionSpec as P

HEADS = 24
TEXT = 77
SIDE_UNIT = 4
SLOTS = 576
LAT_ROW = 4
GROUP = 16
SEATS = 8

HEAD_SCALE = 64**-0.5
LANES = 128
UNITS = 768
HIGHEST = lax.Precision.HIGHEST
NORM_EPS = 1e-06
MASKED = -1000000000.0


def bit_count(size):
    return size.bit_length() - 1


def swap(values, axis_name, size, bit):
    return lax.ppermute(values, axis_name, [(i, i ^ (1 << bit)) for i in range(size)])


def scatter_orders(size):
    bits = list(range(bit_count(size) - 1))
    return [bits[turn:] + bits[:turn] + [len(bits)] for turn in range(3)]


def column_pieces(width, count):
    if count == 1:
        return [(0, width)]
    unit = width // 12
    return [(0, 5 * unit), (5 * unit, 5 * unit), (10 * unit, 2 * unit)]


class Chain:
    def __init__(self):
        self.token = None

    def call(self, kernel, grid, ins, outs, scratch, *operands, scalars=(), after=()):
        earlier = (() if self.token is None else (self.token,)) + tuple(after)
        held, count = len(scalars), len(operands)

        def body(*refs):
            before, rest = refs[: held + count], refs[held + count + len(earlier) :]
            rest[len(outs)][...] = jnp.zeros_like(rest[len(outs)])
            kernel(*before, *rest[: len(outs)], *rest[len(outs) + 1 :])

        token_spec = pl.BlockSpec((8, 128), lambda *_: (0, 0))
        done = pl.pallas_call(
            body,
            grid_spec=pltpu.PrefetchScalarGridSpec(
                num_scalar_prefetch=held,
                grid=grid,
                in_specs=list(ins) + [pl.BlockSpec(memory_space=pl.ANY)] * len(earlier),
                out_specs=[spec for _, _, spec in outs] + [token_spec],
                scratch_shapes=list(scratch),
            ),
            out_shape=[jax.ShapeDtypeStruct(shape, dtype) for shape, dtype, _ in outs]
            + [jax.ShapeDtypeStruct((8, 128), jnp.float32)],
            compiler_params=pltpu.CompilerParams(vmem_limit_bytes=56 << 20),
        )(*scalars, *operands, *earlier)
        self.token = done[-1]
        return done[:-1]


def whole_array(shape):
    return pl.BlockSpec(shape, lambda *_: (0,) * len(shape))


class Gather:
    def __init__(self, chain, shards, orders, inner, outer):
        self.chain, self.inner, self.outer = chain, inner, outer
        self.counts = [len(some) for some in orders]
        self.orders = [order[::-1] for some in orders for order in some]
        first = self.orders[0][0]
        self.held, self.came = [], []
        for shard, some in zip(shards, orders):
            came = swap(shard[None], "fsdp", outer, first)
            for start, size in column_pieces(shard.shape[1], len(some)):
                self.held.append((shard[None], start // size, size))
                self.came.append((came, start // size, size))
        self.offsets = [[0] for _ in self.orders]
        self.number = 0

    def step(self):
        held = join(self.chain, self.held, self.came)
        self.advance()
        self.held = [(v, 0, v.shape[2]) for v in held]
        self.came = []
        for v, order in zip(held, self.orders):
            came = swap(v, "fsdp", self.outer, order[self.number])
            self.came.append((came, 0, v.shape[2]))

    def advance(self):
        for index, order in enumerate(self.orders):
            bit = 1 << order[self.number]
            self.offsets[index] = self.offsets[index] + [o ^ bit for o in self.offsets[index]]
        self.number += 1

    def finish(self, after=()):
        half = len(self.offsets[0])
        self.advance()
        places = [[offs[:half] for offs in self.offsets], [offs[half:] for offs in self.offsets]]
        parts = [[v for v, _, _ in self.held], [v for v, _, _ in self.came]]
        own = place_blocks(self.chain, parts, places, self.counts, self.outer, after)
        whole = []
        for v in own:
            some = [v]
            for bit in range(bit_count(self.inner)):
                some = some + [swap(p, "dp", self.inner, bit) for p in some]
            whole.append(some)
        return whole


def in_order(parts):
    stacked = jnp.stack(parts)
    inner = lax.axis_index("dp")
    return jnp.concatenate(
        [lax.dynamic_index_in_dim(stacked, inner ^ n, 0, keepdims=False) for n in range(len(parts))], axis=0
    )


def sides(parts):
    if len(parts) == 2:
        return parts
    whole = in_order(parts)
    half = whole.shape[0] // 2
    mine = lax.axis_index("dp") // (len(parts) // 2)
    return [lax.dynamic_slice_in_dim(whole, side * half, half, axis=0) for side in (mine, 1 - mine)]


def join_kernel(count, half, *refs):
    step = pl.program_id(0)
    for index in range(count):

        @pl.when(step < half)
        def _(index=index):
            refs[2 * count + index][...] = refs[index][...]

        @pl.when(step >= half)
        def _(index=index):
            refs[2 * count + index][...] = refs[count + index][...]


def join(chain, first, second):
    number = first[0][0].shape[0]
    each = max(number // 2, 1)
    half = number // each

    def blocks(rows, width, cut, where):
        return pl.BlockSpec((each, rows, width), lambda j, *_: (where(j), 0, cut))

    return chain.call(
        functools.partial(join_kernel, len(first), half),
        (2 * half,),
        [blocks(v.shape[1], w, n, lambda j: jnp.minimum(j, half - 1)) for v, n, w in first]
        + [blocks(v.shape[1], w, n, lambda j: jnp.maximum(j - half, 0)) for v, n, w in second],
        [
            ((2 * number, v.shape[1], w), v.dtype, blocks(v.shape[1], w, 0, lambda j: j))
            for v, n, w in first
        ],
        [],
        *[v for v, _, _ in first],
        *[v for v, _, _ in second],
    )


def place_blocks(chain, parts, places, counts, blocks, after):
    count, pieces = len(parts), len(parts[0])
    where = {}
    for number, place in enumerate(places):
        for index, offs in enumerate(place):
            for k, o in enumerate(offs):
                where[(index, o)] = (number, k)
    me = lax.axis_index("fsdp")
    offsets = [o for place in places for o in place[0]]
    part_of = [[where[(i, o)][0] for o in offsets] for i in range(pieces)]
    slot_of = [[where[(i, o)][1] for o in offsets] for i in range(pieces)]
    goal = jnp.asarray(offsets, jnp.int32) ^ me.astype(jnp.int32)
    shown = []
    for i in range(pieces):
        for p in range(count):
            now, row = 0, []
            for step in range(blocks):
                if part_of[i][step] == p:
                    now = slot_of[i][step]
                row.append(now)
            shown.append(row)
    operands = [parts[p][i] for i in range(pieces) for p in range(count)]
    outs, goals, at = [], [], 0
    for n, some in enumerate(counts):
        rows = parts[0][at].shape[1]
        width = sum(v.shape[2] for v in parts[0][at : at + some])
        goals += [(n, start, size) for start, size in column_pieces(width, some)]
        outs.append(
            (
                (blocks, rows, width),
                parts[0][at].dtype,
                pl.BlockSpec((1, rows, width), lambda b, goal, shown, part: (goal[b], 0, 0)),
            )
        )
        at += some
    return chain.call(
        functools.partial(place_kernel, count, goals),
        (blocks,),
        [
            pl.BlockSpec((1,) + v.shape[1:], lambda b, goal, shown, part, n=n: (shown[n, b], 0, 0))
            for n, v in enumerate(operands)
        ],
        outs,
        [],
        *operands,
        scalars=(goal, jnp.asarray(shown, jnp.int32), jnp.asarray(part_of, jnp.int32)),
        after=after,
    )


def place_kernel(count, goals, goal_ref, shown_ref, part_ref, *refs):
    step = pl.program_id(0)
    for i, (out, start, width) in enumerate(goals):
        for p in range(count):

            @pl.when(part_ref[i, step] == p)
            def _(i=i, out=out, start=start, width=width, source=refs[i * count + p]):
                refs[len(goals) * count + out][:, :, start : start + width] = source[...]


class Weight:
    def __init__(self, gathered, place, rows, block=lambda step, *_: step):
        if rows % GROUP:
            some = gathered[:, place * rows : (place + 1) * rows]
            gathered, place, rows = some.reshape(-1, UNITS, some.shape[2]), 0, UNITS
        self.gathered, self.place, self.rows, self.block = gathered, place, rows, block
        self.total = gathered.shape[0] * rows
        self.width = gathered.shape[2]

    def by(self, block):
        return Weight(self.gathered, self.place, self.rows, block)

    def spec(self):
        return pl.BlockSpec(
            (UNITS // self.rows, self.rows, self.width), lambda *at: (self.block(*at), self.place, 0)
        )


def rows_of(ref):
    return ref[...].reshape(UNITS, ref.shape[2])


class Piece:
    def __init__(self, base, order, bits, cut=0, width=None):
        self.base, self.order, self.bits, self.cut = base, list(order), list(bits), cut
        self.free, self.fixed, self.come, self.come_cut = list(bits), [], None, 0
        self.width = base.shape[-1] if width is None else width


def fold(chain, pieces, inner, outer, after=(), hold=False):
    if len(pieces[0].free) == 1:
        return fold_last(chain, pieces, inner, outer, after)
    me = lax.axis_index("dp") * outer + lax.axis_index("fsdp")
    left = len(pieces[0].free) - 1
    inside = min(max(left - 1, 0), 2)
    ins, outs, operands, plans, bits = [], [], [], [], []
    for piece in pieces:
        lazy = piece.come is None
        bit = piece.order.pop(0)
        bits.append(bit)
        rest = [b for b in piece.free if b != bit]
        near = rest[len(rest) - inside :]
        far = rest[: len(rest) - inside]

        def spec(axes, cut, width, rows, bit=bit, near=near, far=far, fixed=tuple(piece.fixed), lazy=lazy):
            def where(k, me_ref):
                place = []
                for b in axes:
                    if b in fixed:
                        place.append((me_ref[0] >> b) & 1)
                    elif b == bit:
                        place.append(1 - ((me_ref[0] >> b) & 1) if lazy else 0)
                    elif b in near:
                        place.append(0)
                    else:
                        place.append((k >> (len(far) - 1 - far.index(b))) & 1)
                return tuple(place) + (0, cut)

            shape = tuple(
                2 if (b in near and b not in fixed) or (b == bit and not lazy) else None for b in axes
            )
            return pl.BlockSpec(shape + (rows, width), where)

        rows = piece.base.shape[-2]
        ins.append(spec(piece.bits, piece.cut, piece.width, rows))
        operands.append(piece.base)
        if not lazy:
            ins.append(spec(piece.free, piece.come_cut, piece.width, rows))
            operands.append(piece.come)
        shape = (2,) * len(rest) + (rows, piece.width)
        outs += [(shape, piece.base.dtype, spec(rest, 0, piece.width, rows))] * (1 if lazy else 2)
        plans.append((lazy, bit, sum(1 for b in near if b > bit)))
        piece.free, piece.come_cut = rest, 0
    done = list(
        chain.call(
            functools.partial(fold_kernel, plans),
            (1 << (left - inside),),
            ins,
            outs,
            [],
            *operands,
            scalars=(me.astype(jnp.int32)[None],),
            after=after,
        )
    )
    for piece, (lazy, bit, _) in zip(pieces, plans):
        away = done.pop(0)
        if lazy:
            piece.fixed.append(bit)
        else:
            piece.base, piece.cut, piece.fixed, piece.bits = done.pop(0), 0, [], list(piece.free)
        piece.away = (away, bit)
    if not hold:
        send(chain, pieces, inner, outer, False)


def send(chain, pieces, inner, outer, wait=True):
    low_bits = bit_count(outer)
    for piece in pieces:
        away, bit = piece.away
        away = late(chain, away) if wait else away
        if bit < low_bits:
            piece.come = swap(away, "fsdp", outer, bit)
        else:
            piece.come = swap(away, "dp", inner, bit - low_bits)


def fold_kernel(plans, me_ref, *refs):
    count = sum(1 if lazy else 2 for lazy, _, _ in plans)
    ins, outs = list(refs[:count]), list(refs[count:])
    for lazy, bit, before in plans:
        if lazy:
            outs.pop(0)[...] = ins.pop(0)[...]
            continue
        base, come = ins.pop(0), ins.pop(0)
        own = (me_ref[0] >> bit) & 1
        for out, side in ((outs.pop(0), 1 - own), (outs.pop(0), own)):
            at = (slice(None),) * before + (side,)
            out[...] = (base[at].astype(jnp.float32) + come[at].astype(jnp.float32)).astype(out.dtype)


def copy_kernel(values_ref, out_ref):
    out_ref[...] = values_ref[...]


def copy_late(chain, values):
    spec = whole_array(values.shape)
    return chain.call(copy_kernel, (1,), [spec], [(values.shape, values.dtype, spec)], [], values)[0]


def keep_kernel(values_ref, token_ref, out_ref):
    pass


def late(chain, values):
    some = pl.BlockSpec(memory_space=pl.ANY)
    return pl.pallas_call(
        keep_kernel,
        out_shape=jax.ShapeDtypeStruct(values.shape, values.dtype),
        in_specs=[some, some],
        out_specs=some,
        input_output_aliases={0: 0},
    )(values, chain.token)


def last_kernel(cuts, bit, me_ref, *refs):
    own = (me_ref[0] >> bit) & 1
    ins, outs = refs[: 2 * len(cuts)], refs[2 * len(cuts) :]
    for n, (group, cut) in enumerate(cuts):
        both = ins[2 * n][...].astype(jnp.float32) + ins[2 * n + 1][...].astype(jnp.float32)
        both = both.astype(outs[2 * group].dtype)
        outs[2 * group][:, :, cut] = jnp.where(own == 0, both[1:2], both[0:1])
        outs[2 * group + 1][:, :, cut] = jnp.where(own == 0, both[0:1], both[1:2])


def fold_last(chain, pieces, inner, outer, after):
    bit = pieces[0].order.pop(0)
    me = lax.axis_index("dp") * outer + lax.axis_index("fsdp")
    operands, cuts, shapes = [], [], []
    for piece in pieces:
        operands += [piece.base, piece.come]
        rows = piece.base.shape[1]
        if not shapes or shapes[-1][1] != rows:
            shapes.append([1, rows, 0])
        start = shapes[-1][2]
        cuts.append((len(shapes) - 1, slice(start, start + piece.width)))
        shapes[-1][2] = start + piece.width
    dtypes = {piece.base.shape[1]: piece.base.dtype for piece in pieces}
    done = chain.call(
        functools.partial(last_kernel, cuts, bit),
        (1,),
        [whole_array(v.shape) for v in operands],
        [(tuple(shape), dtypes[shape[1]], whole_array(tuple(shape))) for shape in shapes for _ in range(2)],
        [],
        *operands,
        scalars=(me.astype(jnp.int32)[None],),
        after=after,
    )
    pieces[:] = [Piece(kept, [], []) for kept in done[1::2]]
    for piece, away in zip(pieces, done[::2]):
        piece.come = swap(away, "fsdp", outer, bit)


def total_kernel(count, *refs):
    for n in range(count):
        refs[2 * count + n][...] = (refs[2 * n][...].astype(jnp.float32) + refs[2 * n + 1][...].astype(jnp.float32))[0]


def totals_of(chain, pieces):
    operands = [v for piece in pieces for v in (piece.base, piece.come)]
    shapes = [piece.base.shape[1:] for piece in pieces]
    return chain.call(
        functools.partial(total_kernel, len(pieces)),
        (1,),
        [whole_array(v.shape) for v in operands],
        [(shape, jnp.float32, whole_array(shape)) for shape in shapes],
        [],
        *operands,
    )


def product(a, b, da, db):
    return lax.dot_general(a, b, (((da,), (db,)), ((), ())), preferred_element_type=jnp.float32)


def by_group(values):
    return values.reshape(values.shape[0] // GROUP, GROUP, values.shape[1])


def spread(seats, member):
    total = member[:, 0:1] * seats[0:1, :]
    for place in range(1, LAT_ROW):
        total = total + member[:, place : place + 1] * seats[place : place + 1, :]
    return total[:, None, :]


def gathered(values, member):
    by = jnp.sum(by_group(values), axis=1)
    rows = [jnp.sum(by * member[:, place : place + 1], axis=0, keepdims=True) for place in range(LAT_ROW)]
    return jnp.concatenate(rows + [jnp.zeros((SEATS - LAT_ROW, values.shape[1]), jnp.float32)], axis=0)


def neighbours(x, geometry):
    slots = x.shape[0]
    above = below = None
    for index, side in enumerate((3 * SIDE_UNIT, 4 * SIDE_UNIT, 6 * SIDE_UNIT)):
        up = geometry[3 + index] * pltpu.roll(x, side, 0)
        down = geometry[6 + index] * pltpu.roll(x, slots - side, 0)
        above = up if above is None else above + up
        below = down if below is None else below + down
    return above, geometry[0] * x, below


def geometry_columns(geometry_ref):
    return [geometry_ref[:, k : k + 1] for k in range(9)]


def entry_kernel(x_ref, taps_ref, geometry_ref, low_ref, normed_ref, scale_ref, conv_ref):
    slots, width = x_ref.shape
    geometry = geometry_columns(geometry_ref)
    total = jnp.zeros((slots, LANES), jnp.float32)
    for start in range(0, width, LANES):
        cut = slice(start, start + LANES)
        rows = neighbours(x_ref[:, cut], geometry)
        left, mid, right = (
            sum(taps_ref[3 * a + b : 3 * a + b + 1, cut] * rows[a] for a in range(3)) for b in range(3)
        )
        conv = (
            taps_ref[9:10, cut]
            + mid
            + geometry[1] * pltpu.roll(left, 1, 0)
            + geometry[2] * pltpu.roll(right, slots - 1, 0)
        )
        conv_ref[:, cut] = conv
        total = total + conv
    mean = jnp.sum(total, axis=1, keepdims=True) * (1.0 / width)
    square = jnp.zeros((slots, LANES), jnp.float32)
    for start in range(0, width, LANES):
        center = conv_ref[:, start : start + LANES] - mean
        square = square + center * center
    scale = lax.rsqrt(jnp.sum(square, axis=1, keepdims=True) * (1.0 / width) + NORM_EPS)
    scale_ref[...] = jnp.broadcast_to(scale, scale_ref.shape)
    for start in range(0, width, LANES):
        cut = slice(start, start + LANES)
        normed = (conv_ref[:, cut] - mean) * scale
        normed_ref[:, cut] = normed
        low_ref[:, cut] = normed.astype(jnp.bfloat16)


def entry(chain, x, taps, geometry):
    slots, width = x.shape
    return chain.call(
        entry_kernel,
        (1,),
        [whole_array(v.shape) for v in (x, taps, geometry)],
        [
            ((slots, width), jnp.bfloat16, whole_array((slots, width))),
            ((slots, width), jnp.float32, whole_array((slots, width))),
            ((slots, LANES), jnp.float32, whole_array((slots, LANES))),
        ],
        [pltpu.VMEM((slots, width), jnp.float32)],
        x,
        taps,
        geometry,
    )


def entry_back_kernel(q_ref, normed_ref, scale_ref, x_ref, res_ref, taps_ref, geometry_ref, bias_grad_ref, grad_ref, taps_grad_ref):
    slots, width = x_ref.shape
    geometry = geometry_columns(geometry_ref)
    scale = scale_ref[:, 0:1]
    plain = jnp.zeros((slots, LANES), jnp.float32)
    along = jnp.zeros((slots, LANES), jnp.float32)
    for start in range(0, width, LANES):
        cut = slice(start, start + LANES)
        q = q_ref[:, cut]
        plain = plain + q
        along = along + q * normed_ref[:, cut]
    plain = jnp.sum(plain, axis=1, keepdims=True) * (1.0 / width)
    along = jnp.sum(along, axis=1, keepdims=True) * (1.0 / width)
    for start in range(0, width, LANES):
        cut = slice(start, start + LANES)
        grad = (q_ref[:, cut] - plain - normed_ref[:, cut] * along) * scale
        sides = (
            pltpu.roll(grad * geometry[1], slots - 1, 0),
            grad,
            pltpu.roll(grad * geometry[2], 1, 0),
        )
        rows = neighbours(x_ref[:, cut], geometry)
        sums = [
            jnp.sum(rows[a] * sides[b], axis=0, keepdims=True) for a in range(3) for b in range(3)
        ]
        sums.append(jnp.sum(grad, axis=0, keepdims=True))
        sums.append(bias_grad_ref[0:1, cut])
        sums.append(jnp.zeros((5, LANES), jnp.float32))
        taps_grad_ref[:, cut] = jnp.concatenate(sums, axis=0)
        above, mid, below = (
            sum(taps_ref[3 * a + b : 3 * a + b + 1, cut] * sides[b] for b in range(3)) for a in range(3)
        )
        back = res_ref[:, cut] + geometry[0] * mid
        for index, side in enumerate((3 * SIDE_UNIT, 4 * SIDE_UNIT, 6 * SIDE_UNIT)):
            back = back + pltpu.roll(geometry[3 + index] * above, slots - side, 0)
            back = back + pltpu.roll(geometry[6 + index] * below, side, 0)
        grad_ref[:, cut] = back


def entry_back(chain, q, normed, scale, x, res, taps, geometry, bias_grad):
    slots, width = x.shape
    operands = (q, normed, scale, x, res, taps, geometry, bias_grad)
    return chain.call(
        entry_back_kernel,
        (1,),
        [whole_array(v.shape) for v in operands],
        [
            ((slots, width), jnp.float32, whole_array((slots, width))),
            ((16, width), jnp.float32, whole_array((16, width))),
        ],
        [],
        *operands,
    )


def hidden_kernel(normed_ref, vecs_ref, member_ref, *refs):
    weight_ref, act_ref, slope_ref, power_ref = refs
    hidden = product(normed_ref[...], rows_of(weight_ref), 1, 1) + vecs_ref[0:1, :]
    below = 0.5 + 0.5 * lax.erf(hidden * (0.5**0.5))
    act = hidden * below
    act_ref[...] = act
    slope_ref[...] = below + hidden * (jnp.exp(-0.5 * hidden * hidden) * (0.5 / jnp.pi) ** 0.5)
    power_ref[...] = gathered(act * act, member_ref[...])


def unit_columns(rows):
    return pl.BlockSpec((rows, UNITS), lambda i, *_: (0, i))


def hidden_step(chain, normed, weight, vecs, member):
    slots, width = normed.shape
    units = weight.total
    return chain.call(
        hidden_kernel,
        (units // UNITS,),
        [whole_array((slots, width)), unit_columns(vecs.shape[0]), whole_array(member.shape)] + [weight.spec()],
        [
            ((slots, units), jnp.float32, unit_columns(slots)),
            ((slots, units), jnp.float32, unit_columns(slots)),
            ((SEATS, units), jnp.float32, unit_columns(SEATS)),
        ],
        [],
        normed,
        vecs,
        member,
        weight.gathered,
    )


def norm_rows(values):
    center = values - jnp.mean(values, axis=-1, keepdims=True)
    scale = lax.rsqrt(jnp.mean(center * center, axis=-1, keepdims=True) + NORM_EPS)
    return center * scale, scale


def branch_kernel(last, side_ref, act_ref, norms_ref, vecs_ref, member_ref, weight_ref, *refs):
    step = pl.program_id(0)
    member = member_ref[...]
    act = by_group(act_ref[...])
    response = act * (1.0 + vecs_ref[1:2, :][None] * spread(norms_ref[...], member)) + vecs_ref[2:3, :][None]
    response = response.reshape(act_ref.shape).astype(jnp.bfloat16)
    part = product(response, rows_of(weight_ref), 1, 0)
    if not last:
        response_ref, total_ref = refs
        response_ref[...] = response

        @pl.when(step == 0)
        def _():
            total_ref[...] = part

        @pl.when(step > 0)
        def _():
            total_ref[...] += part

        return
    before_ref, live_ref, x_ref, bias_ref, pair_ref, response_ref, res_ref, time_ref, low_ref, total_ref = refs
    response_ref[...] = response

    @pl.when(step == 0)
    def _():
        total_ref[...] = before_ref[...] + part

    @pl.when(step > 0)
    def _():
        total_ref[...] += part

    @pl.when(step == pl.num_programs(0) - 1)
    def _():
        width = x_ref.shape[1]
        after_res = x_ref[...] + live_ref[:, 0:1] * (total_ref[...] + bias_ref[...])
        res_ref[...] = after_res
        per = spread(pair_ref[...], member)
        after_time = by_group(after_res) * (1.0 + per[:, :, :width]) + per[:, :, width:]
        after_time = after_time.reshape(after_res.shape)
        time_ref[...] = after_time
        low_ref[...] = norm_rows(after_time)[0].astype(jnp.bfloat16)


def side_block(half):
    return lambda step, side_ref: side_ref[0] * half + step


def branch_step(chain, act, norms, vecs, weight, member, side, rest=()):
    slots, units = act.shape
    width = weight.width
    steps = units // UNITS
    whole = ((slots, width), jnp.float32, whole_array((slots, width)))
    outs = [((slots, units), jnp.bfloat16, unit_columns(slots)), whole]
    if rest:
        outs += [whole, ((slots, width), jnp.bfloat16, whole_array((slots, width)))]
    return chain.call(
        functools.partial(branch_kernel, len(rest) > 0),
        (steps,),
        [
            unit_columns(slots),
            unit_columns(SEATS),
            unit_columns(vecs.shape[0]),
            whole_array(member.shape),
            weight.by(side_block(steps)).spec(),
        ]
        + [whole_array(v.shape) for v in rest],
        outs,
        [pltpu.VMEM((slots, width), jnp.float32)] if rest else [],
        act,
        norms,
        vecs,
        member,
        weight.gathered,
        *rest,
        scalars=(side,),
    )


def time_back_kernel(q_ref, time_ref, res_ref, cot_ref, pair_ref, member_ref, live_ref, grad_ref, low_ref, pair_grad_ref, bias_grad_ref):
    width = q_ref.shape[1]
    member = member_ref[...]
    normed, scale = norm_rows(time_ref[...])
    q = q_ref[...]
    plain = jnp.mean(q, axis=-1, keepdims=True)
    along = jnp.mean(q * normed, axis=-1, keepdims=True)
    grad_time = cot_ref[...] + (q - plain - normed * along) * scale
    pair_grad_ref[:, :width] = gathered(grad_time * res_ref[...], member)
    pair_grad_ref[:, width:] = gathered(grad_time, member)
    per = spread(pair_ref[:, :width], member)
    grad_res = (by_group(grad_time) * (1.0 + per)).reshape(q.shape)
    grad_ref[...] = grad_res
    low = (live_ref[:, 0:1] * grad_res).astype(jnp.bfloat16)
    low_ref[...] = low
    bias_grad_ref[...] = jnp.broadcast_to(jnp.sum(low.astype(jnp.float32), axis=0, keepdims=True), bias_grad_ref.shape)


def time_back(chain, q, after_time, after_res, cot, pair, member, live):
    slots, width = q.shape
    operands = (q, after_time, after_res, cot, pair, member, live)
    return chain.call(
        time_back_kernel,
        (1,),
        [whole_array(v.shape) for v in operands],
        [
            ((slots, width), jnp.float32, whole_array((slots, width))),
            ((slots, width), jnp.bfloat16, whole_array((slots, width))),
            ((SEATS, 2 * width), jnp.float32, whole_array((SEATS, 2 * width))),
            ((SEATS, width), jnp.float32, whole_array((SEATS, width))),
        ],
        [],
        *operands,
    )


def response_back_kernel(side_ref, branch_ref, act_ref, response_ref, member_ref, weight_ref, grad_ref, sums_ref, shift_ref, rows_ref):
    grad = product(branch_ref[...], rows_of(weight_ref), 1, 1)
    grad_ref[...] = grad
    sums_ref[...] = gathered(grad * act_ref[...], member_ref[...])
    shift_ref[...] = jnp.broadcast_to(jnp.sum(grad, axis=0, keepdims=True), shift_ref.shape)
    rows_ref[...] = product(response_ref[...], branch_ref[...], 0, 0).astype(jnp.bfloat16)


def response_back(chain, branch, weight, act, response, member, side):
    slots, width = branch.shape
    units = act.shape[1]
    steps = units // UNITS
    return chain.call(
        response_back_kernel,
        (steps,),
        [
            whole_array(branch.shape),
            unit_columns(slots),
            unit_columns(slots),
            whole_array(member.shape),
            weight.by(side_block(steps)).spec(),
        ],
        [
            ((slots, units), jnp.float32, unit_columns(slots)),
            ((SEATS, units), jnp.float32, unit_columns(SEATS)),
            ((SEATS, units), jnp.float32, unit_columns(SEATS)),
            ((units, width), jnp.bfloat16, pl.BlockSpec((UNITS, width), lambda i, *_: (i, 0))),
        ],
        [],
        branch,
        act,
        response,
        member,
        weight.gathered,
        scalars=(side,),
    )


def hidden_back_kernel(added, grad_ref, act_ref, slope_ref, vecs_ref, norms_ref, ratio_ref, member_ref, normed_ref, weight_ref, *refs):
    bias_ref, normed_grad_ref, rows_ref, total_ref = refs[-4:]
    step = pl.program_id(0)
    member = member_ref[...]
    grad = by_group(grad_ref[...]) * (1.0 + vecs_ref[1:2, :][None] * spread(norms_ref[...], member))
    grad = grad + by_group(act_ref[...]) * spread(ratio_ref[...], member)
    low = (grad.reshape(act_ref.shape) * slope_ref[...]).astype(jnp.bfloat16)
    bias_ref[...] = jnp.broadcast_to(jnp.sum(low.astype(jnp.float32), axis=0, keepdims=True), bias_ref.shape)
    rows_ref[...] = product(low, normed_ref[...], 0, 0).astype(jnp.bfloat16)
    part = product(low, rows_of(weight_ref), 1, 0)

    @pl.when(step == 0)
    def _():
        total_ref[...] = part + refs[0][...] if added else part

    @pl.when(step > 0)
    def _():
        total_ref[...] += part

    @pl.when(step == pl.num_programs(0) - 1)
    def _():
        normed_grad_ref[...] = total_ref[...]


def hidden_back(chain, grad, act, slope, vecs, norms, ratio, member, normed, weight, before=None):
    slots, units = act.shape
    width = weight.width
    before = () if before is None else (before,)
    return chain.call(
        functools.partial(hidden_back_kernel, len(before) > 0),
        (units // UNITS,),
        [unit_columns(slots)] * 3
        + [unit_columns(vecs.shape[0]), unit_columns(SEATS), unit_columns(SEATS)]
        + [whole_array(member.shape), whole_array(normed.shape), weight.spec()]
        + [whole_array(v.shape) for v in before],
        [
            ((SEATS, units), jnp.float32, unit_columns(SEATS)),
            ((slots, width), jnp.float32, whole_array((slots, width))),
            ((units, width), jnp.bfloat16, pl.BlockSpec((UNITS, width), lambda i, *_: (i, 0))),
        ],
        [pltpu.VMEM((slots, width), jnp.float32)],
        grad,
        act,
        slope,
        vecs,
        norms,
        ratio,
        member,
        normed,
        weight.gathered,
        *before,
    )


def project_kernel(source_ref, grad_ref, bias_ref, *refs):
    weight_ref, out_ref, att_grad_ref, total_ref = refs
    step = pl.program_id(0)
    each = pl.num_programs(0) // 4
    weight = rows_of(weight_ref)

    @pl.when(step < 3 * each)
    def _():
        out = (product(source_ref[...], weight, 1, 1) + bias_ref[0:1, :]).astype(jnp.bfloat16)
        scale = jnp.where(step < each, HEAD_SCALE, 1.0).astype(jnp.bfloat16)
        out_ref[...] = out * scale

    @pl.when(step >= 3 * each)
    def _():
        part = product(grad_ref[...], weight, 1, 0)

        @pl.when(step == 3 * each)
        def _():
            total_ref[...] = part

        @pl.when(step > 3 * each)
        def _():
            total_ref[...] += part

        @pl.when(step == 4 * each - 1)
        def _():
            att_grad_ref[...] = total_ref[...].astype(jnp.bfloat16)


def project(chain, source, grad, bias, weight):
    count, width = source.shape
    slots = grad.shape[0]
    each = width // UNITS
    return chain.call(
        project_kernel,
        (4 * each,),
        [
            whole_array(source.shape),
            pl.BlockSpec((slots, UNITS), lambda i, *_: (0, jnp.maximum(i - 3 * each, 0))),
            pl.BlockSpec((SEATS, UNITS), lambda i, *_: (0, jnp.minimum(i, 3 * each - 1))),
        ]
        + [weight.spec()],
        [
            (
                (count, 3 * width),
                jnp.bfloat16,
                pl.BlockSpec((count, UNITS), lambda i, *_: (0, jnp.minimum(i, 3 * each - 1))),
            ),
            ((slots, width), jnp.bfloat16, whole_array((slots, width))),
        ],
        [pltpu.VMEM((slots, width), jnp.float32)],
        source,
        grad,
        bias,
        weight.gathered,
    )


def source_back_kernel(query_ref, key_ref, value_ref, *refs):
    weight_ref, slot_ref, text_ref, total_ref = refs
    step = pl.program_id(0)
    each = pl.num_programs(0) // 3
    slots = slot_ref.shape[0]
    weight = rows_of(weight_ref)

    @pl.when(step == 0)
    def _():
        total_ref[...] = product(key_ref[...], weight, 1, 0)

    @pl.when((step > 0) & (step < each))
    def _():
        total_ref[...] += product(key_ref[...], weight, 1, 0)

    @pl.when((step >= each) & (step < 2 * each))
    def _():
        total_ref[...] += product(value_ref[...], weight, 1, 0)

    @pl.when(step >= 2 * each)
    def _():
        total_ref[:slots, :] += product(query_ref[...], weight, 1, 0)

    @pl.when(step == 3 * each - 1)
    def _():
        slot_ref[...] = total_ref[:slots, :]
        text_ref[...] = total_ref[slots:, :].astype(jnp.bfloat16)


def source_back(chain, query, keys, values, weight):
    slots, width = query.shape
    count = keys.shape[0]
    each = width // UNITS

    def columns(rows, turn):
        return pl.BlockSpec((rows, UNITS), lambda i, *_: (0, jnp.clip(i - turn * each, 0, each - 1)))

    return chain.call(
        source_back_kernel,
        (3 * each,),
        [columns(slots, 2), columns(count, 0), columns(count, 1)]
        + [weight.spec()],
        [
            ((slots, width), jnp.float32, whole_array((slots, width))),
            ((count - slots, width), jnp.bfloat16, whole_array((count - slots, width))),
        ],
        [pltpu.VMEM((count, width), jnp.float32)],
        query,
        keys,
        values,
        weight.gathered,
    )


def output_kernel(attended_ref, time_ref, live_ref, bias_ref, weight_ref, out_ref):
    out = product(attended_ref[...], rows_of(weight_ref), 1, 1) + bias_ref[0:1, :]
    out_ref[...] = time_ref[...] + live_ref[:, 0:1] * out


def output_step(chain, attended, after_time, live, bias, weight):
    slots, width = attended.shape
    each = width // UNITS
    columns = pl.BlockSpec((slots, UNITS), lambda i, *_: (0, i))
    return chain.call(
        output_kernel,
        (each,),
        [
            whole_array(attended.shape),
            columns,
            whole_array(live.shape),
            pl.BlockSpec((SEATS, UNITS), lambda i, *_: (0, i)),
        ]
        + [weight.spec()],
        [((slots, width), jnp.float32, columns)],
        [],
        attended,
        after_time,
        live,
        bias,
        weight.gathered,
    )[0]


def attn_half_kernel(added, half_ref, query_ref, key_ref, value_ref, proj_ref, source_ref, attended_ref, *refs):
    out_ref = refs[-1]
    role = 2 * half_ref[0] + pl.program_id(0) // (pl.num_programs(0) // 2)
    slots = query_ref.shape[0]

    def store(total):
        if added:
            total = total + refs[0][...].astype(jnp.float32)
        out_ref[...] = total.astype(jnp.bfloat16)

    @pl.when(role == 0)
    def _():
        store(product(query_ref[...], source_ref[:slots, :], 0, 0))

    @pl.when(role == 1)
    def _():
        store(product(key_ref[...], source_ref[...], 0, 0))

    @pl.when(role == 2)
    def _():
        store(product(value_ref[...], source_ref[...], 0, 0))

    @pl.when(role == 3)
    def _():
        store(product(proj_ref[...], attended_ref[...], 0, 0))


def attn_half(chain, query, keys, values, proj, source, attended, half, come=None):
    width = source.shape[1]
    each = width // UNITS
    rows = pl.BlockSpec((UNITS, width), lambda i, *_: (i, 0))

    def columns(values, role):
        def where(i, half_ref):
            return (0, jnp.where(2 * half_ref[0] + i // each == role, i % each, 0))

        return pl.BlockSpec((values.shape[0], UNITS), where)

    return chain.call(
        functools.partial(attn_half_kernel, come is not None),
        (2 * each,),
        [columns(v, n) for n, v in enumerate((query, keys, values, proj))]
        + [whole_array(source.shape), whole_array(attended.shape)]
        + ([] if come is None else [rows]),
        [((2 * width, width), jnp.bfloat16, rows)],
        [],
        query,
        keys,
        values,
        proj,
        source,
        attended,
        *(() if come is None else (come,)),
        scalars=(half.astype(jnp.int32)[None],),
    )[0]


def attention_kernel(q_ref, k_ref, v_ref, g_ref, bias_ref, att_ref, dq_ref, dk_ref, dv_ref):
    slots, width = q_ref.shape
    half = width // 2
    low = jnp.bfloat16
    lanes = lax.broadcasted_iota(jnp.int32, (1, width), 1)
    first = lanes < half
    keys, values = k_ref[...], v_ref[...]

    def both(ref):
        rows, none = ref[...], jnp.zeros((), low)
        return jnp.concatenate([jnp.where(first, rows, none), jnp.where(first, none, rows)], axis=0)

    def beside(turned):
        rows = turned.T
        return jnp.where(first, rows[:slots], rows[slots:])

    query, grad = both(q_ref), both(g_ref)
    scores = product(keys, query, 1, 1) + bias_ref[...]
    exponent = jnp.exp(scores - jnp.max(scores, axis=0, keepdims=True))
    probs = exponent * (1.0 / jnp.sum(exponent, axis=0, keepdims=True))
    probs_low = probs.astype(low)
    att_ref[...] = beside(product(values, probs_low, 0, 0)).astype(low)
    grad_probs = product(values, grad, 1, 1)
    inner_sum = jnp.sum(probs * grad_probs, axis=0, keepdims=True)
    grad_scores = (probs * (grad_probs - inner_sum)).astype(low)
    dv_ref[...] = product(probs_low, grad, 1, 0).astype(low)
    dk_ref[...] = product(grad_scores, query, 1, 0).astype(low)
    dq_ref[...] = (beside(product(keys, grad_scores, 0, 0)) * HEAD_SCALE).astype(low)


def attention(chain, mixed, grad, bias):
    slots, width = grad.shape
    count = mixed.shape[0]
    pair = 2 * (width // HEADS)
    each = width // pair

    def columns(rows, turn=0):
        return pl.BlockSpec((rows, pair), lambda h, *_: (0, turn * each + h))

    low = jnp.bfloat16
    return chain.call(
        attention_kernel,
        (each,),
        [columns(slots), columns(count, 1), columns(count, 2), columns(slots), whole_array(bias.shape)],
        [
            ((slots, width), low, columns(slots)),
            ((slots, width), low, columns(slots)),
            ((count, width), low, columns(count)),
            ((count, width), low, columns(count)),
        ],
        [],
        mixed,
        mixed,
        mixed,
        grad,
        bias,
    )


def layout(heights_row, widths_row):
    pixels = heights_row * widths_row
    ends_at = jnp.cumsum(pixels)
    starts_at = ends_at - pixels
    slot_ids = jnp.arange(SLOTS, dtype=jnp.int32)
    segment = jnp.sum((ends_at[None, :] <= slot_ids[:, None]).astype(jnp.int32), axis=1)
    member = segment[:, None] == jnp.arange(LAT_ROW, dtype=jnp.int32)[None, :]
    start_at = jnp.sum(jnp.where(member, starts_at[None, :], 0), axis=1)
    height_at = jnp.sum(jnp.where(member, heights_row[None, :], 0), axis=1)
    width_at = jnp.sum(jnp.where(member, widths_row[None, :], 0), axis=1)
    place_in = slot_ids - start_at
    safe_width = jnp.maximum(width_at, 1)
    column = place_in % safe_width
    row_index = place_in // safe_width
    return (segment, member, height_at, width_at, row_index, column)


def score_bias(segment, counts_row, key_pad):
    live_query = segment < LAT_ROW
    image_ok = (segment[:, None] == segment[None, :]) & live_query[None, :]
    text_index = jnp.arange(LAT_ROW * TEXT, dtype=jnp.int32)
    text_latent = text_index // TEXT
    text_limit = jnp.sum(
        jnp.where(
            text_latent[:, None] == jnp.arange(LAT_ROW, dtype=jnp.int32)[None, :],
            counts_row[None, :],
            0,
        ),
        axis=1,
    )
    text_ok = (text_latent[:, None] == segment[None, :]) & (text_index % TEXT < text_limit)[:, None]
    no_pad = jnp.zeros((key_pad, segment.shape[0]), bool)
    return jnp.where(jnp.concatenate([image_ok, text_ok, no_pad], axis=0), 0.0, MASKED)


def geometry_table(heights_row, widths_row):
    segment, member, height_at, width_at, row_index, column = layout(heights_row, widths_row)
    live = segment < LAT_ROW
    left = live & (column >= 1)
    right = live & (column + 1 < width_at)
    up = live & (row_index >= 1)
    down = live & (row_index + 1 < height_at)
    sides = [width_at == k * SIDE_UNIT for k in (3, 4, 6)]
    columns = [live, left, right] + [up & s for s in sides] + [down & s for s in sides]
    columns = columns + [jnp.zeros_like(live)] * 7
    return segment, member, jnp.stack(columns, axis=1).astype(jnp.float32)


def local(
    inner,
    outer,
    latents,
    text_embed,
    time_embed,
    heights,
    widths,
    text_counts,
    res_vecs,
    fc1_w,
    ff_vecs,
    fc2_w,
    time_w,
    time_b,
    kv_w,
    attn_w,
    attn_vecs,
    cotangent,
):
    low, full = jnp.bfloat16, jnp.float32
    orders = scatter_orders(outer)
    outer_bits, inner_bits = bit_count(outer), bit_count(inner)
    blocks = inner * outer
    x, cot = latents[0], cotangent[0]
    slots, width = x.shape
    text_width = text_embed.shape[3]
    text_total = LAT_ROW * TEXT
    key_pad = -(slots + text_total) % 128
    mine = lax.axis_index("dp") >> (inner_bits - 1)
    chain = Chain()

    def along(spec, a, b):
        return jnp.einsum(spec, a, b, preferred_element_type=full)

    small_owned = (res_vecs, ff_vecs, time_w, time_b[None], attn_vecs)
    small_sizes = [v.size for v in small_owned]
    small_pad = -sum(small_sizes) % (16 * 128)
    small_shard = jnp.concatenate(
        [v.astype(low).reshape(-1) for v in small_owned] + [jnp.zeros((small_pad,), low)]
    )
    rows, kv_rows = fc2_w.shape[0], kv_w.shape[0]
    def to_all(shard):
        shard = jnp.pad(shard, ((0, -shard.shape[0] % 8), (0, 0)))
        return lax.all_gather(late(chain, shard), ("dp", "fsdp"), axis=0, tiled=True).reshape(blocks, -1, width)

    first = Gather(
        chain, [fc1_w.T.astype(low), small_shard.reshape(-1, 128)], [orders, orders[2:]], inner, outer
    )
    first.step()
    first.step()
    second_all = to_all(jnp.concatenate([fc2_w.astype(low), kv_w.astype(low)], axis=0))
    for _ in range(outer_bits - 3):
        first.step()
    fc1_parts, small_all = first.finish()
    attn_all = to_all(attn_w.T.astype(low))
    fc1_t = [Weight(part, 0, rows) for part in sides(fc1_parts)]
    small_all = in_order(small_all).reshape(blocks, -1)
    small_full = []
    taken = 0
    for owned, size in zip(small_owned, small_sizes):
        some = small_all[:, taken : taken + size].reshape(blocks, owned.shape[0], owned.shape[1])
        small_full.append(some.transpose(1, 0, 2).reshape(owned.shape[0], -1).astype(full))
        taken += size
    res_all, ff_all, time_w_all, time_b_all, vecs_all = small_full
    taps = jnp.pad(res_all[:10], ((0, 6), (0, 0)))
    mine_index = mine.astype(jnp.int32)[None]
    side_index = [mine_index, 1 - mine_index]

    def halves(values):
        half = values.shape[1] // 2
        return [lax.dynamic_slice_in_dim(values, side * half, half, axis=1) for side in (mine, 1 - mine)]

    def ordered(own, other):
        return jnp.where(
            mine == 0, jnp.concatenate([own, other], axis=1), jnp.concatenate([other, own], axis=1)
        )

    vecs = halves(jnp.pad(ff_all, ((0, 5), (0, 0))))

    segment, member_slots, geometry = geometry_table(heights[0], widths[0])
    member = jnp.pad(member_slots[::GROUP].astype(full), ((0, 0), (0, SEATS - LAT_ROW)))
    bias = score_bias(segment, text_counts[0], key_pad)
    bias = jnp.concatenate([bias, bias], axis=1)
    live = geometry

    normed_low, normed, entry_scale = entry(chain, x, taps, geometry)
    hidden = [hidden_step(chain, normed_low, fc1_t[n], vecs[n], member) for n in range(2)]
    act, slope, power = zip(*hidden)
    second_all = late(chain, second_all)
    fc2_full = Weight(second_all, 0, rows)
    kv_full = second_all[:, rows : rows + kv_rows].reshape(-1, width)
    norm = [jnp.sqrt(v + NORM_EPS) for v in power]
    units = 2 * act[0].shape[1]
    norm_mean = sum(jnp.sum(v, axis=1, keepdims=True) for v in norm) * (1.0 / units) + NORM_EPS
    norms = [v / norm_mean for v in norm]
    time_low = jnp.pad(time_embed[0].astype(low), ((0, SEATS - LAT_ROW), (0, 0)))
    pair = along("lt,tc->lc", time_low, time_w_all.astype(low)) + time_b_all
    response_own, branch_part = branch_step(chain, act[0], norms[0], vecs[0], fc2_full, member, side_index[0])
    response_other, after_res, after_time, normed_two = branch_step(
        chain, act[1], norms[1], vecs[1], fc2_full, member, side_index[1],
        (branch_part, live, x, res_all[10:11], pair),
    )

    each = width // UNITS
    text = text_embed[0].astype(full).reshape(text_total, text_width)
    silu_text, silu_back = jax.vjp(jax.nn.silu, text)
    silu_low = silu_text.astype(low)
    mapped = (along("tk,kc->tc", silu_low, kv_full) + vecs_all[3]).astype(low)
    source = jnp.concatenate([normed_two, mapped, jnp.zeros((key_pad, width), low)], axis=0)
    source = copy_late(chain, source)
    attn_t = Weight(late(chain, attn_all), 0, rows)
    grad_proj = (live[:, 0:1] * cot).astype(low)
    mixed_bias = jnp.concatenate([vecs_all[0], jnp.zeros((width,), full), vecs_all[1]])
    mixed, grad_attended = project(
        chain, source, grad_proj, jnp.broadcast_to(mixed_bias, (SEATS, 3 * width)), attn_t
    )
    attended, grad_query, grad_key, grad_value = attention(chain, mixed, grad_attended, bias)

    free = list(reversed(range(outer_bits + inner_bits - 1)))
    early = [b for b in free if b >= outer_bits]

    def pieces_of(kept, come=None):
        kept = kept.reshape((2,) * len(free) + (-1, width))
        pieces = []
        for order, (start, size) in zip(orders, column_pieces(width, len(orders))):
            pieces.append(Piece(kept, early + order, free, start // size, size))
            if come is not None:
                pieces[-1].come, pieces[-1].come_cut = come.reshape(kept.shape), start // size
        return pieces

    def to_partner(away):
        return swap(away, "dp", inner, inner_bits - 1)

    def halved(terms):
        half = blocks // 2
        come = to_partner(lax.dynamic_slice_in_dim(terms, (1 - mine) * half, half, axis=0))
        kept = lax.dynamic_slice_in_dim(terms, mine * half, half, axis=0)
        some = Piece(kept.reshape((2,) * len(free) + terms.shape[1:]), early + orders[2], free)
        some.come = come.reshape(some.base.shape)
        return some

    def step(group, hold=False):
        fold(chain, group, inner, outer, (), hold)

    def finished(group):
        while group[0].order:
            step(group)
        return totals_of(chain, group)

    parts = (grad_query, grad_key, grad_value, grad_proj, source, attended)
    come = to_partner(attn_half(chain, *parts, 1 - mine))
    grad_normed_two, grad_text = source_back(
        chain,
        grad_query,
        grad_key,
        grad_value,
        attn_t.by(lambda i, *_: jnp.where(i < 2 * each, i + each, i - 2 * each)),
    )
    grad_mapped = grad_text[:text_total]
    kv_terms = along("tk,tc->kc", silu_low, grad_mapped).astype(low)
    kv_piece = halved(kv_terms.reshape(blocks, -1, width))
    attn_sum = pieces_of(attn_half(chain, *parts, mine, come)) + [kv_piece]
    for _ in early:
        step(attn_sum)
    step(attn_sum)
    grad_res, grad_branch, pair_grad, res_bias_grad = time_back(
        chain, grad_normed_two, after_time, after_res, cot, pair, member, live
    )
    grad_other, sums_other, shift_other, fc2_away = response_back(
        chain, grad_branch, fc2_full, act[1], response_other, member, side_index[1]
    )
    grad_own, sums_own, shift_own, fc2_kept = response_back(
        chain, grad_branch, fc2_full, act[0], response_own, member, side_index[0]
    )
    step(attn_sum)
    fc2_come = to_partner(late(chain, fc2_away))
    sums = [sums_own, sums_other]
    gain_grad = ordered(*[jnp.sum(v * n, axis=0, keepdims=True) for v, n in zip(sums, norms)])
    shift_grad = ordered(shift_own[:1], shift_other[:1])
    norms_grad = [g[1:2] * v for g, v in zip(vecs, sums)]
    common = sum(jnp.sum(g * n, axis=1, keepdims=True) for g, n in zip(norms_grad, norm)) / (
        units * norm_mean * norm_mean
    )
    ratio = [(g / norm_mean - common) / n for g, n in zip(norms_grad, norm)]

    def hidden_grads(n, grad, before=None):
        return hidden_back(
            chain, grad, act[n], slope[n], vecs[n], norms[n], ratio[n], member, normed_low, fc1_t[n], before
        )

    bias_away, grad_normed, fc1_away = hidden_grads(1, grad_other)
    step(attn_sum)
    fc2_sum = pieces_of(fc2_kept, fc2_come)
    for _ in early:
        step(fc2_sum)
    step(fc2_sum, True)
    for _ in range(outer_bits - 3):
        step(attn_sum)
    send(chain, fc2_sum, inner, outer)
    bias_kept, grad_normed, fc1_kept = hidden_grads(0, grad_own, grad_normed)
    hidden_bias_grad = ordered(bias_kept[:1], bias_away[:1])
    latents_grad, taps_grad = entry_back(
        chain, grad_normed, normed, entry_scale, x, grad_res, taps, geometry, res_bias_grad
    )
    attn_grad, kv_grad = finished(attn_sum)
    step(fc2_sum)
    taps_grad = copy_late(chain, taps_grad)
    fc1_come = to_partner(late(chain, fc1_away))
    time_grad = jnp.einsum("lt,lc->tc", time_low.astype(full), pair_grad, precision=HIGHEST)
    small_terms = (
        taps_grad[: res_vecs.shape[0]],
        jnp.concatenate([hidden_bias_grad[:1], gain_grad, shift_grad[:1]], axis=0),
        time_grad,
        jnp.sum(pair_grad, axis=0, keepdims=True),
        jnp.stack(
            [
                jnp.sum(grad_query.astype(full), axis=0),
                jnp.sum(grad_value.astype(full), axis=0),
                jnp.sum(grad_proj.astype(full), axis=0),
                jnp.sum(grad_mapped.astype(full), axis=0),
            ]
        ),
    )
    small_blocks = jnp.concatenate(
        [g.reshape(g.shape[0], blocks, -1).transpose(1, 0, 2).reshape(blocks, -1) for g in small_terms]
        + [jnp.zeros((blocks, -sum(small_sizes) % 1024), full)],
        axis=1,
    ).reshape(blocks, -1, 128)
    small_piece = halved(small_blocks)
    step(fc2_sum)
    fc1_sum = pieces_of(fc1_kept, fc1_come) + [small_piece]
    for _ in early:
        step(fc1_sum)
    step(fc1_sum, True)
    for _ in range(outer_bits - 3):
        step(fc2_sum)
    send(chain, fc1_sum, inner, outer)
    output = output_step(
        chain,
        attended,
        after_time,
        live,
        jnp.broadcast_to(vecs_all[2], (SEATS, width)),
        attn_t.by(lambda i, *_: 3 * each + i),
    )
    (fc2_grad,) = finished(fc2_sum)
    step(fc1_sum)
    step(fc1_sum)
    fc1_grad, small_total = finished(fc1_sum)
    small_total = small_total.reshape(-1)
    text_grad = silu_back(along("tc,kc->tk", grad_mapped, kv_full))[0]

    small_grads = []
    taken = 0
    for owned, size in zip(small_owned, small_sizes):
        small_grads.append(small_total[taken : taken + size].reshape(owned.shape))
        taken += size
    return (
        output[None],
        latents_grad[None],
        text_grad.reshape(text_embed.shape),
        small_grads[0],
        fc1_grad.T,
        small_grads[1],
        fc2_grad,
        small_grads[2],
        small_grads[3][0],
        kv_grad,
        attn_grad.T,
        small_grads[4],
    )


def solution(mesh):
    return jax.shard_map(
        functools.partial(local, mesh.shape["dp"], mesh.shape["fsdp"]),
        mesh=mesh,
        in_specs=(
            P(("dp", "fsdp"), None, None),
            P(("dp", "fsdp"), None, None, None),
            P(("dp", "fsdp"), None, None),
            P(("dp", "fsdp"), None),
            P(("dp", "fsdp"), None),
            P(("dp", "fsdp"), None),
            P(None, ("dp", "fsdp")),
            P(None, ("dp", "fsdp")),
            P(None, ("dp", "fsdp")),
            P(("dp", "fsdp"), None),
            P(None, ("dp", "fsdp")),
            P(("dp", "fsdp")),
            P(("dp", "fsdp"), None),
            P(None, ("dp", "fsdp")),
            P(None, ("dp", "fsdp")),
            P(("dp", "fsdp"), None, None),
        ),
        out_specs=(
            P(("dp", "fsdp"), None, None),
            P(("dp", "fsdp"), None, None),
            P(("dp", "fsdp"), None, None, None),
            P(None, ("dp", "fsdp")),
            P(None, ("dp", "fsdp")),
            P(None, ("dp", "fsdp")),
            P(("dp", "fsdp"), None),
            P(None, ("dp", "fsdp")),
            P(("dp", "fsdp")),
            P(("dp", "fsdp"), None),
            P(None, ("dp", "fsdp")),
            P(None, ("dp", "fsdp")),
        ),
        check_vma=False,
    )
```

```python
import functools

import jax
import jax.numpy as jnp
from jax import lax
from jax.experimental import pallas as pl
from jax.experimental.pallas import tpu as pltpu
from jax.sharding import PartitionSpec as P

HEADS = 24
TEXT = 77
SIDE_UNIT = 4
SLOTS = 576
LAT_ROW = 4
GROUP = 16
SEATS = 8

HEAD_SCALE = 64**-0.5
LANES = 128
UNITS = 768
HIGHEST = lax.Precision.HIGHEST
NORM_EPS = 1e-06
MASKED = -1000000000.0


def bit_count(size):
    return size.bit_length() - 1


def swap(values, axis_name, size, bit):
    return lax.ppermute(values, axis_name, [(i, i ^ (1 << bit)) for i in range(size)])


def scatter_orders(size):
    bits = list(range(bit_count(size) - 1))
    return [bits[turn:] + bits[:turn] + [len(bits)] for turn in range(3)]


def column_pieces(width, count):
    if count == 1:
        return [(0, width)]
    unit = width // 12
    return [(0, 5 * unit), (5 * unit, 5 * unit), (10 * unit, 2 * unit)]


class Chain:
    def __init__(self):
        self.token = None

    def call(self, kernel, grid, ins, outs, scratch, *operands, scalars=(), after=()):
        earlier = (() if self.token is None else (self.token,)) + tuple(after)
        held, count = len(scalars), len(operands)

        def body(*refs):
            before, rest = refs[: held + count], refs[held + count + len(earlier) :]
            rest[len(outs)][...] = jnp.zeros_like(rest[len(outs)])
            kernel(*before, *rest[: len(outs)], *rest[len(outs) + 1 :])

        token_spec = pl.BlockSpec((8, 128), lambda *_: (0, 0))
        done = pl.pallas_call(
            body,
            grid_spec=pltpu.PrefetchScalarGridSpec(
                num_scalar_prefetch=held,
                grid=grid,
                in_specs=list(ins) + [pl.BlockSpec(memory_space=pl.ANY)] * len(earlier),
                out_specs=[spec for _, _, spec in outs] + [token_spec],
                scratch_shapes=list(scratch),
            ),
            out_shape=[jax.ShapeDtypeStruct(shape, dtype) for shape, dtype, _ in outs]
            + [jax.ShapeDtypeStruct((8, 128), jnp.float32)],
            compiler_params=pltpu.CompilerParams(vmem_limit_bytes=56 << 20),
        )(*scalars, *operands, *earlier)
        self.token = done[-1]
        return done[:-1]


def whole_array(shape):
    return pl.BlockSpec(shape, lambda *_: (0,) * len(shape))


class Gather:
    def __init__(self, chain, shards, orders, inner, outer):
        self.chain, self.inner, self.outer = chain, inner, outer
        self.counts = [len(some) for some in orders]
        self.orders = [order[::-1] for some in orders for order in some]
        first = self.orders[0][0]
        self.held, self.came = [], []
        for shard, some in zip(shards, orders):
            came = swap(shard[None], "fsdp", outer, first)
            for start, size in column_pieces(shard.shape[1], len(some)):
                self.held.append((shard[None], start // size, size))
                self.came.append((came, start // size, size))
        self.offsets = [[0] for _ in self.orders]
        self.number = 0

    def step(self):
        held = join(self.chain, self.held, self.came)
        self.advance()
        self.held = [(v, 0, v.shape[2]) for v in held]
        self.came = []
        for v, order in zip(held, self.orders):
            came = swap(v, "fsdp", self.outer, order[self.number])
            self.came.append((came, 0, v.shape[2]))

    def advance(self):
        for index, order in enumerate(self.orders):
            bit = 1 << order[self.number]
            self.offsets[index] = self.offsets[index] + [o ^ bit for o in self.offsets[index]]
        self.number += 1

    def finish(self, after=()):
        half = len(self.offsets[0])
        self.advance()
        places = [[offs[:half] for offs in self.offsets], [offs[half:] for offs in self.offsets]]
        parts = [[v for v, _, _ in self.held], [v for v, _, _ in self.came]]
        own = place_blocks(self.chain, parts, places, self.counts, self.outer, after)
        whole = []
        for v in own:
            some = [v]
            for bit in range(bit_count(self.inner)):
                some = some + [swap(p, "dp", self.inner, bit) for p in some]
            whole.append(some)
        return whole


def in_order(parts):
    stacked = jnp.stack(parts)
    inner = lax.axis_index("dp")
    return jnp.concatenate(
        [lax.dynamic_index_in_dim(stacked, inner ^ n, 0, keepdims=False) for n in range(len(parts))], axis=0
    )


def sides(parts):
    if len(parts) == 2:
        return parts
    whole = in_order(parts)
    half = whole.shape[0] // 2
    mine = lax.axis_index("dp") // (len(parts) // 2)
    return [lax.dynamic_slice_in_dim(whole, side * half, half, axis=0) for side in (mine, 1 - mine)]


def join_kernel(count, half, *refs):
    step = pl.program_id(0)
    for index in range(count):

        @pl.when(step < half)
        def _(index=index):
            refs[2 * count + index][...] = refs[index][...]

        @pl.when(step >= half)
        def _(index=index):
            refs[2 * count + index][...] = refs[count + index][...]


def join(chain, first, second):
    number = first[0][0].shape[0]
    each = max(number // 2, 1)
    half = number // each

    def blocks(rows, width, cut, where):
        return pl.BlockSpec((each, rows, width), lambda j, *_: (where(j), 0, cut))

    return chain.call(
        functools.partial(join_kernel, len(first), half),
        (2 * half,),
        [blocks(v.shape[1], w, n, lambda j: jnp.minimum(j, half - 1)) for v, n, w in first]
        + [blocks(v.shape[1], w, n, lambda j: jnp.maximum(j - half, 0)) for v, n, w in second],
        [
            ((2 * number, v.shape[1], w), v.dtype, blocks(v.shape[1], w, 0, lambda j: j))
            for v, n, w in first
        ],
        [],
        *[v for v, _, _ in first],
        *[v for v, _, _ in second],
    )


def place_blocks(chain, parts, places, counts, blocks, after):
    count, pieces = len(parts), len(parts[0])
    where = {}
    for number, place in enumerate(places):
        for index, offs in enumerate(place):
            for k, o in enumerate(offs):
                where[(index, o)] = (number, k)
    me = lax.axis_index("fsdp")
    offsets = [o for place in places for o in place[0]]
    part_of = [[where[(i, o)][0] for o in offsets] for i in range(pieces)]
    slot_of = [[where[(i, o)][1] for o in offsets] for i in range(pieces)]
    goal = jnp.asarray(offsets, jnp.int32) ^ me.astype(jnp.int32)
    shown = []
    for i in range(pieces):
        for p in range(count):
            now, row = 0, []
            for step in range(blocks):
                if part_of[i][step] == p:
                    now = slot_of[i][step]
                row.append(now)
            shown.append(row)
    operands = [parts[p][i] for i in range(pieces) for p in range(count)]
    outs, goals, at = [], [], 0
    for n, some in enumerate(counts):
        rows = parts[0][at].shape[1]
        width = sum(v.shape[2] for v in parts[0][at : at + some])
        goals += [(n, start, size) for start, size in column_pieces(width, some)]
        outs.append(
            (
                (blocks, rows, width),
                parts[0][at].dtype,
                pl.BlockSpec((1, rows, width), lambda b, goal, shown, part: (goal[b], 0, 0)),
            )
        )
        at += some
    return chain.call(
        functools.partial(place_kernel, count, goals),
        (blocks,),
        [
            pl.BlockSpec((1,) + v.shape[1:], lambda b, goal, shown, part, n=n: (shown[n, b], 0, 0))
            for n, v in enumerate(operands)
        ],
        outs,
        [],
        *operands,
        scalars=(goal, jnp.asarray(shown, jnp.int32), jnp.asarray(part_of, jnp.int32)),
        after=after,
    )


def place_kernel(count, goals, goal_ref, shown_ref, part_ref, *refs):
    step = pl.program_id(0)
    for i, (out, start, width) in enumerate(goals):
        for p in range(count):

            @pl.when(part_ref[i, step] == p)
            def _(i=i, out=out, start=start, width=width, source=refs[i * count + p]):
                refs[len(goals) * count + out][:, :, start : start + width] = source[...]


class Weight:
    def __init__(self, gathered, place, rows, block=lambda step, *_: step):
        if rows % GROUP:
            some = gathered[:, place * rows : (place + 1) * rows]
            gathered, place, rows = some.reshape(-1, UNITS, some.shape[2]), 0, UNITS
        self.gathered, self.place, self.rows, self.block = gathered, place, rows, block
        self.total = gathered.shape[0] * rows
        self.width = gathered.shape[2]

    def by(self, block):
        return Weight(self.gathered, self.place, self.rows, block)

    def spec(self):
        return pl.BlockSpec(
            (UNITS // self.rows, self.rows, self.width), lambda *at: (self.block(*at), self.place, 0)
        )


def rows_of(ref):
    return ref[...].reshape(UNITS, ref.shape[2])


class Piece:
    def __init__(self, base, order, bits, cut=0, width=None):
        self.base, self.order, self.bits, self.cut = base, list(order), list(bits), cut
        self.free, self.fixed, self.come, self.come_cut = list(bits), [], None, 0
        self.width = base.shape[-1] if width is None else width


def fold(chain, pieces, inner, outer, after=(), hold=False):
    if len(pieces[0].free) == 1:
        return fold_last(chain, pieces, inner, outer, after)
    me = lax.axis_index("dp") * outer + lax.axis_index("fsdp")
    left = len(pieces[0].free) - 1
    inside = min(max(left - 1, 0), 2)
    ins, outs, operands, plans, bits = [], [], [], [], []
    for piece in pieces:
        lazy = piece.come is None
        bit = piece.order.pop(0)
        bits.append(bit)
        rest = [b for b in piece.free if b != bit]
        near = rest[len(rest) - inside :]
        far = rest[: len(rest) - inside]

        def spec(axes, cut, width, rows, bit=bit, near=near, far=far, fixed=tuple(piece.fixed), lazy=lazy):
            def where(k, me_ref):
                place = []
                for b in axes:
                    if b in fixed:
                        place.append((me_ref[0] >> b) & 1)
                    elif b == bit:
                        place.append(1 - ((me_ref[0] >> b) & 1) if lazy else 0)
                    elif b in near:
                        place.append(0)
                    else:
                        place.append((k >> (len(far) - 1 - far.index(b))) & 1)
                return tuple(place) + (0, cut)

            shape = tuple(
                2 if (b in near and b not in fixed) or (b == bit and not lazy) else None for b in axes
            )
            return pl.BlockSpec(shape + (rows, width), where)

        rows = piece.base.shape[-2]
        ins.append(spec(piece.bits, piece.cut, piece.width, rows))
        operands.append(piece.base)
        if not lazy:
            ins.append(spec(piece.free, piece.come_cut, piece.width, rows))
            operands.append(piece.come)
        shape = (2,) * len(rest) + (rows, piece.width)
        outs += [(shape, piece.base.dtype, spec(rest, 0, piece.width, rows))] * (1 if lazy else 2)
        plans.append((lazy, bit, sum(1 for b in near if b > bit)))
        piece.free, piece.come_cut = rest, 0
    done = list(
        chain.call(
            functools.partial(fold_kernel, plans),
            (1 << (left - inside),),
            ins,
            outs,
            [],
            *operands,
            scalars=(me.astype(jnp.int32)[None],),
            after=after,
        )
    )
    for piece, (lazy, bit, _) in zip(pieces, plans):
        away = done.pop(0)
        if lazy:
            piece.fixed.append(bit)
        else:
            piece.base, piece.cut, piece.fixed, piece.bits = done.pop(0), 0, [], list(piece.free)
        piece.away = (away, bit)
    if not hold:
        send(chain, pieces, inner, outer, False)


def send(chain, pieces, inner, outer, wait=True):
    low_bits = bit_count(outer)
    for piece in pieces:
        away, bit = piece.away
        away = late(chain, away) if wait else away
        if bit < low_bits:
            piece.come = swap(away, "fsdp", outer, bit)
        else:
            piece.come = swap(away, "dp", inner, bit - low_bits)


def fold_kernel(plans, me_ref, *refs):
    count = sum(1 if lazy else 2 for lazy, _, _ in plans)
    ins, outs = list(refs[:count]), list(refs[count:])
    for lazy, bit, before in plans:
        if lazy:
            outs.pop(0)[...] = ins.pop(0)[...]
            continue
        base, come = ins.pop(0), ins.pop(0)
        own = (me_ref[0] >> bit) & 1
        for out, side in ((outs.pop(0), 1 - own), (outs.pop(0), own)):
            at = (slice(None),) * before + (side,)
            out[...] = (base[at].astype(jnp.float32) + come[at].astype(jnp.float32)).astype(out.dtype)


def copy_kernel(values_ref, out_ref):
    out_ref[...] = values_ref[...]


def copy_late(chain, values):
    spec = whole_array(values.shape)
    return chain.call(copy_kernel, (1,), [spec], [(values.shape, values.dtype, spec)], [], values)[0]


def keep_kernel(values_ref, token_ref, out_ref):
    pass


def late(chain, values):
    some = pl.BlockSpec(memory_space=pl.ANY)
    return pl.pallas_call(
        keep_kernel,
        out_shape=jax.ShapeDtypeStruct(values.shape, values.dtype),
        in_specs=[some, some],
        out_specs=some,
        input_output_aliases={0: 0},
    )(values, chain.token)


def last_kernel(cuts, bit, me_ref, *refs):
    own = (me_ref[0] >> bit) & 1
    ins, outs = refs[: 2 * len(cuts)], refs[2 * len(cuts) :]
    for n, (group, cut) in enumerate(cuts):
        both = ins[2 * n][...].astype(jnp.float32) + ins[2 * n + 1][...].astype(jnp.float32)
        both = both.astype(outs[2 * group].dtype)
        outs[2 * group][:, :, cut] = jnp.where(own == 0, both[1:2], both[0:1])
        outs[2 * group + 1][:, :, cut] = jnp.where(own == 0, both[0:1], both[1:2])


def fold_last(chain, pieces, inner, outer, after):
    bit = pieces[0].order.pop(0)
    me = lax.axis_index("dp") * outer + lax.axis_index("fsdp")
    operands, cuts, shapes = [], [], []
    for piece in pieces:
        operands += [piece.base, piece.come]
        rows = piece.base.shape[1]
        if not shapes or shapes[-1][1] != rows:
            shapes.append([1, rows, 0])
        start = shapes[-1][2]
        cuts.append((len(shapes) - 1, slice(start, start + piece.width)))
        shapes[-1][2] = start + piece.width
    dtypes = {piece.base.shape[1]: piece.base.dtype for piece in pieces}
    done = chain.call(
        functools.partial(last_kernel, cuts, bit),
        (1,),
        [whole_array(v.shape) for v in operands],
        [(tuple(shape), dtypes[shape[1]], whole_array(tuple(shape))) for shape in shapes for _ in range(2)],
        [],
        *operands,
        scalars=(me.astype(jnp.int32)[None],),
        after=after,
    )
    pieces[:] = [Piece(kept, [], []) for kept in done[1::2]]
    for piece, away in zip(pieces, done[::2]):
        piece.come = swap(away, "fsdp", outer, bit)


def total_kernel(count, *refs):
    for n in range(count):
        refs[2 * count + n][...] = (refs[2 * n][...].astype(jnp.float32) + refs[2 * n + 1][...].astype(jnp.float32))[0]


def totals_of(chain, pieces, after=()):
    operands = [v for piece in pieces for v in (piece.base, piece.come)]
    shapes = [piece.base.shape[1:] for piece in pieces]
    return chain.call(
        functools.partial(total_kernel, len(pieces)),
        (1,),
        [whole_array(v.shape) for v in operands],
        [(shape, jnp.float32, whole_array(shape)) for shape in shapes],
        [],
        *operands,
        after=after,
    )


def product(a, b, da, db):
    return lax.dot_general(a, b, (((da,), (db,)), ((), ())), preferred_element_type=jnp.float32)


def by_group(values):
    return values.reshape(values.shape[0] // GROUP, GROUP, values.shape[1])


def spread(seats, member):
    total = member[:, 0:1] * seats[0:1, :]
    for place in range(1, LAT_ROW):
        total = total + member[:, place : place + 1] * seats[place : place + 1, :]
    return total[:, None, :]


def gathered(values, member):
    by = jnp.sum(by_group(values), axis=1)
    rows = [jnp.sum(by * member[:, place : place + 1], axis=0, keepdims=True) for place in range(LAT_ROW)]
    return jnp.concatenate(rows + [jnp.zeros((SEATS - LAT_ROW, values.shape[1]), jnp.float32)], axis=0)


def neighbours(x, geometry):
    slots = x.shape[0]
    above = below = None
    for index, side in enumerate((3 * SIDE_UNIT, 4 * SIDE_UNIT, 6 * SIDE_UNIT)):
        up = geometry[3 + index] * pltpu.roll(x, side, 0)
        down = geometry[6 + index] * pltpu.roll(x, slots - side, 0)
        above = up if above is None else above + up
        below = down if below is None else below + down
    return above, geometry[0] * x, below


def geometry_columns(geometry_ref):
    return [geometry_ref[:, k : k + 1] for k in range(9)]


def entry_kernel(x_ref, taps_ref, geometry_ref, low_ref, normed_ref, scale_ref, conv_ref):
    slots, width = x_ref.shape
    geometry = geometry_columns(geometry_ref)
    total = jnp.zeros((slots, LANES), jnp.float32)
    for start in range(0, width, LANES):
        cut = slice(start, start + LANES)
        rows = neighbours(x_ref[:, cut], geometry)
        left, mid, right = (
            sum(taps_ref[3 * a + b : 3 * a + b + 1, cut] * rows[a] for a in range(3)) for b in range(3)
        )
        conv = (
            taps_ref[9:10, cut]
            + mid
            + geometry[1] * pltpu.roll(left, 1, 0)
            + geometry[2] * pltpu.roll(right, slots - 1, 0)
        )
        conv_ref[:, cut] = conv
        total = total + conv
    mean = jnp.sum(total, axis=1, keepdims=True) * (1.0 / width)
    square = jnp.zeros((slots, LANES), jnp.float32)
    for start in range(0, width, LANES):
        center = conv_ref[:, start : start + LANES] - mean
        square = square + center * center
    scale = lax.rsqrt(jnp.sum(square, axis=1, keepdims=True) * (1.0 / width) + NORM_EPS)
    scale_ref[...] = jnp.broadcast_to(scale, scale_ref.shape)
    for start in range(0, width, LANES):
        cut = slice(start, start + LANES)
        normed = (conv_ref[:, cut] - mean) * scale
        normed_ref[:, cut] = normed
        low_ref[:, cut] = normed.astype(jnp.bfloat16)


def entry(chain, x, taps, geometry):
    slots, width = x.shape
    return chain.call(
        entry_kernel,
        (1,),
        [whole_array(v.shape) for v in (x, taps, geometry)],
        [
            ((slots, width), jnp.bfloat16, whole_array((slots, width))),
            ((slots, width), jnp.float32, whole_array((slots, width))),
            ((slots, LANES), jnp.float32, whole_array((slots, LANES))),
        ],
        [pltpu.VMEM((slots, width), jnp.float32)],
        x,
        taps,
        geometry,
    )


def entry_back_kernel(q_ref, normed_ref, scale_ref, x_ref, res_ref, taps_ref, geometry_ref, bias_grad_ref, grad_ref, taps_grad_ref):
    slots, width = x_ref.shape
    geometry = geometry_columns(geometry_ref)
    scale = scale_ref[:, 0:1]
    plain = jnp.zeros((slots, LANES), jnp.float32)
    along = jnp.zeros((slots, LANES), jnp.float32)
    for start in range(0, width, LANES):
        cut = slice(start, start + LANES)
        q = q_ref[:, cut]
        plain = plain + q
        along = along + q * normed_ref[:, cut]
    plain = jnp.sum(plain, axis=1, keepdims=True) * (1.0 / width)
    along = jnp.sum(along, axis=1, keepdims=True) * (1.0 / width)
    for start in range(0, width, LANES):
        cut = slice(start, start + LANES)
        grad = (q_ref[:, cut] - plain - normed_ref[:, cut] * along) * scale
        sides = (
            pltpu.roll(grad * geometry[1], slots - 1, 0),
            grad,
            pltpu.roll(grad * geometry[2], 1, 0),
        )
        rows = neighbours(x_ref[:, cut], geometry)
        sums = [
            jnp.sum(rows[a] * sides[b], axis=0, keepdims=True) for a in range(3) for b in range(3)
        ]
        sums.append(jnp.sum(grad, axis=0, keepdims=True))
        sums.append(bias_grad_ref[0:1, cut])
        sums.append(jnp.zeros((5, LANES), jnp.float32))
        taps_grad_ref[:, cut] = jnp.concatenate(sums, axis=0)
        above, mid, below = (
            sum(taps_ref[3 * a + b : 3 * a + b + 1, cut] * sides[b] for b in range(3)) for a in range(3)
        )
        back = res_ref[:, cut] + geometry[0] * mid
        for index, side in enumerate((3 * SIDE_UNIT, 4 * SIDE_UNIT, 6 * SIDE_UNIT)):
            back = back + pltpu.roll(geometry[3 + index] * above, slots - side, 0)
            back = back + pltpu.roll(geometry[6 + index] * below, side, 0)
        grad_ref[:, cut] = back


def entry_back(chain, q, normed, scale, x, res, taps, geometry, bias_grad):
    slots, width = x.shape
    operands = (q, normed, scale, x, res, taps, geometry, bias_grad)
    return chain.call(
        entry_back_kernel,
        (1,),
        [whole_array(v.shape) for v in operands],
        [
            ((slots, width), jnp.float32, whole_array((slots, width))),
            ((16, width), jnp.float32, whole_array((16, width))),
        ],
        [],
        *operands,
    )


def hidden_kernel(normed_ref, vecs_ref, member_ref, *refs):
    weight_ref, act_ref, slope_ref, power_ref = refs
    hidden = product(normed_ref[...], rows_of(weight_ref), 1, 1) + vecs_ref[0:1, :]
    below = 0.5 + 0.5 * lax.erf(hidden * (0.5**0.5))
    act = hidden * below
    act_ref[...] = act
    slope_ref[...] = below + hidden * (jnp.exp(-0.5 * hidden * hidden) * (0.5 / jnp.pi) ** 0.5)
    power_ref[...] = gathered(act * act, member_ref[...])


def unit_columns(rows):
    return pl.BlockSpec((rows, UNITS), lambda i, *_: (0, i))


def hidden_step(chain, normed, weight, vecs, member):
    slots, width = normed.shape
    units = weight.total
    return chain.call(
        hidden_kernel,
        (units // UNITS,),
        [whole_array((slots, width)), unit_columns(vecs.shape[0]), whole_array(member.shape)] + [weight.spec()],
        [
            ((slots, units), jnp.float32, unit_columns(slots)),
            ((slots, units), jnp.float32, unit_columns(slots)),
            ((SEATS, units), jnp.float32, unit_columns(SEATS)),
        ],
        [],
        normed,
        vecs,
        member,
        weight.gathered,
    )


def norm_rows(values):
    center = values - jnp.mean(values, axis=-1, keepdims=True)
    scale = lax.rsqrt(jnp.mean(center * center, axis=-1, keepdims=True) + NORM_EPS)
    return center * scale, scale


def branch_kernel(last, side_ref, act_ref, norms_ref, vecs_ref, member_ref, weight_ref, *refs):
    step = pl.program_id(0)
    member = member_ref[...]
    act = by_group(act_ref[...])
    response = act * (1.0 + vecs_ref[1:2, :][None] * spread(norms_ref[...], member)) + vecs_ref[2:3, :][None]
    response = response.reshape(act_ref.shape).astype(jnp.bfloat16)
    part = product(response, rows_of(weight_ref), 1, 0)
    if not last:
        response_ref, total_ref = refs
        response_ref[...] = response

        @pl.when(step == 0)
        def _():
            total_ref[...] = part

        @pl.when(step > 0)
        def _():
            total_ref[...] += part

        return
    before_ref, live_ref, x_ref, bias_ref, pair_ref, response_ref, res_ref, time_ref, low_ref, total_ref = refs
    response_ref[...] = response

    @pl.when(step == 0)
    def _():
        total_ref[...] = before_ref[...] + part

    @pl.when(step > 0)
    def _():
        total_ref[...] += part

    @pl.when(step == pl.num_programs(0) - 1)
    def _():
        width = x_ref.shape[1]
        after_res = x_ref[...] + live_ref[:, 0:1] * (total_ref[...] + bias_ref[...])
        res_ref[...] = after_res
        per = spread(pair_ref[...], member)
        after_time = by_group(after_res) * (1.0 + per[:, :, :width]) + per[:, :, width:]
        after_time = after_time.reshape(after_res.shape)
        time_ref[...] = after_time
        low_ref[...] = norm_rows(after_time)[0].astype(jnp.bfloat16)


def side_block(half):
    return lambda step, side_ref: side_ref[0] * half + step


def branch_step(chain, act, norms, vecs, weight, member, side, rest=()):
    slots, units = act.shape
    width = weight.width
    steps = units // UNITS
    whole = ((slots, width), jnp.float32, whole_array((slots, width)))
    outs = [((slots, units), jnp.bfloat16, unit_columns(slots)), whole]
    if rest:
        outs += [whole, ((slots, width), jnp.bfloat16, whole_array((slots, width)))]
    return chain.call(
        functools.partial(branch_kernel, len(rest) > 0),
        (steps,),
        [
            unit_columns(slots),
            unit_columns(SEATS),
            unit_columns(vecs.shape[0]),
            whole_array(member.shape),
            weight.by(side_block(steps)).spec(),
        ]
        + [whole_array(v.shape) for v in rest],
        outs,
        [pltpu.VMEM((slots, width), jnp.float32)] if rest else [],
        act,
        norms,
        vecs,
        member,
        weight.gathered,
        *rest,
        scalars=(side,),
    )


def time_back_kernel(q_ref, time_ref, res_ref, cot_ref, pair_ref, member_ref, live_ref, grad_ref, low_ref, pair_grad_ref, bias_grad_ref):
    width = q_ref.shape[1]
    member = member_ref[...]
    normed, scale = norm_rows(time_ref[...])
    q = q_ref[...]
    plain = jnp.mean(q, axis=-1, keepdims=True)
    along = jnp.mean(q * normed, axis=-1, keepdims=True)
    grad_time = cot_ref[...] + (q - plain - normed * along) * scale
    pair_grad_ref[:, :width] = gathered(grad_time * res_ref[...], member)
    pair_grad_ref[:, width:] = gathered(grad_time, member)
    per = spread(pair_ref[:, :width], member)
    grad_res = (by_group(grad_time) * (1.0 + per)).reshape(q.shape)
    grad_ref[...] = grad_res
    low = (live_ref[:, 0:1] * grad_res).astype(jnp.bfloat16)
    low_ref[...] = low
    bias_grad_ref[...] = jnp.broadcast_to(jnp.sum(low.astype(jnp.float32), axis=0, keepdims=True), bias_grad_ref.shape)


def time_back(chain, q, after_time, after_res, cot, pair, member, live):
    slots, width = q.shape
    operands = (q, after_time, after_res, cot, pair, member, live)
    return chain.call(
        time_back_kernel,
        (1,),
        [whole_array(v.shape) for v in operands],
        [
            ((slots, width), jnp.float32, whole_array((slots, width))),
            ((slots, width), jnp.bfloat16, whole_array((slots, width))),
            ((SEATS, 2 * width), jnp.float32, whole_array((SEATS, 2 * width))),
            ((SEATS, width), jnp.float32, whole_array((SEATS, width))),
        ],
        [],
        *operands,
    )


def response_back_kernel(side_ref, branch_ref, act_ref, response_ref, member_ref, weight_ref, grad_ref, sums_ref, shift_ref, rows_ref):
    grad = product(branch_ref[...], rows_of(weight_ref), 1, 1)
    grad_ref[...] = grad
    sums_ref[...] = gathered(grad * act_ref[...], member_ref[...])
    shift_ref[...] = jnp.broadcast_to(jnp.sum(grad, axis=0, keepdims=True), shift_ref.shape)
    rows_ref[...] = product(response_ref[...], branch_ref[...], 0, 0).astype(jnp.bfloat16)


def response_back(chain, branch, weight, act, response, member, side):
    slots, width = branch.shape
    units = act.shape[1]
    steps = units // UNITS
    return chain.call(
        response_back_kernel,
        (steps,),
        [
            whole_array(branch.shape),
            unit_columns(slots),
            unit_columns(slots),
            whole_array(member.shape),
            weight.by(side_block(steps)).spec(),
        ],
        [
            ((slots, units), jnp.float32, unit_columns(slots)),
            ((SEATS, units), jnp.float32, unit_columns(SEATS)),
            ((SEATS, units), jnp.float32, unit_columns(SEATS)),
            ((units, width), jnp.bfloat16, pl.BlockSpec((UNITS, width), lambda i, *_: (i, 0))),
        ],
        [],
        branch,
        act,
        response,
        member,
        weight.gathered,
        scalars=(side,),
    )


def hidden_back_kernel(added, grad_ref, act_ref, slope_ref, vecs_ref, norms_ref, ratio_ref, member_ref, normed_ref, weight_ref, *refs):
    bias_ref, normed_grad_ref, rows_ref, total_ref = refs[-4:]
    step = pl.program_id(0)
    member = member_ref[...]
    grad = by_group(grad_ref[...]) * (1.0 + vecs_ref[1:2, :][None] * spread(norms_ref[...], member))
    grad = grad + by_group(act_ref[...]) * spread(ratio_ref[...], member)
    low = (grad.reshape(act_ref.shape) * slope_ref[...]).astype(jnp.bfloat16)
    bias_ref[...] = jnp.broadcast_to(jnp.sum(low.astype(jnp.float32), axis=0, keepdims=True), bias_ref.shape)
    rows_ref[...] = product(low, normed_ref[...], 0, 0).astype(jnp.bfloat16)
    part = product(low, rows_of(weight_ref), 1, 0)

    @pl.when(step == 0)
    def _():
        total_ref[...] = part + refs[0][...] if added else part

    @pl.when(step > 0)
    def _():
        total_ref[...] += part

    @pl.when(step == pl.num_programs(0) - 1)
    def _():
        normed_grad_ref[...] = total_ref[...]


def hidden_back(chain, grad, act, slope, vecs, norms, ratio, member, normed, weight, before=None):
    slots, units = act.shape
    width = weight.width
    before = () if before is None else (before,)
    return chain.call(
        functools.partial(hidden_back_kernel, len(before) > 0),
        (units // UNITS,),
        [unit_columns(slots)] * 3
        + [unit_columns(vecs.shape[0]), unit_columns(SEATS), unit_columns(SEATS)]
        + [whole_array(member.shape), whole_array(normed.shape), weight.spec()]
        + [whole_array(v.shape) for v in before],
        [
            ((SEATS, units), jnp.float32, unit_columns(SEATS)),
            ((slots, width), jnp.float32, whole_array((slots, width))),
            ((units, width), jnp.bfloat16, pl.BlockSpec((UNITS, width), lambda i, *_: (i, 0))),
        ],
        [pltpu.VMEM((slots, width), jnp.float32)],
        grad,
        act,
        slope,
        vecs,
        norms,
        ratio,
        member,
        normed,
        weight.gathered,
        *before,
    )


def project_kernel(source_ref, grad_ref, bias_ref, *refs):
    weight_ref, out_ref, att_grad_ref, total_ref = refs
    step = pl.program_id(0)
    each = pl.num_programs(0) // 4
    weight = rows_of(weight_ref)

    @pl.when(step < 3 * each)
    def _():
        out = (product(source_ref[...], weight, 1, 1) + bias_ref[0:1, :]).astype(jnp.bfloat16)
        scale = jnp.where(step < each, HEAD_SCALE, 1.0).astype(jnp.bfloat16)
        out_ref[...] = out * scale

    @pl.when(step >= 3 * each)
    def _():
        part = product(grad_ref[...], weight, 1, 0)

        @pl.when(step == 3 * each)
        def _():
            total_ref[...] = part

        @pl.when(step > 3 * each)
        def _():
            total_ref[...] += part

        @pl.when(step == 4 * each - 1)
        def _():
            att_grad_ref[...] = total_ref[...].astype(jnp.bfloat16)


def project(chain, source, grad, bias, weight):
    count, width = source.shape
    slots = grad.shape[0]
    each = width // UNITS
    return chain.call(
        project_kernel,
        (4 * each,),
        [
            whole_array(source.shape),
            pl.BlockSpec((slots, UNITS), lambda i, *_: (0, jnp.maximum(i - 3 * each, 0))),
            pl.BlockSpec((SEATS, UNITS), lambda i, *_: (0, jnp.minimum(i, 3 * each - 1))),
        ]
        + [weight.spec()],
        [
            (
                (count, 3 * width),
                jnp.bfloat16,
                pl.BlockSpec((count, UNITS), lambda i, *_: (0, jnp.minimum(i, 3 * each - 1))),
            ),
            ((slots, width), jnp.bfloat16, whole_array((slots, width))),
        ],
        [pltpu.VMEM((slots, width), jnp.float32)],
        source,
        grad,
        bias,
        weight.gathered,
    )


def source_back_kernel(query_ref, key_ref, value_ref, *refs):
    weight_ref, slot_ref, text_ref, total_ref = refs
    step = pl.program_id(0)
    each = pl.num_programs(0) // 3
    slots = slot_ref.shape[0]
    weight = rows_of(weight_ref)

    @pl.when(step == 0)
    def _():
        total_ref[...] = product(key_ref[...], weight, 1, 0)

    @pl.when((step > 0) & (step < each))
    def _():
        total_ref[...] += product(key_ref[...], weight, 1, 0)

    @pl.when((step >= each) & (step < 2 * each))
    def _():
        total_ref[...] += product(value_ref[...], weight, 1, 0)

    @pl.when(step >= 2 * each)
    def _():
        total_ref[:slots, :] += product(query_ref[...], weight, 1, 0)

    @pl.when(step == 3 * each - 1)
    def _():
        slot_ref[...] = total_ref[:slots, :]
        text_ref[...] = total_ref[slots:, :].astype(jnp.bfloat16)


def source_back(chain, query, keys, values, weight):
    slots, width = query.shape
    count = keys.shape[0]
    each = width // UNITS

    def columns(rows, turn):
        return pl.BlockSpec((rows, UNITS), lambda i, *_: (0, jnp.clip(i - turn * each, 0, each - 1)))

    return chain.call(
        source_back_kernel,
        (3 * each,),
        [columns(slots, 2), columns(count, 0), columns(count, 1)]
        + [weight.spec()],
        [
            ((slots, width), jnp.float32, whole_array((slots, width))),
            ((count - slots, width), jnp.bfloat16, whole_array((count - slots, width))),
        ],
        [pltpu.VMEM((count, width), jnp.float32)],
        query,
        keys,
        values,
        weight.gathered,
    )


def output_kernel(attended_ref, time_ref, live_ref, bias_ref, weight_ref, out_ref):
    out = product(attended_ref[...], rows_of(weight_ref), 1, 1) + bias_ref[0:1, :]
    out_ref[...] = time_ref[...] + live_ref[:, 0:1] * out


def output_step(chain, attended, after_time, live, bias, weight):
    slots, width = attended.shape
    each = width // UNITS
    columns = pl.BlockSpec((slots, UNITS), lambda i, *_: (0, i))
    return chain.call(
        output_kernel,
        (each,),
        [
            whole_array(attended.shape),
            columns,
            whole_array(live.shape),
            pl.BlockSpec((SEATS, UNITS), lambda i, *_: (0, i)),
        ]
        + [weight.spec()],
        [((slots, width), jnp.float32, columns)],
        [],
        attended,
        after_time,
        live,
        bias,
        weight.gathered,
    )[0]


def attn_half_kernel(added, half_ref, query_ref, key_ref, value_ref, proj_ref, source_ref, attended_ref, *refs):
    out_ref = refs[-1]
    role = 2 * half_ref[0] + pl.program_id(0) // (pl.num_programs(0) // 2)
    slots = query_ref.shape[0]

    def store(total):
        if added:
            total = total + refs[0][...].astype(jnp.float32)
        out_ref[...] = total.astype(jnp.bfloat16)

    @pl.when(role == 0)
    def _():
        store(product(query_ref[...], source_ref[:slots, :], 0, 0))

    @pl.when(role == 1)
    def _():
        store(product(key_ref[...], source_ref[...], 0, 0))

    @pl.when(role == 2)
    def _():
        store(product(value_ref[...], source_ref[...], 0, 0))

    @pl.when(role == 3)
    def _():
        store(product(proj_ref[...], attended_ref[...], 0, 0))


def attn_half(chain, query, keys, values, proj, source, attended, half, come=None):
    width = source.shape[1]
    each = width // UNITS
    rows = pl.BlockSpec((UNITS, width), lambda i, *_: (i, 0))

    def columns(values, role):
        def where(i, half_ref):
            return (0, jnp.where(2 * half_ref[0] + i // each == role, i % each, 0))

        return pl.BlockSpec((values.shape[0], UNITS), where)

    return chain.call(
        functools.partial(attn_half_kernel, come is not None),
        (2 * each,),
        [columns(v, n) for n, v in enumerate((query, keys, values, proj))]
        + [whole_array(source.shape), whole_array(attended.shape)]
        + ([] if come is None else [rows]),
        [((2 * width, width), jnp.bfloat16, rows)],
        [],
        query,
        keys,
        values,
        proj,
        source,
        attended,
        *(() if come is None else (come,)),
        scalars=(half.astype(jnp.int32)[None],),
    )[0]


def attention_kernel(q_ref, k_ref, v_ref, g_ref, bias_ref, att_ref, dq_ref, dk_ref, dv_ref):
    slots, width = q_ref.shape
    half = width // 2
    low = jnp.bfloat16
    lanes = lax.broadcasted_iota(jnp.int32, (1, width), 1)
    first = lanes < half
    keys, values = k_ref[...], v_ref[...]

    def both(ref):
        rows, none = ref[...], jnp.zeros((), low)
        return jnp.concatenate([jnp.where(first, rows, none), jnp.where(first, none, rows)], axis=0)

    def beside(turned):
        rows = turned.T
        return jnp.where(first, rows[:slots], rows[slots:])

    query, grad = both(q_ref), both(g_ref)
    scores = product(keys, query, 1, 1) + bias_ref[...]
    exponent = jnp.exp(scores - jnp.max(scores, axis=0, keepdims=True))
    probs = exponent * (1.0 / jnp.sum(exponent, axis=0, keepdims=True))
    probs_low = probs.astype(low)
    att_ref[...] = beside(product(values, probs_low, 0, 0)).astype(low)
    grad_probs = product(values, grad, 1, 1)
    inner_sum = jnp.sum(probs * grad_probs, axis=0, keepdims=True)
    grad_scores = (probs * (grad_probs - inner_sum)).astype(low)
    dv_ref[...] = product(probs_low, grad, 1, 0).astype(low)
    dk_ref[...] = product(grad_scores, query, 1, 0).astype(low)
    dq_ref[...] = (beside(product(keys, grad_scores, 0, 0)) * HEAD_SCALE).astype(low)


def attention(chain, mixed, grad, bias):
    slots, width = grad.shape
    count = mixed.shape[0]
    pair = 2 * (width // HEADS)
    each = width // pair

    def columns(rows, turn=0):
        return pl.BlockSpec((rows, pair), lambda h, *_: (0, turn * each + h))

    low = jnp.bfloat16
    return chain.call(
        attention_kernel,
        (each,),
        [columns(slots), columns(count, 1), columns(count, 2), columns(slots), whole_array(bias.shape)],
        [
            ((slots, width), low, columns(slots)),
            ((slots, width), low, columns(slots)),
            ((count, width), low, columns(count)),
            ((count, width), low, columns(count)),
        ],
        [],
        mixed,
        mixed,
        mixed,
        grad,
        bias,
    )


def layout(heights_row, widths_row):
    pixels = heights_row * widths_row
    ends_at = jnp.cumsum(pixels)
    starts_at = ends_at - pixels
    slot_ids = jnp.arange(SLOTS, dtype=jnp.int32)
    segment = jnp.sum((ends_at[None, :] <= slot_ids[:, None]).astype(jnp.int32), axis=1)
    member = segment[:, None] == jnp.arange(LAT_ROW, dtype=jnp.int32)[None, :]
    start_at = jnp.sum(jnp.where(member, starts_at[None, :], 0), axis=1)
    height_at = jnp.sum(jnp.where(member, heights_row[None, :], 0), axis=1)
    width_at = jnp.sum(jnp.where(member, widths_row[None, :], 0), axis=1)
    place_in = slot_ids - start_at
    safe_width = jnp.maximum(width_at, 1)
    column = place_in % safe_width
    row_index = place_in // safe_width
    return (segment, member, height_at, width_at, row_index, column)


def score_bias(segment, counts_row, key_pad):
    live_query = segment < LAT_ROW
    image_ok = (segment[:, None] == segment[None, :]) & live_query[None, :]
    text_index = jnp.arange(LAT_ROW * TEXT, dtype=jnp.int32)
    text_latent = text_index // TEXT
    text_limit = jnp.sum(
        jnp.where(
            text_latent[:, None] == jnp.arange(LAT_ROW, dtype=jnp.int32)[None, :],
            counts_row[None, :],
            0,
        ),
        axis=1,
    )
    text_ok = (text_latent[:, None] == segment[None, :]) & (text_index % TEXT < text_limit)[:, None]
    no_pad = jnp.zeros((key_pad, segment.shape[0]), bool)
    return jnp.where(jnp.concatenate([image_ok, text_ok, no_pad], axis=0), 0.0, MASKED)


def geometry_table(heights_row, widths_row):
    segment, member, height_at, width_at, row_index, column = layout(heights_row, widths_row)
    live = segment < LAT_ROW
    left = live & (column >= 1)
    right = live & (column + 1 < width_at)
    up = live & (row_index >= 1)
    down = live & (row_index + 1 < height_at)
    sides = [width_at == k * SIDE_UNIT for k in (3, 4, 6)]
    columns = [live, left, right] + [up & s for s in sides] + [down & s for s in sides]
    columns = columns + [jnp.zeros_like(live)] * 7
    return segment, member, jnp.stack(columns, axis=1).astype(jnp.float32)


def local(
    inner,
    outer,
    latents,
    text_embed,
    time_embed,
    heights,
    widths,
    text_counts,
    res_vecs,
    fc1_w,
    ff_vecs,
    fc2_w,
    time_w,
    time_b,
    kv_w,
    attn_w,
    attn_vecs,
    cotangent,
):
    low, full = jnp.bfloat16, jnp.float32
    orders = scatter_orders(outer)
    outer_bits, inner_bits = bit_count(outer), bit_count(inner)
    blocks = inner * outer
    x, cot = latents[0], cotangent[0]
    slots, width = x.shape
    text_width = text_embed.shape[3]
    text_total = LAT_ROW * TEXT
    key_pad = -(slots + text_total) % 128
    mine = lax.axis_index("dp") >> (inner_bits - 1)
    chain = Chain()

    def along(spec, a, b):
        return jnp.einsum(spec, a, b, preferred_element_type=full)

    small_owned = (res_vecs, ff_vecs, time_w, time_b[None], attn_vecs)
    small_sizes = [v.size for v in small_owned]
    small_pad = -sum(small_sizes) % (16 * 128)
    small_shard = jnp.concatenate(
        [v.astype(low).reshape(-1) for v in small_owned] + [jnp.zeros((small_pad,), low)]
    )
    rows, kv_rows = fc2_w.shape[0], kv_w.shape[0]
    def to_all(shard):
        shard = jnp.pad(shard, ((0, -shard.shape[0] % 8), (0, 0)))
        return lax.all_gather(late(chain, shard), ("dp", "fsdp"), axis=0, tiled=True).reshape(blocks, -1, width)

    first = Gather(
        chain, [fc1_w.T.astype(low), small_shard.reshape(-1, 128)], [orders, orders[2:]], inner, outer
    )
    first.step()
    second_all = to_all(jnp.concatenate([fc2_w.astype(low), kv_w.astype(low)], axis=0))
    for _ in range(outer_bits - 2):
        first.step()
    attn_all = to_all(attn_w.T.astype(low))
    fc1_parts, small_all = first.finish()
    fc1_t = [Weight(part, 0, rows) for part in sides(fc1_parts)]
    small_all = in_order(small_all).reshape(blocks, -1)
    small_full = []
    taken = 0
    for owned, size in zip(small_owned, small_sizes):
        some = small_all[:, taken : taken + size].reshape(blocks, owned.shape[0], owned.shape[1])
        small_full.append(some.transpose(1, 0, 2).reshape(owned.shape[0], -1).astype(full))
        taken += size
    res_all, ff_all, time_w_all, time_b_all, vecs_all = small_full
    taps = jnp.pad(res_all[:10], ((0, 6), (0, 0)))
    mine_index = mine.astype(jnp.int32)[None]
    side_index = [mine_index, 1 - mine_index]

    def halves(values):
        half = values.shape[1] // 2
        return [lax.dynamic_slice_in_dim(values, side * half, half, axis=1) for side in (mine, 1 - mine)]

    def ordered(own, other):
        return jnp.where(
            mine == 0, jnp.concatenate([own, other], axis=1), jnp.concatenate([other, own], axis=1)
        )

    vecs = halves(jnp.pad(ff_all, ((0, 5), (0, 0))))

    segment, member_slots, geometry = geometry_table(heights[0], widths[0])
    member = jnp.pad(member_slots[::GROUP].astype(full), ((0, 0), (0, SEATS - LAT_ROW)))
    bias = score_bias(segment, text_counts[0], key_pad)
    bias = jnp.concatenate([bias, bias], axis=1)
    live = geometry

    normed_low, normed, entry_scale = entry(chain, x, taps, geometry)
    hidden = [hidden_step(chain, normed_low, fc1_t[n], vecs[n], member) for n in range(2)]
    act, slope, power = zip(*hidden)
    second_all = late(chain, second_all)
    fc2_full = Weight(second_all, 0, rows)
    kv_full = second_all[:, rows : rows + kv_rows].reshape(-1, width)
    norm = [jnp.sqrt(v + NORM_EPS) for v in power]
    units = 2 * act[0].shape[1]
    norm_mean = sum(jnp.sum(v, axis=1, keepdims=True) for v in norm) * (1.0 / units) + NORM_EPS
    norms = [v / norm_mean for v in norm]
    time_low = jnp.pad(time_embed[0].astype(low), ((0, SEATS - LAT_ROW), (0, 0)))
    pair = along("lt,tc->lc", time_low, time_w_all.astype(low)) + time_b_all
    response_own, branch_part = branch_step(chain, act[0], norms[0], vecs[0], fc2_full, member, side_index[0])
    response_other, after_res, after_time, normed_two = branch_step(
        chain, act[1], norms[1], vecs[1], fc2_full, member, side_index[1],
        (branch_part, live, x, res_all[10:11], pair),
    )

    each = width // UNITS
    text = text_embed[0].astype(full).reshape(text_total, text_width)
    silu_text, silu_back = jax.vjp(jax.nn.silu, text)
    silu_low = silu_text.astype(low)
    mapped = (along("tk,kc->tc", silu_low, kv_full) + vecs_all[3]).astype(low)
    source = jnp.concatenate([normed_two, mapped, jnp.zeros((key_pad, width), low)], axis=0)
    source = copy_late(chain, source)
    attn_t = Weight(late(chain, attn_all), 0, rows)
    grad_proj = (live[:, 0:1] * cot).astype(low)
    mixed_bias = jnp.concatenate([vecs_all[0], jnp.zeros((width,), full), vecs_all[1]])
    mixed, grad_attended = project(
        chain, source, grad_proj, jnp.broadcast_to(mixed_bias, (SEATS, 3 * width)), attn_t
    )
    attended, grad_query, grad_key, grad_value = attention(chain, mixed, grad_attended, bias)

    free = list(reversed(range(outer_bits + inner_bits - 1)))
    early = [b for b in free if b >= outer_bits]

    def pieces_of(kept, come=None):
        kept = kept.reshape((2,) * len(free) + (-1, width))
        pieces = []
        for order, (start, size) in zip(orders, column_pieces(width, len(orders))):
            pieces.append(Piece(kept, early + order, free, start // size, size))
            if come is not None:
                pieces[-1].come, pieces[-1].come_cut = come.reshape(kept.shape), start // size
        return pieces

    def to_partner(away):
        return swap(away, "dp", inner, inner_bits - 1)

    def halved(terms):
        half = blocks // 2
        come = to_partner(lax.dynamic_slice_in_dim(terms, (1 - mine) * half, half, axis=0))
        kept = lax.dynamic_slice_in_dim(terms, mine * half, half, axis=0)
        some = Piece(kept.reshape((2,) * len(free) + terms.shape[1:]), early + orders[2], free)
        some.come = come.reshape(some.base.shape)
        return some

    def step(group, hold=False):
        fold(chain, group, inner, outer, (), hold)

    def finished(group):
        while group[0].order:
            step(group)
        return totals_of(chain, group)

    parts = (grad_query, grad_key, grad_value, grad_proj, source, attended)
    come = to_partner(attn_half(chain, *parts, 1 - mine))
    grad_normed_two, grad_text = source_back(
        chain,
        grad_query,
        grad_key,
        grad_value,
        attn_t.by(lambda i, *_: jnp.where(i < 2 * each, i + each, i - 2 * each)),
    )
    grad_mapped = grad_text[:text_total]
    kv_terms = along("tk,tc->kc", silu_low, grad_mapped).astype(low)
    kv_piece = halved(kv_terms.reshape(blocks, -1, width))
    attn_sum = pieces_of(attn_half(chain, *parts, mine, come)) + [kv_piece]
    for _ in early:
        step(attn_sum)
    step(attn_sum)
    grad_res, grad_branch, pair_grad, res_bias_grad = time_back(
        chain, grad_normed_two, after_time, after_res, cot, pair, member, live
    )
    grad_other, sums_other, shift_other, fc2_away = response_back(
        chain, grad_branch, fc2_full, act[1], response_other, member, side_index[1]
    )
    grad_own, sums_own, shift_own, fc2_kept = response_back(
        chain, grad_branch, fc2_full, act[0], response_own, member, side_index[0]
    )
    step(attn_sum)
    fc2_come = to_partner(late(chain, fc2_away))
    sums = [sums_own, sums_other]
    gain_grad = ordered(*[jnp.sum(v * n, axis=0, keepdims=True) for v, n in zip(sums, norms)])
    shift_grad = ordered(shift_own[:1], shift_other[:1])
    norms_grad = [g[1:2] * v for g, v in zip(vecs, sums)]
    common = sum(jnp.sum(g * n, axis=1, keepdims=True) for g, n in zip(norms_grad, norm)) / (
        units * norm_mean * norm_mean
    )
    ratio = [(g / norm_mean - common) / n for g, n in zip(norms_grad, norm)]

    def hidden_grads(n, grad, before=None):
        return hidden_back(
            chain, grad, act[n], slope[n], vecs[n], norms[n], ratio[n], member, normed_low, fc1_t[n], before
        )

    bias_away, grad_normed, fc1_away = hidden_grads(1, grad_other)
    step(attn_sum)
    fc2_sum = pieces_of(fc2_kept, fc2_come)
    for _ in early:
        step(fc2_sum)
    step(fc2_sum, True)
    for _ in range(outer_bits - 3):
        step(attn_sum)
    send(chain, fc2_sum, inner, outer)
    bias_kept, grad_normed, fc1_kept = hidden_grads(0, grad_own, grad_normed)
    hidden_bias_grad = ordered(bias_kept[:1], bias_away[:1])
    output = output_step(
        chain,
        attended,
        after_time,
        live,
        jnp.broadcast_to(vecs_all[2], (SEATS, width)),
        attn_t.by(lambda i, *_: 3 * each + i),
    )
    attn_grad, kv_grad = finished(attn_sum)
    step(fc2_sum)
    fc1_come = to_partner(late(chain, fc1_away))
    latents_grad, taps_grad = entry_back(
        chain, grad_normed, normed, entry_scale, x, grad_res, taps, geometry, res_bias_grad
    )
    step(fc2_sum)
    taps_grad = copy_late(chain, taps_grad)
    time_grad = jnp.einsum("lt,lc->tc", time_low.astype(full), pair_grad, precision=HIGHEST)
    small_terms = (
        taps_grad[: res_vecs.shape[0]],
        jnp.concatenate([hidden_bias_grad[:1], gain_grad, shift_grad[:1]], axis=0),
        time_grad,
        jnp.sum(pair_grad, axis=0, keepdims=True),
        jnp.stack(
            [
                jnp.sum(grad_query.astype(full), axis=0),
                jnp.sum(grad_value.astype(full), axis=0),
                jnp.sum(grad_proj.astype(full), axis=0),
                jnp.sum(grad_mapped.astype(full), axis=0),
            ]
        ),
    )
    small_blocks = jnp.concatenate(
        [g.reshape(g.shape[0], blocks, -1).transpose(1, 0, 2).reshape(blocks, -1) for g in small_terms]
        + [jnp.zeros((blocks, -sum(small_sizes) % 1024), full)],
        axis=1,
    ).reshape(blocks, -1, 128)
    small_piece = halved(small_blocks)
    fc1_sum = pieces_of(fc1_kept, fc1_come) + [small_piece]
    for _ in early:
        step(fc1_sum)
    step(fc1_sum, True)
    for _ in range(outer_bits - 3):
        step(fc2_sum)
    send(chain, fc1_sum, inner, outer)
    (fc2_grad,) = finished(fc2_sum)
    step(fc1_sum)
    step(fc1_sum)
    while fc1_sum[0].order:
        step(fc1_sum)
    (small_total,) = totals_of(chain, fc1_sum[1:])
    small_total = small_total.reshape(-1)
    small_grads = []
    taken = 0
    for owned, size in zip(small_owned, small_sizes):
        small_grads.append(small_total[taken : taken + size].reshape(owned.shape))
        taken += size
    text_grad = silu_back(along("tc,kc->tk", grad_mapped, kv_full))[0]
    (fc1_grad,) = totals_of(chain, fc1_sum[:1], small_grads)
    return (
        output[None],
        latents_grad[None],
        text_grad.reshape(text_embed.shape),
        small_grads[0],
        fc1_grad.T,
        small_grads[1],
        fc2_grad,
        small_grads[2],
        small_grads[3][0],
        kv_grad,
        attn_grad.T,
        small_grads[4],
    )


def solution(mesh):
    return jax.shard_map(
        functools.partial(local, mesh.shape["dp"], mesh.shape["fsdp"]),
        mesh=mesh,
        in_specs=(
            P(("dp", "fsdp"), None, None),
            P(("dp", "fsdp"), None, None, None),
            P(("dp", "fsdp"), None, None),
            P(("dp", "fsdp"), None),
            P(("dp", "fsdp"), None),
            P(("dp", "fsdp"), None),
            P(None, ("dp", "fsdp")),
            P(None, ("dp", "fsdp")),
            P(None, ("dp", "fsdp")),
            P(("dp", "fsdp"), None),
            P(None, ("dp", "fsdp")),
            P(("dp", "fsdp")),
            P(("dp", "fsdp"), None),
            P(None, ("dp", "fsdp")),
            P(None, ("dp", "fsdp")),
            P(("dp", "fsdp"), None, None),
        ),
        out_specs=(
            P(("dp", "fsdp"), None, None),
            P(("dp", "fsdp"), None, None),
            P(("dp", "fsdp"), None, None, None),
            P(None, ("dp", "fsdp")),
            P(None, ("dp", "fsdp")),
            P(None, ("dp", "fsdp")),
            P(("dp", "fsdp"), None),
            P(None, ("dp", "fsdp")),
            P(("dp", "fsdp")),
            P(("dp", "fsdp"), None),
            P(None, ("dp", "fsdp")),
            P(None, ("dp", "fsdp")),
        ),
        check_vma=False,
    )
```
